32 devices in a mesh: ctx: 8 (over y, x, core), head: 4 (over z).
Axes of the slice: x: 2, y: 2, z: 4, core: 2. Of those that a mesh axis runs over, the one named last changes fastest.
Arguments:
- hidden_in: bfloat16 [2, 4096, 2048], P(None, 'ctx', 'head'), may hold values from -6 to 6
- projected: bfloat16 [3, 2, 4096, 2048], P(None, None, 'ctx', 'head'), may hold values from -4.5 to 4.5
- w_out: bfloat16 [2048, 2048], P(None, 'head'), may hold values from -0.125 to 0.125
- fast_up: bfloat16 [2, 4, 512, 512], P(None, 'head'), may hold values from -0.25 to 0.25
- fast_down: bfloat16 [4, 512, 512], P('head'), may hold values from -0.25 to 0.25
- learn_rates: float32 [4, 2, 4096], P('head', None, 'ctx'), may hold values from 0.02 to 0.2
Outputs:
- layer_out: bfloat16 [2, 4096, 2048], P(None, 'ctx', 'head')
- fast_up_final: float32 [2, 4, 512, 512], P(None, 'head')
- fast_down_final: float32 [4, 512, 512], P('head')
The draws below stay inside these ranges and needn't reach their ends.
All inputs are finite; a program needn't handle non-finite values.
Results may differ from the reference program's by a relative error of at most 0.0087.
Values may be sent and summed in bfloat16 or wider, within the bound.
No kernel may reach another device: no remote copies, remote signals or barrier semaphores. Data moves between devices by JAX's collectives and lax.ppermute only.
A program may use at most 128 MiB of HBM per device.

```python
import math
import jax
import jax.numpy as jnp
from jax import lax

D = 2048
HA = 16
HD = 128
HF = 4
FD = 512
FH = 512
WIN = 512
BLOCKS = 2
BLOCK_LEN = 4096


def draw_projected(key, part):
    base_key = jax.random.fold_in(jax.random.fold_in(key, 7), 0)
    full_shape = (3, BLOCKS, BLOCK_LEN, D)
    base_draw = jnp.clip(jax.random.normal(base_key, full_shape, jnp.float32), -4.5, 4.5)
    return base_draw.astype(jnp.bfloat16)


def steps_of(key, shape, shards, low, top_value):
    def one(dim, parts):
        draws = jax.random.uniform(jax.random.fold_in(jax.random.fold_in(key, 6), dim), (parts,), jnp.float32, low / len(shards), top_value / len(shards))
        return jnp.repeat(jnp.exp(draws), shape[dim] // parts).reshape((-1,) + (1,) * (len(shape) - dim - 1))

    loudness = one(*shards[0])
    for cut in shards[1:]:
        loudness = loudness * one(*cut)
    return loudness


def centred(own_key, dims, spread, bound, shards=(), kind=jnp.bfloat16):
    array = spread * jax.random.normal(own_key, dims, jnp.float32)
    if shards:
        array = array * steps_of(own_key, dims, shards, -0.22, 0.18)
    return jnp.clip(array, -bound, bound).astype(kind)


def setup_inputs(seed: int = 0) -> dict:
    arg_keys = jax.random.split(jax.random.key(seed), 7)
    return {
        "hidden_in": centred(arg_keys[0], (BLOCKS, BLOCK_LEN, D), 1.0, 6.0, ((1, 8), (2, 4))),
        "projected": draw_projected(jax.random.fold_in(arg_keys[6], 71), 0),
        "w_out": centred(arg_keys[2], (D, D), D ** -0.5, 0.125, ((1, 4),)),
        "fast_up": centred(arg_keys[3], (2, HF, FD, FH), FD ** -0.5, 0.25, ((1, 4),)),
        "fast_down": centred(arg_keys[4], (HF, FH, FD), FH ** -0.5, 0.25, ((0, 4),)),
        "learn_rates": jnp.clip(jnp.exp(math.log(0.2) - 2.3025851 * jax.random.uniform(arg_keys[5], (HF, BLOCKS, BLOCK_LEN), jnp.float32) ** steps_of(arg_keys[5], (HF, BLOCKS, BLOCK_LEN), ((0, 4), (2, 8)), -0.2, 0.2)), 0.02, 0.2),
    }


def attention(projected):
    seq_len = BLOCKS * BLOCK_LEN
    queries = projected[0].reshape(seq_len, HA, HD)
    key_rows = projected[1].reshape(seq_len, HA, HD)
    value_rows = projected[2].reshape(seq_len, HA, HD)
    padding = jnp.zeros((WIN, HA, HD), jnp.bfloat16)
    key_padded = jnp.concatenate([padding, key_rows], axis=0)
    value_padded = jnp.concatenate([padding, value_rows], axis=0)
    score_scale = 1.0 / math.sqrt(HD)
    row_ids = jnp.arange(WIN, dtype=jnp.int32)[:, None]
    col_ids = jnp.arange(2 * WIN, dtype=jnp.int32)[None, :]
    distance = row_ids + WIN - col_ids

    def one_block(block_index):
        start_row = (block_index * WIN).astype(jnp.int32)
        query_block = lax.dynamic_slice_in_dim(queries, start_row, WIN, 0)
        key_block = lax.dynamic_slice_in_dim(key_padded, start_row, 2 * WIN, 0)
        value_block = lax.dynamic_slice_in_dim(value_padded, start_row, 2 * WIN, 0)
        scores = jnp.einsum('qhd,khd->hqk', query_block.astype(jnp.float32), key_block.astype(jnp.float32)) * score_scale
        allowed = (distance >= 0) & (distance < WIN) & (col_ids + start_row >= WIN)
        scores = jnp.where(allowed[None], scores, -1e+30)
        row_peak = lax.optimization_barrier(jnp.max(scores, axis=-1, keepdims=True))
        lifted = jnp.exp(scores - row_peak)
        weights = (lifted / lax.optimization_barrier(jnp.sum(lifted, axis=-1, keepdims=True))).astype(jnp.bfloat16)
        result = jnp.einsum('hqk,khd->qhd', weights.astype(jnp.float32), value_block.astype(jnp.float32))
        return result.astype(jnp.bfloat16).reshape(WIN, HA * HD)
    blocks_out = lax.map(one_block, jnp.arange(seq_len // WIN, dtype=jnp.int32))
    return blocks_out.reshape(BLOCKS, BLOCK_LEN, HA * HD)

def fast_apply(rows_in, w_one, w_three, w_two):
    pre_gate = jnp.dot(rows_in, w_one, preferred_element_type=jnp.float32)
    pre_up = jnp.dot(rows_in, w_three, preferred_element_type=jnp.float32)
    hidden = (pre_gate * jax.nn.sigmoid(pre_gate) * pre_up).astype(jnp.bfloat16)
    result = jnp.dot(hidden, w_two, preferred_element_type=jnp.float32)
    return result * lax.rsqrt(lax.optimization_barrier(jnp.mean(result * result, axis=-1, keepdims=True)) + 1e-05)

def fast_grads(key_rows, value_rows, step_size, w_one, w_three, w_two):
    pre_gate = jnp.dot(key_rows, w_one, preferred_element_type=jnp.float32)
    pre_up = jnp.dot(key_rows, w_three, preferred_element_type=jnp.float32)
    gate_sig = jax.nn.sigmoid(pre_gate)
    hidden = (pre_gate * gate_sig * pre_up).astype(jnp.bfloat16)
    out_grad = (-step_size[:, None] * value_rows.astype(jnp.float32)).astype(jnp.bfloat16)
    grad_two = jnp.dot(hidden.T, out_grad, preferred_element_type=jnp.float32)
    hidden_grad = jnp.dot(out_grad, w_two.T, preferred_element_type=jnp.float32)
    gate_grad = (hidden_grad * pre_up * gate_sig * (1.0 + pre_gate * (1.0 - gate_sig))).astype(jnp.bfloat16)
    up_grad = (hidden_grad * pre_gate * gate_sig).astype(jnp.bfloat16)
    grad_one = jnp.dot(key_rows.T, gate_grad, preferred_element_type=jnp.float32)
    grad_three = jnp.dot(key_rows.T, up_grad, preferred_element_type=jnp.float32)
    return (grad_one, grad_three, grad_two)

def renorm(old_weight, gradient):
    moved_weight = old_weight - gradient
    return moved_weight * (jnp.sqrt(jnp.sum(old_weight * old_weight)) / jnp.sqrt(jnp.sum(moved_weight * moved_weight) + 1e-06))

def reference(hidden_in, projected, w_out, fast_up, fast_down, learn_rates):
    attended = attention(projected)
    step_scale = 1.0 / math.sqrt(BLOCK_LEN)
    mixed_heads = []
    final_one = []
    final_three = []
    final_two = []
    for head_idx in range(HF):
        low = head_idx * FD
        high = low + FD
        weights_now = (fast_up[0, head_idx].astype(jnp.float32), fast_up[1, head_idx].astype(jnp.float32), fast_down[head_idx].astype(jnp.float32))
        pieces = []
        for block_idx in range(BLOCKS):
            w_one = weights_now[0].astype(jnp.bfloat16)
            w_three = weights_now[1].astype(jnp.bfloat16)
            w_two = weights_now[2].astype(jnp.bfloat16)
            fast_out = fast_apply(projected[0, block_idx, :, low:high], w_one, w_three, w_two)
            pieces.append((attended[block_idx, :, low:high].astype(jnp.float32) + fast_out).astype(jnp.bfloat16))
            gradients = fast_grads(projected[1, block_idx, :, low:high], projected[2, block_idx, :, low:high], learn_rates[head_idx, block_idx] * step_scale, w_one, w_three, w_two)
            weights_now = (renorm(weights_now[0], gradients[0]), renorm(weights_now[1], gradients[1]), renorm(weights_now[2], gradients[2]))
        mixed_heads.append(jnp.stack(pieces))
        final_one.append(weights_now[0])
        final_three.append(weights_now[1])
        final_two.append(weights_now[2])
    mixed = jnp.concatenate(mixed_heads, axis=2).reshape(BLOCKS * BLOCK_LEN, D)
    projected_out = jnp.dot(mixed, w_out, preferred_element_type=jnp.float32).reshape(BLOCKS, BLOCK_LEN, D)
    layer_out = (hidden_in.astype(jnp.float32) + projected_out).astype(jnp.bfloat16)
    fast_up_final = jnp.stack([jnp.stack(final_one), jnp.stack(final_three)])
    fast_down_final = jnp.stack(final_two)
    return (layer_out, fast_up_final, fast_down_final)
```

```python
import functools
import math

import jax
import jax.numpy as jnp
from jax import lax
from jax.experimental import pallas as pl
from jax.experimental.pallas import tpu as pltpu
from jax.sharding import PartitionSpec as P

HD = 128
WIN = 512
TILE = 256
MASKED = -1e30
BF = jnp.bfloat16
F32 = jnp.float32
LIMIT = 48 * 1024 * 1024


def mm(a, b):
    return jnp.dot(a, b, preferred_element_type=F32)


def mm_nt(a, b):
    return lax.dot_general(a, b, (((1,), (1,)), ((), ())), preferred_element_type=F32)


def mm_tn(a, b):
    return lax.dot_general(a, b, (((0,), (0,)), ((), ())), preferred_element_type=F32)


def sigmoid(x):
    return 0.5 + 0.5 * jnp.tanh(0.5 * x)


def whole(array):
    zeros = (0,) * array.ndim
    return pl.BlockSpec(array.shape, lambda *_: zeros)


def whole_out(shape):
    zeros = (0,) * len(shape)
    return pl.BlockSpec(shape, lambda *_: zeros)


def call(kernel, name, scalars, inputs, specs, outs, scratch=(), grid=(1,), flops=0, nbytes=0):
    single = not isinstance(outs, (list, tuple))
    outs_list = [outs] if single else list(outs)
    got = pl.pallas_call(
        kernel,
        out_shape=outs_list,
        grid_spec=pltpu.PrefetchScalarGridSpec(
            num_scalar_prefetch=1,
            grid=grid,
            in_specs=specs,
            out_specs=[whole_out(o.shape) for o in outs_list],
            scratch_shapes=list(scratch),
        ),
        compiler_params=pltpu.CompilerParams(vmem_limit_bytes=LIMIT),
        cost_estimate=pl.CostEstimate(flops=flops, bytes_accessed=nbytes, transcendentals=0),
        name=name,
    )(scalars, *inputs)
    return got[0] if single else got


def grads_kernel(block, step_scale, sc, k_ref, v_ref, lr_ref, w1_ref, w3_ref, w2_ref, keep_ref, send_ref, acc):
    step = pl.program_id(0)
    k = k_ref[...]
    w_two = w2_ref[...]
    rates = lr_ref[0, block : block + 1, :] * step_scale
    rates = jnp.broadcast_to(rates, (HD, rates.shape[1])).T[:, :1]
    out_grad = (-rates * v_ref[...].astype(F32)).astype(BF)
    gate = mm(k, w1_ref[...])
    up = mm(k, w3_ref[...])
    hidden_grad = mm_nt(out_grad, w_two)
    sig = sigmoid(gate)
    gate_sig = gate * sig
    hidden = (gate_sig * up).astype(BF)
    up_grad = (hidden_grad * gate_sig).astype(BF)
    gate_grad = (hidden_grad * up * sig * (1.0 + gate - gate_sig)).astype(BF)
    parts = (mm_tn(k, gate_grad), mm_tn(k, up_grad), mm_tn(hidden, out_grad))

    @pl.when(step == 0)
    def _():
        for i, part in enumerate(parts):
            acc[i] = part

    @pl.when(step > 0)
    def _():
        for i, part in enumerate(parts):
            acc[i] = acc[i] + part

    @pl.when(step == pl.num_programs(0) - 1)
    def _():
        half = keep_ref.shape[1]
        own = pl.multiple_of(sc[0] * half, half)
        other = pl.multiple_of((1 - sc[0]) * half, half)
        keep_ref[...] = acc[:, pl.ds(own, half), :].astype(BF)
        send_ref[...] = acc[:, pl.ds(other, half), :].astype(BF)


def block_grads(block, scalars, projected, learn_rates, weights, step_scale, weight_specs):
    _, _, rows, feats = projected.shape
    half = feats // 2
    shape = jax.ShapeDtypeStruct((3, half, feats), BF)
    tile = min(TILE, rows)
    return call(
        functools.partial(grads_kernel, block, step_scale),
        f"grads_{block}",
        scalars,
        (projected, projected, learn_rates, *weights),
        [
            pl.BlockSpec((None, None, tile, feats), lambda i, s: (1, block, i, 0)),
            pl.BlockSpec((None, None, tile, feats), lambda i, s: (2, block, i, 0)),
            pl.BlockSpec((1, learn_rates.shape[1], tile), lambda i, s: (0, 0, i)),
            *weight_specs,
        ],
        [shape, shape],
        scratch=[pltpu.VMEM((3, feats, feats), F32)],
        grid=(rows // tile,),
        flops=12 * rows * feats * feats,
        nbytes=4 * feats * feats * 2,
    )


def attend_rows(q, keys, values, usable):
    rows = q.shape[0]
    row_ids = lax.broadcasted_iota(jnp.int32, (rows, rows), 0)
    col_ids = lax.broadcasted_iota(jnp.int32, (rows, rows), 1)
    scale = math.log2(math.e) / math.sqrt(HD)
    scores = []
    last = len(keys) - 1
    for i, (key, before) in enumerate(keys):
        s = mm_nt(q, key)
        if before:
            s = s + usable
        if i == 0:
            s = jnp.where(col_ids > row_ids, s, MASKED)
        if i == last:
            s = jnp.where(col_ids <= row_ids, s, MASKED)
        scores.append(s)
    top = functools.reduce(jnp.maximum, scores)
    peak = jnp.max(top, axis=-1, keepdims=True) * scale
    total = None
    result = None
    for s, value in zip(scores, values):
        lifted = jnp.exp2(s * scale - peak)
        total = lifted if total is None else total + lifted
        part = mm(lifted.astype(BF), value)
        result = part if result is None else result + part
    return (result / jnp.sum(total, axis=-1, keepdims=True)).astype(BF)


def attend(q_ref, k_ref, v_ref, halo_ref, usable, store):
    rows, feats = q_ref.shape
    tile = min(TILE, rows)
    for start in range(0, rows, tile):
        for head in range(feats // HD):
            cols = slice(head * HD, (head + 1) * HD)
            keys, values = [], []
            for at in range(start - WIN, start + tile, tile):
                before = at < 0
                where = slice(at + WIN, at + WIN + tile) if before else slice(at, at + tile)
                keys.append(((halo_ref[0, where, cols] if before else k_ref[where, cols]), before))
                values.append(halo_ref[1, where, cols] if before else v_ref[where, cols])
            store(slice(start, start + tile), cols, attend_rows(q_ref[start : start + tile, cols], keys, values, usable))


def fast_rows(q, w_one, w_three, w_two):
    gate = mm(q, w_one)
    up = mm(q, w_three)
    hidden = (gate * sigmoid(gate) * up).astype(BF)
    result = mm(hidden, w_two)
    return result * lax.rsqrt(jnp.mean(result * result, axis=-1, keepdims=True) + 1e-05)


def usable_bias(block, sc):
    return jnp.where((sc[1] > 0) | (block > 0), 0.0, MASKED).astype(F32)


def mixed_kernel(block, sc, q_ref, k_ref, v_ref, halo_ref, w1_ref, w3_ref, w2_ref, out_ref, att):
    def store(rows, cols, value):
        att[rows, cols] = value

    attend(q_ref, k_ref, v_ref, halo_ref, usable_bias(block, sc), store)
    rows = q_ref.shape[0]
    tile = min(TILE, rows)
    for start in range(0, rows, tile):
        at = slice(start, start + tile)
        fast = fast_rows(q_ref[at, :], w1_ref[...], w3_ref[...], w2_ref[...])
        out_ref[at, :] = (att[at, :].astype(F32) + fast).astype(BF)


def attend_kernel(block, sc, q_ref, k_ref, v_ref, halo_ref, out_ref):
    def store(rows, cols, value):
        out_ref[rows, cols] = value

    attend(q_ref, k_ref, v_ref, halo_ref, usable_bias(block, sc), store)


def qkv_specs(block, projected):
    _, _, rows, feats = projected.shape
    return [
        pl.BlockSpec((None, None, rows, feats), functools.partial(lambda kind, i, s: (kind, block, 0, 0), kind))
        for kind in range(3)
    ]


def attention_only(block, scalars, projected, halo):
    _, _, rows, feats = projected.shape
    return call(
        functools.partial(attend_kernel, block),
        f"attend_{block}",
        scalars,
        (projected, projected, projected, halo),
        [*qkv_specs(block, projected), whole(halo)],
        jax.ShapeDtypeStruct((rows, feats), BF),
        flops=8 * rows * WIN * feats,
        nbytes=6 * rows * feats * 2,
    )


def mixed_first(block, scalars, projected, halo, weights, weight_specs):
    _, _, rows, feats = projected.shape
    return call(
        functools.partial(mixed_kernel, block),
        f"mixed_{block}",
        scalars,
        (projected, projected, projected, halo, *weights),
        [*qkv_specs(block, projected), whole(halo), *weight_specs],
        jax.ShapeDtypeStruct((rows, feats), BF),
        scratch=[pltpu.VMEM((rows, feats), BF)],
        flops=8 * rows * WIN * feats + 6 * rows * feats * feats,
        nbytes=8 * rows * feats * 2,
    )


def renorm_into(sc, old, mine_ref, theirs_ref, moved):
    half = mine_ref.shape[1]
    own = pl.multiple_of(sc[0] * half, half)
    other = pl.multiple_of((1 - sc[0]) * half, half)
    for i in range(3):
        before = jnp.zeros((), F32)
        after = jnp.zeros((), F32)
        for start, part in ((own, mine_ref), (other, theirs_ref)):
            w = old(i, pl.ds(start, half)).astype(F32)
            new = w - part[i].astype(F32)
            moved[i, pl.ds(start, half), :] = new
            before += jnp.sum(w * w)
            after += jnp.sum(new * new)
        ratio = jnp.sqrt(before) / jnp.sqrt(after + 1e-06)
        moved[i] = moved[i] * ratio


def update_kernel(first, sc, mine_ref, theirs_ref, up_ref, down_ref, q_ref, att_ref, mix_ref, new_ref, new_bf_ref):
    if first:
        old = lambda i, rows: up_ref[i, 0, rows, :] if i < 2 else down_ref[0, rows, :]
    else:
        old = lambda i, rows: up_ref[i, rows, :]
    renorm_into(sc, old, mine_ref, theirs_ref, new_ref)
    new_bf_ref[...] = new_ref[...].astype(BF)
    rows = q_ref.shape[0]
    tile = min(TILE, rows)
    for start in range(0, rows, tile):
        at = slice(start, start + tile)
        fast = fast_rows(q_ref[at, :], new_bf_ref[0], new_bf_ref[1], new_bf_ref[2])
        mix_ref[at, :] = (att_ref[at, :].astype(F32) + fast).astype(BF)


def update_and_mix(block, scalars, mine, theirs, state, projected, attended):
    _, _, rows, feats = projected.shape
    first = block == 1
    return call(
        functools.partial(update_kernel, first),
        f"update_{block}",
        scalars,
        (mine, theirs, state[0], state[1], projected, attended),
        [
            whole(mine),
            whole(theirs),
            whole(state[0]),
            whole(state[1]),
            pl.BlockSpec((None, None, rows, feats), lambda i, s: (0, block, 0, 0)),
            whole(attended),
        ],
        [
            jax.ShapeDtypeStruct((rows, feats), BF),
            jax.ShapeDtypeStruct((3, feats, feats), F32),
            jax.ShapeDtypeStruct((3, feats, feats), BF),
        ],
        flops=6 * rows * feats * feats,
        nbytes=9 * feats * feats * 2,
    )


def final_kernel(first, sc, mine_ref, theirs_ref, up_ref, down_ref, up_out, down_out, moved):
    if first:
        old = lambda i, rows: up_ref[i, 0, rows, :] if i < 2 else down_ref[0, rows, :]
    else:
        old = lambda i, rows: up_ref[i, rows, :]
    renorm_into(sc, old, mine_ref, theirs_ref, moved)
    up_out[0, 0] = moved[0]
    up_out[1, 0] = moved[1]
    down_out[0] = moved[2]


def final_update(first, scalars, mine, theirs, state):
    feats = mine.shape[2]
    return call(
        functools.partial(final_kernel, first),
        "final_update",
        scalars,
        (mine, theirs, *state),
        [whole(mine), whole(theirs), whole(state[0]), whole(state[1])],
        [jax.ShapeDtypeStruct((2, 1, feats, feats), F32), jax.ShapeDtypeStruct((1, feats, feats), F32)],
        scratch=[pltpu.VMEM((3, feats, feats), F32)],
        flops=10 * feats * feats,
        nbytes=9 * feats * feats * 2,
    )


def edge_kernel(sc, m_ref, ya_ref, yb_ref, v_ref, out_ref):
    out_ref[...] = (mm(m_ref[...], v_ref[0]) + mm(ya_ref[...], v_ref[1]) + mm(yb_ref[...], v_ref[2])).astype(BF)


def edge_part(block, scalars, m, ya, yb, v):
    rows, feats = m.shape
    return call(
        edge_kernel,
        f"edge_{block}",
        scalars,
        (m, ya, yb, v),
        [whole(m), whole(ya), whole(yb), whole(v)],
        jax.ShapeDtypeStruct((rows, feats), BF),
        flops=6 * rows * feats * feats,
        nbytes=7 * rows * feats * 2,
    )


def own_kernel(sc, m_ref, x_ref, ya_ref, yb_ref, w_ref, hid_ref, out_ref):
    feats = m_ref.shape[1]
    head = sc[2]

    def weight(which):
        return w_ref[pl.ds(pl.multiple_of(which * feats, feats), feats), :]

    out_ref[...] = hid_ref[...].astype(F32) + mm(m_ref[...], weight(head))

    @pl.when(sc[3] == 1)
    def _():
        out_ref[...] = (
            out_ref[...]
            + mm(x_ref[...], weight(head ^ 1))
            + mm(ya_ref[...], weight(head ^ 3))
            + mm(yb_ref[...], weight(head ^ 2))
        )


def own_part(block, scalars, m, x, ya, yb, w_out, hidden_in):
    rows, feats = m.shape
    return call(
        own_kernel,
        f"own_{block}",
        scalars,
        (m, x, ya, yb, w_out, hidden_in),
        [
            whole(m),
            whole(x),
            whole(ya),
            whole(yb),
            whole(w_out),
            pl.BlockSpec((None, rows, feats), lambda i, s: (block, 0, 0)),
        ],
        jax.ShapeDtypeStruct((rows, feats), F32),
        flops=8 * rows * feats * feats,
        nbytes=10 * rows * feats * 2,
    )


def move(x, axis, pairs):
    return lax.ppermute(x, axis, pairs)


def flip(x, bit):
    count = lax.axis_size("ctx")
    return move(x, "ctx", [(i, i ^ (1 << bit)) for i in range(count)])


def add(a, b):
    return (a.astype(F32) + b.astype(F32)).astype(BF)


def sum_over_ctx(keep, send):
    count = lax.axis_size("ctx")
    bits = list(range(1, count.bit_length() - 1))
    total = add(keep, flip(send, 0))
    for step in range(len(bits)):
        pairs = []
        for i in range(count):
            order = bits if i % 2 == 0 else bits[::-1]
            pairs.append((i, i ^ (1 << order[step])))
        total = add(total, move(total, "ctx", pairs))
    return total, flip(total, 0)


def body(hidden_in, projected, w_out, fast_up, fast_down, learn_rates):
    blocks, rows, feats = hidden_in.shape
    ctx = lax.axis_index("ctx")
    head = lax.axis_index("head")
    ctx_count = lax.axis_size("ctx")
    parity = ctx % 2
    inner = ((head == 1) | (head == 2)).astype(jnp.int32)
    scalars = jnp.stack([parity, ctx, head, inner]).astype(jnp.int32)
    step_scale = 1.0 / math.sqrt(rows * ctx_count)

    kv = projected[1:3, :, rows - WIN :, :]
    forward = [(i, i + 1) for i in range(ctx_count - 1)]
    halos = []
    for block in range(blocks):
        if block == 0:
            halos.append(move(kv[:, 0], "ctx", forward))
        else:
            source = jnp.where(ctx == ctx_count - 1, kv[:, block - 1], kv[:, block])
            halos.append(move(source, "ctx", forward + [(ctx_count - 1, 0)]))

    edge_in = [(0, 1), (3, 2)]
    middle = [(1, 2), (2, 1)]
    w_parts = w_out.reshape(4, feats, w_out.shape[1])
    half = feats // 2
    v_send = jnp.stack(
        [
            lax.dynamic_slice(w_parts, (head ^ k, parity * half, 0), (1, half, w_out.shape[1]))[0]
            for k in (1, 2, 3)
        ]
    )
    v_mine = move(v_send, "head", edge_in)
    v_other = flip(v_mine, 0)
    v = jnp.where(
        parity == 0,
        jnp.concatenate([v_mine, v_other], axis=1),
        jnp.concatenate([v_other, v_mine], axis=1),
    )

    up_spec = [
        pl.BlockSpec((None, None, feats, feats), lambda *_: (0, 0, 0, 0)),
        pl.BlockSpec((None, None, feats, feats), lambda *_: (1, 0, 0, 0)),
        pl.BlockSpec((None, feats, feats), lambda *_: (0, 0, 0)),
    ]
    bf_spec = [
        pl.BlockSpec((None, feats, feats), functools.partial(lambda k, *_: (k, 0, 0), k)) for k in range(3)
    ]
    weights, specs = (fast_up, fast_up, fast_down), up_spec
    state = (fast_up, fast_down)
    mine = theirs = None
    c_before = None
    accs, edges = [], []
    for block in range(blocks):
        if block == 0:
            mixed = mixed_first(block, scalars, projected, halos[block], weights, specs)
        else:
            attended = attention_only(block, scalars, projected, halos[block])
            mixed, new, new_bf = update_and_mix(block, scalars, mine, theirs, state, projected, attended)
            weights, specs = (new_bf, new_bf, new_bf), bf_spec
            state = (new, new_bf)
        keep, send = block_grads(block, scalars, projected, learn_rates, weights, step_scale, specs)
        mine, theirs = sum_over_ctx(keep, send)
        if block == 0:
            x = move(mixed, "head", edge_in)
        else:
            x = move(
                jnp.where(inner == 1, c_before, mixed), "head", [(0, 1), (1, 0), (2, 3), (3, 2)]
            )
            edges.append(x)
        ya = move(mixed, "head", middle)
        yb = move(x, "head", middle)
        c_before = edge_part(block, scalars, mixed, ya, yb, v)
        accs.append(own_part(block, scalars, mixed, x, ya, yb, w_out, hidden_in))
    edges.append(move(c_before, "head", [(1, 0), (2, 3)]))
    up_final, down_final = final_update(blocks == 1, scalars, mine, theirs, state)
    is_edge = (inner == 0).astype(F32)
    layer_out = jnp.stack(
        [(acc + is_edge * edge.astype(F32)).astype(BF) for acc, edge in zip(accs, edges)]
    )
    return layer_out, up_final, down_final


def solution(mesh):
    in_specs = (
        P(None, "ctx", "head"),
        P(None, None, "ctx", "head"),
        P(None, "head"),
        P(None, "head", None, None),
        P("head", None, None),
        P("head", None, "ctx"),
    )
    out_specs = (P(None, "ctx", "head"), P(None, "head", None, None), P("head", None, None))
    return jax.shard_map(body, mesh=mesh, in_specs=in_specs, out_specs=out_specs, check_vma=False)
```

```python
import functools
import math

import jax
import jax.numpy as jnp
from jax import lax
from jax.experimental import pallas as pl
from jax.experimental.pallas import tpu as pltpu
from jax.sharding import PartitionSpec as P

HD = 128
WIN = 512
TILE = 256
MASKED = -1e30
BF = jnp.bfloat16
F32 = jnp.float32
LIMIT = 48 * 1024 * 1024


def mm(a, b):
    return jnp.dot(a, b, preferred_element_type=F32)


def mm_nt(a, b):
    return lax.dot_general(a, b, (((1,), (1,)), ((), ())), preferred_element_type=F32)


def mm_tn(a, b):
    return lax.dot_general(a, b, (((0,), (0,)), ((), ())), preferred_element_type=F32)


def sigmoid(x):
    return 0.5 + 0.5 * jnp.tanh(0.5 * x)


def whole(array):
    zeros = (0,) * array.ndim
    return pl.BlockSpec(array.shape, lambda *_: zeros)


def whole_out(shape):
    zeros = (0,) * len(shape)
    return pl.BlockSpec(shape, lambda *_: zeros)


def call(kernel, name, scalars, inputs, specs, outs, earlier=(), scratch=(), grid=(1,), out_specs=None, aliases=None):
    single = not isinstance(outs, (list, tuple))
    outs_list = [outs] if single else list(outs)
    first = 1 + len(inputs)

    def ordered(*refs):
        kernel(*refs[:first], *refs[first + len(earlier) :])

    got = pl.pallas_call(
        ordered,
        out_shape=outs_list,
        grid_spec=pltpu.PrefetchScalarGridSpec(
            num_scalar_prefetch=1,
            grid=grid,
            in_specs=[*specs, *[pl.BlockSpec(memory_space=pl.ANY) for _ in earlier]],
            out_specs=out_specs or [whole_out(o.shape) for o in outs_list],
            scratch_shapes=list(scratch),
        ),
        input_output_aliases={k + 1: v for k, v in (aliases or {}).items()},
        compiler_params=pltpu.CompilerParams(vmem_limit_bytes=LIMIT),
        cost_estimate=pl.CostEstimate(flops=20 * 10**9, bytes_accessed=1, transcendentals=0),
        name=name,
    )(scalars, *inputs, *earlier)
    return got[0] if single else got


def like(array, dtype=None):
    return jax.ShapeDtypeStruct(array.shape, dtype or array.dtype)


def grads_kernel(block, step_scale, sc, k_ref, v_ref, lr_ref, w1_ref, w3_ref, w2_ref, keep_ref, send_ref, acc):
    step = pl.program_id(0)
    k = k_ref[...]
    w_two = w2_ref[...]
    rates = lr_ref[0, block : block + 1, :] * step_scale
    rates = jnp.broadcast_to(rates, (HD, rates.shape[1])).T[:, :1]
    out_grad = (-rates * v_ref[...].astype(F32)).astype(BF)
    gate = mm(k, w1_ref[...])
    up = mm(k, w3_ref[...])
    hidden_grad = mm_nt(out_grad, w_two)
    sig = sigmoid(gate)
    gate_sig = gate * sig
    hidden = (gate_sig * up).astype(BF)
    up_grad = (hidden_grad * gate_sig).astype(BF)
    gate_grad = (hidden_grad * up * sig * (1.0 + gate - gate_sig)).astype(BF)
    parts = (mm_tn(k, gate_grad), mm_tn(k, up_grad), mm_tn(hidden, out_grad))

    @pl.when(step == 0)
    def _():
        for i, part in enumerate(parts):
            acc[i] = part

    @pl.when(step > 0)
    def _():
        for i, part in enumerate(parts):
            acc[i] = acc[i] + part

    @pl.when(step == pl.num_programs(0) - 1)
    def _():
        half = keep_ref.shape[1]
        own = pl.multiple_of(sc[0] * half, half)
        other = pl.multiple_of((1 - sc[0]) * half, half)
        keep_ref[...] = acc[:, pl.ds(own, half), :].astype(BF)
        send_ref[...] = acc[:, pl.ds(other, half), :].astype(BF)


def block_grads(block, scalars, projected, learn_rates, weights, step_scale, weight_specs, earlier=()):
    _, _, rows, feats = projected.shape
    half = feats // 2
    shape = jax.ShapeDtypeStruct((3, half, feats), BF)
    tile = min(TILE, rows)
    return call(
        functools.partial(grads_kernel, block, step_scale),
        f"grads_{block}",
        scalars,
        (projected, projected, learn_rates, *weights),
        [
            pl.BlockSpec((None, None, tile, feats), lambda i, s: (1, block, i, 0)),
            pl.BlockSpec((None, None, tile, feats), lambda i, s: (2, block, i, 0)),
            pl.BlockSpec((1, learn_rates.shape[1], tile), lambda i, s: (0, 0, i)),
            *weight_specs,
        ],
        [shape, shape],
        scratch=[pltpu.VMEM((3, feats, feats), F32)],
        grid=(rows // tile,),
        earlier=earlier,
    )


def attend_rows(q, keys, values, usable):
    rows = q.shape[0]
    row_ids = lax.broadcasted_iota(jnp.int32, (rows, rows), 0)
    col_ids = lax.broadcasted_iota(jnp.int32, (rows, rows), 1)
    scale = math.log2(math.e) / math.sqrt(HD)
    scores = []
    last = len(keys) - 1
    for i, (key, before) in enumerate(keys):
        s = mm_nt(q, key)
        if before:
            s = s + usable
        if i == 0:
            s = jnp.where(col_ids > row_ids, s, MASKED)
        if i == last:
            s = jnp.where(col_ids <= row_ids, s, MASKED)
        scores.append(s)
    top = functools.reduce(jnp.maximum, scores)
    peak = jnp.max(top, axis=-1, keepdims=True) * scale
    total = None
    result = None
    for s, value in zip(scores, values):
        lifted = jnp.exp2(s * scale - peak)
        total = lifted if total is None else total + lifted
        part = mm(lifted.astype(BF), value)
        result = part if result is None else result + part
    return (result / jnp.sum(total, axis=-1, keepdims=True)).astype(BF)


def attend(q_ref, k_ref, v_ref, halo_ref, usable, store):
    rows, feats = q_ref.shape
    tile = min(TILE, rows)
    for start in range(0, rows, tile):
        for head in range(feats // HD):
            cols = slice(head * HD, (head + 1) * HD)
            keys, values = [], []
            for at in range(start - WIN, start + tile, tile):
                before = at < 0
                where = slice(at + WIN, at + WIN + tile) if before else slice(at, at + tile)
                keys.append(((halo_ref[0, where, cols] if before else k_ref[where, cols]), before))
                values.append(halo_ref[1, where, cols] if before else v_ref[where, cols])
            store(slice(start, start + tile), cols, attend_rows(q_ref[start : start + tile, cols], keys, values, usable))


def fast_rows(q, w_one, w_three, w_two):
    gate = mm(q, w_one)
    up = mm(q, w_three)
    hidden = (gate * sigmoid(gate) * up).astype(BF)
    result = mm(hidden, w_two)
    return result * lax.rsqrt(jnp.mean(result * result, axis=-1, keepdims=True) + 1e-05)


def usable_bias(block, sc):
    return jnp.where((sc[1] > 0) | (block > 0), 0.0, MASKED).astype(F32)


def mixed_kernel(block, sc, q_ref, k_ref, v_ref, halo_ref, w1_ref, w3_ref, w2_ref, out_ref, att):
    def store(rows, cols, value):
        att[rows, cols] = value

    attend(q_ref, k_ref, v_ref, halo_ref, usable_bias(block, sc), store)
    rows = q_ref.shape[0]
    tile = min(TILE, rows)
    for start in range(0, rows, tile):
        at = slice(start, start + tile)
        fast = fast_rows(q_ref[at, :], w1_ref[...], w3_ref[...], w2_ref[...])
        out_ref[at, :] = (att[at, :].astype(F32) + fast).astype(BF)


def attend_kernel(block, sc, q_ref, k_ref, v_ref, halo_ref, out_ref):
    def store(rows, cols, value):
        out_ref[rows, cols] = value

    attend(q_ref, k_ref, v_ref, halo_ref, usable_bias(block, sc), store)


def qkv_specs(block, projected):
    _, _, rows, feats = projected.shape
    return [
        pl.BlockSpec((None, None, rows, feats), functools.partial(lambda kind, i, s: (kind, block, 0, 0), kind))
        for kind in range(3)
    ]


def attention_only(block, scalars, projected, halo, earlier=()):
    _, _, rows, feats = projected.shape
    return call(
        functools.partial(attend_kernel, block),
        f"attend_{block}",
        scalars,
        (projected, projected, projected, halo),
        [*qkv_specs(block, projected), whole(halo)],
        jax.ShapeDtypeStruct((rows, feats), BF),
        earlier=earlier,
    )


def mixed_first(block, scalars, projected, halo, weights, weight_specs, earlier=()):
    _, _, rows, feats = projected.shape
    return call(
        functools.partial(mixed_kernel, block),
        f"mixed_{block}",
        scalars,
        (projected, projected, projected, halo, *weights),
        [*qkv_specs(block, projected), whole(halo), *weight_specs],
        jax.ShapeDtypeStruct((rows, feats), BF),
        scratch=[pltpu.VMEM((rows, feats), BF)],
        earlier=earlier,
    )


def renorm_into(sc, old, mine_ref, theirs_ref, moved):
    half = mine_ref.shape[1]
    own = pl.multiple_of(sc[0] * half, half)
    other = pl.multiple_of((1 - sc[0]) * half, half)
    for i in range(3):
        before = jnp.zeros((), F32)
        after = jnp.zeros((), F32)
        for start, part in ((own, mine_ref), (other, theirs_ref)):
            w = old(i, pl.ds(start, half)).astype(F32)
            new = w - part[i].astype(F32)
            moved[i, pl.ds(start, half), :] = new
            before += jnp.sum(w * w)
            after += jnp.sum(new * new)
        ratio = jnp.sqrt(before) / jnp.sqrt(after + 1e-06)
        moved[i] = moved[i] * ratio


def update_kernel(first, sc, mine_ref, theirs_ref, up_ref, down_ref, q_ref, att_ref, mix_ref, new_ref, new_bf_ref):
    if first:
        old = lambda i, rows: up_ref[i, 0, rows, :] if i < 2 else down_ref[0, rows, :]
    else:
        old = lambda i, rows: up_ref[i, rows, :]
    renorm_into(sc, old, mine_ref, theirs_ref, new_ref)
    new_bf_ref[...] = new_ref[...].astype(BF)
    rows = q_ref.shape[0]
    tile = min(TILE, rows)
    for start in range(0, rows, tile):
        at = slice(start, start + tile)
        fast = fast_rows(q_ref[at, :], new_bf_ref[0], new_bf_ref[1], new_bf_ref[2])
        mix_ref[at, :] = (att_ref[at, :].astype(F32) + fast).astype(BF)


def update_and_mix(block, scalars, mine, theirs, state, projected, attended, earlier=()):
    _, _, rows, feats = projected.shape
    first = block == 1
    return call(
        functools.partial(update_kernel, first),
        f"update_{block}",
        scalars,
        (mine, theirs, state[0], state[1], projected, attended),
        [
            whole(mine),
            whole(theirs),
            whole(state[0]),
            whole(state[1]),
            pl.BlockSpec((None, None, rows, feats), lambda i, s: (0, block, 0, 0)),
            whole(attended),
        ],
        [
            jax.ShapeDtypeStruct((rows, feats), BF),
            jax.ShapeDtypeStruct((3, feats, feats), F32),
            jax.ShapeDtypeStruct((3, feats, feats), BF),
        ],
        earlier=earlier,
    )


def final_kernel(first, sc, mine_ref, theirs_ref, up_ref, down_ref, up_out, down_out, moved):
    if first:
        old = lambda i, rows: up_ref[i, 0, rows, :] if i < 2 else down_ref[0, rows, :]
    else:
        old = lambda i, rows: up_ref[i, rows, :]
    renorm_into(sc, old, mine_ref, theirs_ref, moved)
    up_out[0, 0] = moved[0]
    up_out[1, 0] = moved[1]
    down_out[0] = moved[2]


def final_update(first, scalars, mine, theirs, state, earlier=()):
    feats = mine.shape[2]
    return call(
        functools.partial(final_kernel, first),
        "final_update",
        scalars,
        (mine, theirs, *state),
        [whole(mine), whole(theirs), whole(state[0]), whole(state[1])],
        [jax.ShapeDtypeStruct((2, 1, feats, feats), F32), jax.ShapeDtypeStruct((1, feats, feats), F32)],
        scratch=[pltpu.VMEM((3, feats, feats), F32)],
        earlier=earlier,
    )


def pick_kernel(sc, w_ref, out_ref):
    half = out_ref.shape[1]
    feats = 2 * half
    for i in range(3):
        start = (sc[2] ^ (i + 1)) * feats + sc[0] * half
        out_ref[i] = w_ref[pl.ds(pl.multiple_of(start, half), half), :]


def pick_parts(scalars, w_out, earlier=()):
    feats = w_out.shape[1]
    return call(
        pick_kernel,
        "pick_parts",
        scalars,
        (w_out,),
        [whole(w_out)],
        jax.ShapeDtypeStruct((3, feats // 2, feats), BF),
        earlier=earlier,
    )


def join_kernel(sc, mine_ref, theirs_ref, x_ref, out_ref, x_out_ref):
    half = mine_ref.shape[1]
    out_ref[:, pl.ds(pl.multiple_of(sc[0] * half, half), half), :] = mine_ref[...]
    out_ref[:, pl.ds(pl.multiple_of((1 - sc[0]) * half, half), half), :] = theirs_ref[...]


def join_halves(scalars, mine, theirs, x, earlier=()):
    count, half, feats = mine.shape
    return call(
        join_kernel,
        "join_halves",
        scalars,
        (mine, theirs, x),
        [whole(mine), whole(theirs), pl.BlockSpec(memory_space=pl.ANY)],
        [jax.ShapeDtypeStruct((count, 2 * half, feats), BF), like(x)],
        out_specs=[whole_out((count, 2 * half, feats)), pl.BlockSpec(memory_space=pl.ANY)],
        aliases={2: 1},
        earlier=earlier,
    )


def gate_kernel(sc, x_ref, x_out_ref):
    pass


def gate(scalars, x, earlier):
    return call(
        gate_kernel,
        "gate",
        scalars,
        (x,),
        [pl.BlockSpec(memory_space=pl.ANY)],
        like(x),
        out_specs=[pl.BlockSpec(memory_space=pl.ANY)],
        aliases={0: 0},
        earlier=earlier,
    )


def add_kernel(sc, a_ref, b_ref, out_ref):
    out_ref[...] = (a_ref[...].astype(F32) + b_ref[...].astype(F32)).astype(BF)


def add(scalars, a, b, earlier=()):
    return call(add_kernel, "add", scalars, (a, b), [whole(a), whole(b)], like(a, BF), earlier=earlier)


def pack_kernel(sc, k_ref, v_ref, out_ref):
    out_ref[0] = k_ref[...]
    out_ref[1] = v_ref[...]


def pack_halo(block, scalars, projected, last, earlier=()):
    _, _, rows, feats = projected.shape

    def which(s):
        return block if block == 0 else jnp.where(s[1] == last, block - 1, block)

    return call(
        pack_kernel,
        f"pack_{block}",
        scalars,
        (projected, projected),
        [
            pl.BlockSpec((None, None, WIN, feats), lambda i, s: (1, which(s), rows // WIN - 1, 0)),
            pl.BlockSpec((None, None, WIN, feats), lambda i, s: (2, which(s), rows // WIN - 1, 0)),
        ],
        jax.ShapeDtypeStruct((2, WIN, feats), BF),
        earlier=earlier,
    )


def edge_kernel(sc, m_ref, ya_ref, yb_ref, v_ref, out_ref):
    out_ref[...] = (mm(m_ref[...], v_ref[0]) + mm(ya_ref[...], v_ref[1]) + mm(yb_ref[...], v_ref[2])).astype(BF)


def edge_part(block, scalars, m, ya, yb, v, earlier=()):
    rows, feats = m.shape
    return call(
        edge_kernel,
        f"edge_{block}",
        scalars,
        (m, ya, yb, v),
        [whole(m), whole(ya), whole(yb), whole(v)],
        jax.ShapeDtypeStruct((rows, feats), BF),
        earlier=earlier,
    )


def own_kernel(sc, m_ref, x_ref, ya_ref, yb_ref, w_ref, hid_ref, out_ref):
    feats = m_ref.shape[1]
    head = sc[2]

    def weight(which):
        return w_ref[pl.ds(pl.multiple_of(which * feats, feats), feats), :]

    out_ref[...] = hid_ref[...].astype(F32) + mm(m_ref[...], weight(head))

    @pl.when(sc[3] == 1)
    def _():
        out_ref[...] = (
            out_ref[...]
            + mm(x_ref[...], weight(head ^ 1))
            + mm(ya_ref[...], weight(head ^ 3))
            + mm(yb_ref[...], weight(head ^ 2))
        )


def own_part(block, scalars, m, x, ya, yb, w_out, hidden_in, earlier=()):
    rows, feats = m.shape
    return call(
        own_kernel,
        f"own_{block}",
        scalars,
        (m, x, ya, yb, w_out, hidden_in),
        [
            whole(m),
            whole(x),
            whole(ya),
            whole(yb),
            whole(w_out),
            pl.BlockSpec((None, rows, feats), lambda i, s: (block, 0, 0)),
        ],
        jax.ShapeDtypeStruct((rows, feats), F32),
        earlier=earlier,
    )


def finish_kernel(sc, acc_ref, c_ref, *refs):
    refs[-1][...] = (acc_ref[...] + c_ref[...].astype(F32)).astype(BF)


def finish(block, blocks, scalars, acc, c, so_far, earlier=()):
    rows, feats = acc.shape
    return call(
        finish_kernel,
        f"finish_{block}",
        scalars,
        (acc, c, *so_far),
        [whole(acc), whole(c), *[pl.BlockSpec(memory_space=pl.ANY) for _ in so_far]],
        jax.ShapeDtypeStruct((blocks, rows, feats), BF),
        out_specs=[pl.BlockSpec((None, rows, feats), lambda i, s: (block, 0, 0))],
        aliases={2: 0} if so_far else None,
        earlier=earlier,
    )


def move(x, axis, pairs):
    return lax.ppermute(x, axis, pairs)


def flip(x, bit):
    count = lax.axis_size("ctx")
    return move(x, "ctx", [(i, i ^ (1 << bit)) for i in range(count)])


def partners(count, step):
    bits = list(range(1, count.bit_length() - 1))
    return [(i, i ^ (1 << (bits if i % 2 == 0 else bits[::-1])[step])) for i in range(count)]


def body(hidden_in, projected, w_out, fast_up, fast_down, learn_rates):
    blocks, rows, feats = hidden_in.shape
    ctx = lax.axis_index("ctx")
    head = lax.axis_index("head")
    ctx_count = lax.axis_size("ctx")
    steps = ctx_count.bit_length() - 2
    parity = ctx % 2
    inner = ((head == 1) | (head == 2)).astype(jnp.int32)
    scalars = jnp.stack([parity, ctx, head, inner]).astype(jnp.int32)
    step_scale = 1.0 / math.sqrt(rows * ctx_count)
    forward = [(i, i + 1) for i in range(ctx_count - 1)]
    around = forward + [(ctx_count - 1, 0)]
    edge_in = [(0, 1), (3, 2)]
    middle = [(1, 2), (2, 1)]
    up_spec = [
        pl.BlockSpec((None, None, feats, feats), lambda *_: (0, 0, 0, 0)),
        pl.BlockSpec((None, None, feats, feats), lambda *_: (1, 0, 0, 0)),
        pl.BlockSpec((None, feats, feats), lambda *_: (0, 0, 0)),
    ]
    bf_spec = [
        pl.BlockSpec((None, feats, feats), functools.partial(lambda k, *_: (k, 0, 0), k)) for k in range(3)
    ]

    weights, specs = (fast_up, fast_up, fast_down), up_spec
    state = (fast_up, fast_down)
    edge_out = [(1, 0), (2, 3)]

    kv_now = pack_halo(0, scalars, projected, ctx_count - 1)
    halo = move(kv_now, "ctx", forward)
    keep, send = block_grads(0, scalars, projected, learn_rates, weights, step_scale, specs, earlier=(kv_now,))
    v_send = pick_parts(scalars, w_out, earlier=(send,))
    total = add(scalars, keep, flip(send, 0), earlier=(v_send,))
    received = move(total, "ctx", partners(ctx_count, 0))
    v_send = gate(scalars, v_send, earlier=(total,))
    v_mine = move(v_send, "head", edge_in)
    v_other = flip(v_mine, 0)
    mixed = mixed_first(0, scalars, projected, halo, weights, specs, earlier=(v_send,))
    x = move(mixed, "head", edge_in)
    ya = move(mixed, "head", middle)
    last = mixed
    so_far = ()
    for block in range(1, blocks):
        for step in range(steps):
            total = last = add(scalars, total, received, earlier=(last,))
            if step + 1 < steps:
                received = move(total, "ctx", partners(ctx_count, step + 1))
            if step == 0:
                kv_now = last = pack_halo(block, scalars, projected, ctx_count - 1, earlier=(last,))
                halo = move(kv_now, "ctx", around)
        theirs = flip(total, 0)
        if block == 1:
            v, x = join_halves(scalars, v_mine, v_other, x, earlier=(last, ya))
            last = v
        else:
            x = last = gate(scalars, x, earlier=(last, ya))
        yb = move(x, "head", middle)
        attended = attention_only(block, scalars, projected, halo, earlier=(last,))
        mixed_next, new, new_bf = update_and_mix(block, scalars, total, theirs, state, projected, attended)
        weights, specs = (new_bf, new_bf, new_bf), bf_spec
        state = (new, new_bf)
        x_next = move(mixed_next, "head", edge_in)
        ya_next = move(mixed_next, "head", middle)
        keep, send = block_grads(
            block, scalars, projected, learn_rates, weights, step_scale, specs, earlier=(mixed_next,)
        )
        c = edge_part(block - 1, scalars, mixed, ya, yb, v, earlier=(send,))
        c_there = move(c, "head", edge_out)
        total = add(scalars, keep, flip(send, 0), earlier=(c,))
        received = move(total, "ctx", partners(ctx_count, 0))
        acc = last = own_part(block - 1, scalars, mixed, x, ya, yb, w_out, hidden_in, earlier=(total,))
        if block < blocks - 1:
            so_far = (finish(block - 1, blocks, scalars, acc, c_there, so_far),)
            last = so_far[0]
        mixed, x, ya = mixed_next, x_next, ya_next
    x = last = gate(scalars, x, earlier=(last, ya))
    yb = move(x, "head", middle)
    for step in range(steps):
        total = last = add(scalars, total, received, earlier=(last,))
        if step + 1 < steps:
            received = move(total, "ctx", partners(ctx_count, step + 1))
        if step == 0:
            c = last = edge_part(blocks - 1, scalars, mixed, ya, yb, v, earlier=(last,))
            c_last = move(c, "head", edge_out)
    theirs = flip(total, 0)
    acc_last = own_part(blocks - 1, scalars, mixed, x, ya, yb, w_out, hidden_in, earlier=(last,))
    up_final, down_final = final_update(blocks == 1, scalars, total, theirs, state, earlier=(acc_last,))
    out = finish(blocks - 2, blocks, scalars, acc, c_there, so_far, earlier=(up_final,))
    layer_out = finish(blocks - 1, blocks, scalars, acc_last, c_last, (out,))
    return layer_out, up_final, down_final


def solution(mesh):
    in_specs = (
        P(None, "ctx", "head"),
        P(None, None, "ctx", "head"),
        P(None, "head"),
        P(None, "head", None, None),
        P("head", None, None),
        P("head", None, "ctx"),
    )
    out_specs = (P(None, "ctx", "head"), P(None, "head", None, None), P("head", None, None))
    return jax.shard_map(body, mesh=mesh, in_specs=in_specs, out_specs=out_specs, check_vma=False)
```

```python
import functools
import math

import jax
import jax.numpy as jnp
from jax import lax
from jax.experimental import pallas as pl
from jax.experimental.pallas import tpu as pltpu
from jax.sharding import PartitionSpec as P

HD = 128
WIN = 512
TILE = 256
MASKED = -1e30
BF = jnp.bfloat16
F32 = jnp.float32
PARTS = 1
LIMIT = 48 * 1024 * 1024


def mm(a, b):
    return jnp.dot(a, b, preferred_element_type=F32)


def mm_nt(a, b):
    return lax.dot_general(a, b, (((1,), (1,)), ((), ())), preferred_element_type=F32)


def mm_tn(a, b):
    return lax.dot_general(a, b, (((0,), (0,)), ((), ())), preferred_element_type=F32)


def sigmoid(x):
    return 0.5 + 0.5 * jnp.tanh(0.5 * x)


def whole(array):
    zeros = (0,) * array.ndim
    return pl.BlockSpec(array.shape, lambda *_: zeros)


def whole_out(shape):
    zeros = (0,) * len(shape)
    return pl.BlockSpec(shape, lambda *_: zeros)


def call(kernel, name, scalars, inputs, specs, outs, earlier=(), scratch=(), grid=(1,), out_specs=None, aliases=None, limit=LIMIT):
    single = not isinstance(outs, (list, tuple))
    outs_list = [outs] if single else list(outs)
    first = 1 + len(inputs)

    def ordered(*refs):
        kernel(*refs[:first], *refs[first + len(earlier) :])

    got = pl.pallas_call(
        ordered,
        out_shape=outs_list,
        grid_spec=pltpu.PrefetchScalarGridSpec(
            num_scalar_prefetch=1,
            grid=grid,
            in_specs=[*specs, *[pl.BlockSpec(memory_space=pl.ANY) for _ in earlier]],
            out_specs=out_specs or [whole_out(o.shape) for o in outs_list],
            scratch_shapes=list(scratch),
        ),
        input_output_aliases={k + 1: v for k, v in (aliases or {}).items()},
        compiler_params=pltpu.CompilerParams(vmem_limit_bytes=limit),
        cost_estimate=pl.CostEstimate(flops=20 * 10**9, bytes_accessed=1, transcendentals=0),
        name=name,
    )(scalars, *inputs, *earlier)
    return got[0] if single else got


def like(array, dtype=None):
    return jax.ShapeDtypeStruct(array.shape, dtype or array.dtype)


def grads_kernel(block, step_scale, sc, k_ref, v_ref, lr_ref, w1_ref, w3_ref, w2_ref, keep_ref, send_ref, acc):
    step = pl.program_id(0)
    k = k_ref[...]
    w_two = w2_ref[...]
    rates = lr_ref[0, block : block + 1, :] * step_scale
    rates = jnp.broadcast_to(rates, (HD, rates.shape[1])).T[:, :1]
    out_grad = (-rates * v_ref[...].astype(F32)).astype(BF)
    gate = mm(k, w1_ref[...])
    up = mm(k, w3_ref[...])
    hidden_grad = mm_nt(out_grad, w_two)
    sig = sigmoid(gate)
    gate_sig = gate * sig
    hidden = (gate_sig * up).astype(BF)
    up_grad = (hidden_grad * gate_sig).astype(BF)
    gate_grad = (hidden_grad * up * sig * (1.0 + gate - gate_sig)).astype(BF)
    parts = (mm_tn(k, gate_grad), mm_tn(k, up_grad), mm_tn(hidden, out_grad))

    @pl.when(step == 0)
    def _():
        for i, part in enumerate(parts):
            acc[i] = part

    @pl.when(step > 0)
    def _():
        for i, part in enumerate(parts):
            acc[i] = acc[i] + part

    @pl.when(step == pl.num_programs(0) - 1)
    def _():
        half = keep_ref.shape[1]
        own = pl.multiple_of(sc[0] * half, half)
        other = pl.multiple_of((1 - sc[0]) * half, half)
        keep_ref[...] = acc[:, pl.ds(own, half), :]
        send_ref[...] = acc[:, pl.ds(other, half), :].astype(BF)


def block_grads(block, scalars, projected, learn_rates, weights, step_scale, weight_specs, earlier=()):
    _, _, rows, feats = projected.shape
    half = feats // 2
    shape = jax.ShapeDtypeStruct((3, half, feats), BF)
    tile = min(TILE, rows)
    return call(
        functools.partial(grads_kernel, block, step_scale),
        f"grads_{block}",
        scalars,
        (projected, projected, learn_rates, *weights),
        [
            pl.BlockSpec((None, None, tile, feats), lambda i, s: (1, block, i, 0)),
            pl.BlockSpec((None, None, tile, feats), lambda i, s: (2, block, i, 0)),
            pl.BlockSpec((1, learn_rates.shape[1], tile), lambda i, s: (0, 0, i)),
            *weight_specs,
        ],
        [jax.ShapeDtypeStruct(shape.shape, F32), shape],
        scratch=[pltpu.VMEM((3, feats, feats), F32)],
        grid=(rows // tile,),
        earlier=earlier,
    )


def attend_rows(q, keys, values, usable):
    rows = q.shape[0]
    row_ids = lax.broadcasted_iota(jnp.int32, (rows, rows), 0)
    col_ids = lax.broadcasted_iota(jnp.int32, (rows, rows), 1)
    scale = math.log2(math.e) / math.sqrt(HD)
    scores = []
    last = len(keys) - 1
    for i, (key, before) in enumerate(keys):
        s = mm_nt(q, key)
        if before:
            s = s + usable
        if i == 0:
            s = jnp.where(col_ids > row_ids, s, MASKED)
        if i == last:
            s = jnp.where(col_ids <= row_ids, s, MASKED)
        scores.append(s)
    top = functools.reduce(jnp.maximum, scores)
    peak = jnp.max(top, axis=-1, keepdims=True) * scale
    total = None
    result = None
    for s, value in zip(scores, values):
        lifted = jnp.exp2(s * scale - peak)
        total = lifted if total is None else total + lifted
        part = mm(lifted.astype(BF), value)
        result = part if result is None else result + part
    return (result / jnp.sum(total, axis=-1, keepdims=True)).astype(BF)


def attend(q_ref, k_ref, v_ref, halo_ref, usable, store):
    rows, feats = q_ref.shape
    tile = min(TILE, rows)
    for start in range(0, rows, tile):
        for head in range(feats // HD):
            cols = slice(head * HD, (head + 1) * HD)
            keys, values = [], []
            for at in range(start - WIN, start + tile, tile):
                before = at < 0
                where = slice(at + WIN, at + WIN + tile) if before else slice(at, at + tile)
                keys.append(((halo_ref[0, where, cols] if before else k_ref[where, cols]), before))
                values.append(halo_ref[1, where, cols] if before else v_ref[where, cols])
            store(slice(start, start + tile), cols, attend_rows(q_ref[start : start + tile, cols], keys, values, usable))


def fast_rows(q, w_one, w_three, w_two):
    gate = mm(q, w_one)
    up = mm(q, w_three)
    hidden = (gate * sigmoid(gate) * up).astype(BF)
    result = mm(hidden, w_two)
    return result * lax.rsqrt(jnp.mean(result * result, axis=-1, keepdims=True) + 1e-05)


def usable_bias(block, sc):
    return jnp.where((sc[1] > 0) | (block > 0), 0.0, MASKED).astype(F32)


def mixed_kernel(block, sc, q_ref, k_ref, v_ref, halo_ref, w1_ref, w3_ref, w2_ref, out_ref, att):
    def store(rows, cols, value):
        att[rows, cols] = value

    attend(q_ref, k_ref, v_ref, halo_ref, usable_bias(block, sc), store)
    rows = q_ref.shape[0]
    tile = min(TILE, rows)
    for start in range(0, rows, tile):
        at = slice(start, start + tile)
        fast = fast_rows(q_ref[at, :], w1_ref[...], w3_ref[...], w2_ref[...])
        out_ref[at, :] = (att[at, :].astype(F32) + fast).astype(BF)


def attend_kernel(block, sc, q_ref, k_ref, v_ref, halo_ref, out_ref):
    def store(rows, cols, value):
        out_ref[rows, cols] = value

    attend(q_ref, k_ref, v_ref, halo_ref, usable_bias(block, sc), store)


def qkv_specs(block, projected):
    _, _, rows, feats = projected.shape
    return [
        pl.BlockSpec((None, None, rows, feats), functools.partial(lambda kind, i, s: (kind, block, 0, 0), kind))
        for kind in range(3)
    ]


def attention_only(block, scalars, projected, halo, earlier=()):
    _, _, rows, feats = projected.shape
    return call(
        functools.partial(attend_kernel, block),
        f"attend_{block}",
        scalars,
        (projected, projected, projected, halo),
        [*qkv_specs(block, projected), whole(halo)],
        jax.ShapeDtypeStruct((rows, feats), BF),
        earlier=earlier,
    )


def mixed_first(block, scalars, projected, halo, weights, weight_specs, earlier=()):
    _, _, rows, feats = projected.shape
    return call(
        functools.partial(mixed_kernel, block),
        f"mixed_{block}",
        scalars,
        (projected, projected, projected, halo, *weights),
        [*qkv_specs(block, projected), whole(halo), *weight_specs],
        jax.ShapeDtypeStruct((rows, feats), BF),
        scratch=[pltpu.VMEM((rows, feats), BF)],
        earlier=earlier,
    )


def halves(parity, mine, theirs):
    half = mine.shape[0]
    own = pl.multiple_of(parity * half, half)
    other = pl.multiple_of((1 - parity) * half, half)
    return ((pl.ds(own, half), mine), (pl.ds(other, half), theirs))


def renorm_one(old, mine, theirs, parity, put):
    before = jnp.zeros((), F32)
    after = jnp.zeros((), F32)
    moved = []
    for rows, part in halves(parity, mine, theirs):
        w = old(rows).astype(F32)
        new = w - part.astype(F32)
        moved.append((rows, new))
        before += jnp.sum(w * w)
        after += jnp.sum(new * new)
    ratio = jnp.sqrt(before) / jnp.sqrt(after + 1e-06)
    for rows, new in moved:
        put(rows, new * ratio)
    return ratio


def old_of(refs, i, rows):
    if len(refs) == 1:
        return refs[0][i, rows, :]
    return refs[0][i, 0, rows, :] if i < 2 else refs[1][0, rows, :]


def update_kernel(states, keep_state, parts, sc, mine_ref, theirs_ref, *refs):
    old, (q_ref, att_ref, mix_ref, new_bf_ref), rest = refs[:states], refs[states : states + 4], refs[states + 4 :]
    piece_refs, ratio_ref = rest[:parts], rest[parts]
    for i in range(3):

        def put(rows, value, i=i):
            new_bf_ref[i, rows, :] = value.astype(BF)
            if keep_state:
                rest[parts + 1][i, rows, :] = value

        ratio = renorm_one(lambda rows, i=i: old_of(old, i, rows), mine_ref[i], theirs_ref[i], sc[0], put)
        ratio_ref[i] = jnp.full(ratio_ref.shape[1:], ratio, F32)
    rows = q_ref.shape[0]
    tile = min(TILE, rows)
    for start in range(0, rows, tile):
        at = slice(start, start + tile)
        fast = fast_rows(q_ref[at, :], new_bf_ref[0], new_bf_ref[1], new_bf_ref[2])
        mix_ref[at, :] = (att_ref[at, :].astype(F32) + fast).astype(BF)
    for i, piece_ref in enumerate(piece_refs):
        size = piece_ref.shape[0]
        piece_ref[...] = mix_ref[i * size : (i + 1) * size, :]


def update_and_mix(block, scalars, mine, theirs, state, keep_state, projected, attended, parts, earlier=()):
    _, _, rows, feats = projected.shape
    pieces = parts if parts > 1 else 0
    got = call(
        functools.partial(update_kernel, len(state), keep_state, pieces),
        f"update_{block}",
        scalars,
        (mine, theirs, *state, projected, attended),
        [
            whole(mine),
            whole(theirs),
            *[whole(a) for a in state],
            pl.BlockSpec((None, None, rows, feats), lambda i, s: (0, block, 0, 0)),
            whole(attended),
        ],
        [
            jax.ShapeDtypeStruct((rows, feats), BF),
            jax.ShapeDtypeStruct((3, feats, feats), BF),
            *[jax.ShapeDtypeStruct((rows // parts, feats), BF) for _ in range(pieces)],
            jax.ShapeDtypeStruct((3, 8, HD), F32),
            *([jax.ShapeDtypeStruct((3, feats, feats), F32)] if keep_state else []),
        ],
        earlier=earlier,
    )
    new_state = got[-1] if keep_state else None
    ratio = got[-2] if keep_state else got[-1]
    return got[0], got[1], got[2 : 2 + pieces] or [got[0]], ratio, new_state


def final_kernel(states, sc, mine_ref, theirs_ref, mine_before, theirs_before, ratio_ref, *refs):
    old = refs[:states]
    up_out, down_out, token, now = refs[states:]
    token[...] = jnp.zeros_like(token)
    step = pl.program_id(0)

    def run(i, out):
        ratio = ratio_ref[i, 0:1, 0:1]
        for rows, part in halves(sc[0], mine_before[i], theirs_before[i]):
            now[rows, :] = (old_of(old, i, rows).astype(F32) - part.astype(F32)) * ratio

        def put(rows, value):
            out[rows, :] = value

        renorm_one(lambda rows: now[rows, :], mine_ref[...], theirs_ref[...], sc[0], put)

    for i in range(3):
        pl.when(step == i)(functools.partial(run, i, up_out if i < 2 else down_out))


def final_update(scalars, mine, theirs, mine_before, theirs_before, ratio, state, earlier=()):
    _, half, feats = mine.shape
    return call(
        functools.partial(final_kernel, len(state)),
        "final_update",
        scalars,
        (mine, theirs, mine_before, theirs_before, ratio, *state),
        [
            pl.BlockSpec((None, half, feats), lambda i, s: (i, 0, 0)),
            pl.BlockSpec((None, half, feats), lambda i, s: (i, 0, 0)),
            *[whole(a) for a in (mine_before, theirs_before, ratio, *state)],
        ],
        [
            jax.ShapeDtypeStruct((2, 1, feats, feats), F32),
            jax.ShapeDtypeStruct((1, feats, feats), F32),
            jax.ShapeDtypeStruct((8, HD), F32),
        ],
        out_specs=[
            pl.BlockSpec((None, None, feats, feats), lambda i, s: (jnp.minimum(i, 1), 0, 0, 0)),
            pl.BlockSpec((None, feats, feats), lambda i, s: (0, 0, 0)),
            pl.BlockSpec((8, HD), lambda i, s: (0, 0)),
        ],
        grid=(3,),
        scratch=[pltpu.VMEM((feats, feats), F32)],
        earlier=earlier,
    )


def pick_kernel(sc, w_ref, out_ref):
    half = out_ref.shape[1]
    feats = 2 * half
    for i in range(3):
        start = (sc[2] ^ (i + 1)) * feats + sc[0] * half
        out_ref[i] = w_ref[pl.ds(pl.multiple_of(start, half), half), :]


def pick_parts(scalars, w_out, earlier=()):
    feats = w_out.shape[1]
    return call(
        pick_kernel,
        "pick_parts",
        scalars,
        (w_out,),
        [whole(w_out)],
        jax.ShapeDtypeStruct((3, feats // 2, feats), BF),
        earlier=earlier,
    )


def gate_kernel(sc, x_ref, x_out_ref):
    pass


def gate(scalars, x, earlier):
    return call(
        gate_kernel,
        "gate",
        scalars,
        (x,),
        [pl.BlockSpec(memory_space=pl.ANY)],
        like(x),
        out_specs=[pl.BlockSpec(memory_space=pl.ANY)],
        aliases={0: 0},
        earlier=earlier,
    )


def add_kernel(sc, a_ref, b_ref, out_ref):
    out_ref[...] = (a_ref[...].astype(F32) + b_ref[...].astype(F32)).astype(BF)


def add(scalars, a, b, earlier=()):
    return call(add_kernel, "add", scalars, (a, b), [whole(a), whole(b)], like(a, BF), earlier=earlier)


def pack_kernel(sc, k_ref, v_ref, out_ref):
    out_ref[0] = k_ref[...]
    out_ref[1] = v_ref[...]


def pack_halo(block, scalars, projected, last, earlier=()):
    _, _, rows, feats = projected.shape

    def which(s):
        return block if block == 0 else jnp.where(s[1] == last, block - 1, block)

    return call(
        pack_kernel,
        f"pack_{block}",
        scalars,
        (projected, projected),
        [
            pl.BlockSpec((None, None, WIN, feats), lambda i, s: (1, which(s), rows // WIN - 1, 0)),
            pl.BlockSpec((None, None, WIN, feats), lambda i, s: (2, which(s), rows // WIN - 1, 0)),
        ],
        jax.ShapeDtypeStruct((2, WIN, feats), BF),
        earlier=earlier,
    )


def edge_kernel(sc, m_ref, ya_ref, yb_ref, mine_ref, theirs_ref, out_ref):
    half = mine_ref.shape[1]
    total = None
    for part, parity in ((mine_ref, sc[0]), (theirs_ref, 1 - sc[0])):
        cols = pl.ds(pl.multiple_of(parity * half, half), half)
        for i, ref in enumerate((m_ref, ya_ref, yb_ref)):
            term = mm(ref[:, cols], part[i])
            total = term if total is None else total + term
    out_ref[...] = total.astype(BF)


def part_spec(rows, feats, part):
    return pl.BlockSpec((rows, feats), lambda i, s: (part, 0))


def edge_part(name, scalars, part, m, ya, yb, v_mine, v_other, earlier=()):
    rows, feats = yb.shape
    return call(
        edge_kernel,
        f"edge_{name}",
        scalars,
        (m, ya, yb, v_mine, v_other),
        [part_spec(rows, feats, part), part_spec(rows, feats, part), whole(yb), whole(v_mine), whole(v_other)],
        jax.ShapeDtypeStruct((rows, feats), BF),
        earlier=earlier,
    )


def own_rows(sc, m, x, ya, yb, w_ref, hid, put, get):
    feats = w_ref.shape[1]
    head = sc[2]

    def weight(which):
        return w_ref[pl.ds(pl.multiple_of(which * feats, feats), feats), :]

    put(hid.astype(F32) + mm(m, weight(head)))

    @pl.when(sc[3] == 1)
    def _():
        put(get() + mm(x[...], weight(head ^ 1)) + mm(ya[...], weight(head ^ 3)) + mm(yb[...], weight(head ^ 2)))


def own_kernel(sc, m_ref, x_ref, ya_ref, yb_ref, w_ref, hid_ref, c_ref, *refs):
    out_ref, acc = refs[-2:]

    def put(value):
        acc[...] = value

    own_rows(sc, m_ref[...], x_ref, ya_ref, yb_ref, w_ref, hid_ref[...], put, lambda: acc[...])
    out_ref[...] = (acc[...] + c_ref[...].astype(F32)).astype(BF)


def own_part(block, scalars, m, x, ya, yb, w_out, hidden_in, c, so_far, earlier=()):
    rows, feats = m.shape
    return call(
        own_kernel,
        f"own_{block}",
        scalars,
        (m, x, ya, yb, w_out, hidden_in, c, *so_far),
        [
            *[whole(a) for a in (m, x, ya, yb, w_out)],
            pl.BlockSpec((None, rows, feats), lambda i, s: (block, 0, 0)),
            whole(c),
            *[pl.BlockSpec(memory_space=pl.ANY) for _ in so_far],
        ],
        like(hidden_in),
        out_specs=[pl.BlockSpec((None, rows, feats), lambda i, s: (block, 0, 0))],
        aliases={7: 0} if so_far else None,
        scratch=[pltpu.VMEM((rows, feats), F32)],
        earlier=earlier,
    )


def last_kernel(parts, sc, *refs):
    m_ref, ya_ref = refs[:2]
    xs, ybs = refs[2 : 2 + parts], refs[2 + parts : 2 + 2 * parts]
    w_ref, hid_ref, out_ref = refs[2 + 2 * parts :]
    rows = m_ref.shape[0] // parts
    for i in range(parts):
        at = pl.ds(i * rows, rows)

        def put(value, at=at):
            out_ref[at, :] = value

        own_rows(
            sc, m_ref[at, :], xs[i], ya_ref.at[at, :], ybs[i], w_ref, hid_ref[at, :], put, lambda at=at: out_ref[at, :]
        )


def own_last(block, scalars, m, xs, ya, ybs, w_out, hidden_in, earlier=()):
    rows, feats = m.shape
    return call(
        functools.partial(last_kernel, len(xs)),
        f"own_{block}",
        scalars,
        (m, ya, *xs, *ybs, w_out, hidden_in),
        [
            *[whole(a) for a in (m, ya, *xs, *ybs, w_out)],
            pl.BlockSpec((None, rows, feats), lambda i, s: (block, 0, 0)),
        ],
        jax.ShapeDtypeStruct((rows, feats), F32),
        earlier=earlier,
    )


def finish_kernel(parts, sc, acc_ref, *refs):
    out_ref = refs[-1]
    rows = acc_ref.shape[0] // parts
    for i in range(parts):
        at = pl.ds(i * rows, rows)
        out_ref[at, :] = (acc_ref[at, :] + refs[i][...].astype(F32)).astype(BF)


def finish(block, scalars, acc, cs, so_far, earlier=()):
    rows, feats = acc.shape
    return call(
        functools.partial(finish_kernel, len(cs)),
        "finish",
        scalars,
        (acc, *cs, *so_far),
        [whole(acc), *[whole(c) for c in cs], *[pl.BlockSpec(memory_space=pl.ANY) for _ in so_far]],
        like(so_far[0]) if so_far else None,
        out_specs=[pl.BlockSpec((None, rows, feats), lambda i, s: (block, 0, 0))],
        aliases={1 + len(cs): 0},
        earlier=earlier,
    )


def move(x, axis, pairs):
    return lax.ppermute(x, axis, pairs)


def flip(x, bit):
    count = lax.axis_size("ctx")
    return move(x, "ctx", [(i, i ^ (1 << bit)) for i in range(count)])


def partners(count, step):
    bits = list(range(1, count.bit_length() - 1))
    return [(i, i ^ (1 << (bits if i % 2 == 0 else bits[::-1])[step])) for i in range(count)]


def body(hidden_in, projected, w_out, fast_up, fast_down, learn_rates):
    blocks, rows, feats = hidden_in.shape
    ctx = lax.axis_index("ctx")
    head = lax.axis_index("head")
    ctx_count = lax.axis_size("ctx")
    steps = ctx_count.bit_length() - 2
    parity = ctx % 2
    inner = ((head == 1) | (head == 2)).astype(jnp.int32)
    scalars = jnp.stack([parity, ctx, head, inner]).astype(jnp.int32)
    step_scale = 1.0 / math.sqrt(rows * ctx_count)
    forward = [(i, i + 1) for i in range(ctx_count - 1)]
    around = forward + [(ctx_count - 1, 0)]
    edge_in = [(0, 1), (3, 2)]
    middle = [(1, 2), (2, 1)]
    up_spec = [
        pl.BlockSpec((None, None, feats, feats), lambda *_: (0, 0, 0, 0)),
        pl.BlockSpec((None, None, feats, feats), lambda *_: (1, 0, 0, 0)),
        pl.BlockSpec((None, feats, feats), lambda *_: (0, 0, 0)),
    ]
    bf_spec = [
        pl.BlockSpec((None, feats, feats), functools.partial(lambda k, *_: (k, 0, 0), k)) for k in range(3)
    ]

    weights, specs = (fast_up, fast_up, fast_down), up_spec
    state = (fast_up, fast_down)
    edge_out = [(1, 0), (2, 3)]

    kv_now = pack_halo(0, scalars, projected, ctx_count - 1)
    halo = move(kv_now, "ctx", forward)
    keep, send = block_grads(0, scalars, projected, learn_rates, weights, step_scale, specs, earlier=(kv_now,))
    v_send = pick_parts(scalars, w_out, earlier=(send,))
    v_mine = move(v_send, "head", edge_in)
    total = add(scalars, keep, flip(send, 0), earlier=(v_send,))
    received = move(total, "ctx", partners(ctx_count, 0))
    kv_now = pack_halo(1, scalars, projected, ctx_count - 1, earlier=(total,))
    halo_next = move(kv_now, "ctx", around)
    mixed = last = mixed_first(0, scalars, projected, halo, weights, specs, earlier=(kv_now,))
    xs = [move(mixed, "head", edge_in)]
    ya = move(mixed, "head", middle)
    so_far = ()
    for block in range(1, blocks):
        at_end = block == blocks - 1
        parts = PARTS if at_end else 1
        for step in range(steps):
            total = last = add(scalars, total, received, earlier=(last,))
            if step + 1 < steps:
                received = move(total, "ctx", partners(ctx_count, step + 1))
            if step == 0:
                attended = last = attention_only(block, scalars, projected, halo_next, earlier=(last,))
                if block == 1:
                    v_mine = last = gate(scalars, v_mine, earlier=(attended,))
                    v_other = flip(v_mine, 0)
        theirs = flip(total, 0)
        xs[0] = last = gate(scalars, xs[0], earlier=(total, last, ya))
        yb = move(xs[0], "head", middle)
        mixed_next, new_bf, pieces, ratio, new_state = update_and_mix(
            block, scalars, total, theirs, state, not at_end, projected, attended, parts, earlier=(last,)
        )
        xs_next = [move(pieces[0], "head", edge_in)]
        ya_next = move(mixed_next, "head", middle)
        xs_next += [move(piece, "head", edge_in) for piece in pieces[1:]]
        weights, specs = (new_bf, new_bf, new_bf), bf_spec
        keep, send = block_grads(
            block, scalars, projected, learn_rates, weights, step_scale, specs, earlier=(mixed_next,)
        )
        c = last = edge_part(block - 1, scalars, 0, mixed, ya, yb, v_mine, v_other, earlier=(send,))
        c_there = move(c, "head", edge_out)
        total_before, theirs_before = total, theirs
        total = last = add(scalars, keep, flip(send, 0), earlier=(last,))
        received = move(total, "ctx", partners(ctx_count, 0))
        if not at_end:
            kv_now = last = pack_halo(block + 1, scalars, projected, ctx_count - 1, earlier=(last,))
            halo_next = move(kv_now, "ctx", around)
            out = last = own_part(
                block - 1, scalars, mixed, xs[0], ya, yb, w_out, hidden_in, c_there, so_far, earlier=(last,)
            )
            so_far = (out,)
            state = (new_state,)
            mixed, xs, ya = mixed_next, xs_next, ya_next
    ybs = []
    for i in range(parts):
        xs_next[i] = last = gate(scalars, xs_next[i], earlier=(last,))
        ybs.append(move(xs_next[i], "head", middle))
    for step in range(steps):
        total = last = add(scalars, total, received, earlier=(last,))
        if step + 1 < steps:
            received = move(total, "ctx", partners(ctx_count, step + 1))
        if step == 0:
            c_last = []
            for i in range(parts):
                c = last = edge_part(
                    f"{blocks - 1}_{i}", scalars, i, mixed_next, ya_next, ybs[i], v_mine, v_other, earlier=(last,)
                )
                c_last.append(move(c, "head", edge_out))
            out = last = own_part(
                blocks - 2, scalars, mixed, xs[0], ya, yb, w_out, hidden_in, c_there, so_far, earlier=(last,)
            )
    theirs = flip(total, 0)
    acc = own_last(blocks - 1, scalars, mixed_next, xs_next, ya_next, ybs, w_out, hidden_in, earlier=(total,))
    up_final, down_final, token = final_update(
        scalars, total, theirs, total_before, theirs_before, ratio, state, earlier=(acc,)
    )
    out = finish(blocks - 1, scalars, acc, c_last, (out,), earlier=(token,))
    return out, up_final, down_final


def solution(mesh):
    in_specs = (
        P(None, "ctx", "head"),
        P(None, None, "ctx", "head"),
        P(None, "head"),
        P(None, "head", None, None),
        P("head", None, None),
        P("head", None, "ctx"),
    )
    out_specs = (P(None, "ctx", "head"), P(None, "head", None, None), P("head", None, None))
    return jax.shard_map(body, mesh=mesh, in_specs=in_specs, out_specs=out_specs, check_vma=False)
```

```python
import functools
import math

import jax
import jax.numpy as jnp
from jax import lax
from jax.experimental import pallas as pl
from jax.experimental.pallas import tpu as pltpu
from jax.sharding import PartitionSpec as P

HD = 128
WIN = 512
TILE = 256
MASKED = -1e30
BF = jnp.bfloat16
F32 = jnp.float32
PARTS = 2
LIMIT = 36 * 1024 * 1024


def mm(a, b):
    return jnp.dot(a, b, preferred_element_type=F32)


def mm_nt(a, b):
    return lax.dot_general(a, b, (((1,), (1,)), ((), ())), preferred_element_type=F32)


def mm_tn(a, b):
    return lax.dot_general(a, b, (((0,), (0,)), ((), ())), preferred_element_type=F32)


def sigmoid(x):
    return 0.5 + 0.5 * jnp.tanh(0.5 * x)


def whole(array):
    zeros = (0,) * array.ndim
    return pl.BlockSpec(array.shape, lambda *_: zeros)


def whole_out(shape):
    zeros = (0,) * len(shape)
    return pl.BlockSpec(shape, lambda *_: zeros)


def call(
    kernel, name, scalars, inputs, specs, outs, earlier=(), passing=(), scratch=(), grid=(1,), out_specs=None, aliases=None
):
    single = not isinstance(outs, (list, tuple)) and not passing
    outs_list = list(outs) if isinstance(outs, (list, tuple)) else [outs]
    any_spec = pl.BlockSpec(memory_space=pl.ANY)
    first = 1 + len(inputs)
    past = first + len(earlier) + len(passing)

    def ordered(*refs):
        kernel(*refs[:first], *refs[past : past + len(outs_list)], *refs[past + len(outs_list) + len(passing) :])

    pass_at = {first + len(earlier) + i: len(outs_list) + i for i in range(len(passing))}
    got = pl.pallas_call(
        ordered,
        out_shape=[*outs_list, *[like(x) for x in passing]],
        grid_spec=pltpu.PrefetchScalarGridSpec(
            num_scalar_prefetch=1,
            grid=grid,
            in_specs=[*specs, *[any_spec for _ in (*earlier, *passing)]],
            out_specs=[*(out_specs or [whole_out(o.shape) for o in outs_list]), *[any_spec for _ in passing]],
            scratch_shapes=list(scratch),
        ),
        input_output_aliases={**{k + 1: v for k, v in (aliases or {}).items()}, **pass_at},
        compiler_params=pltpu.CompilerParams(vmem_limit_bytes=LIMIT),
        cost_estimate=pl.CostEstimate(flops=20 * 10**9, bytes_accessed=1, transcendentals=0),
        name=name,
    )(scalars, *inputs, *earlier, *passing)
    return got[0] if single else got


def like(array, dtype=None):
    return jax.ShapeDtypeStruct(array.shape, dtype or array.dtype)


def grads_kernel(block, step_scale, sc, k_ref, v_ref, lr_ref, w1_ref, w3_ref, w2_ref, keep_ref, send_ref, acc):
    step = pl.program_id(0)
    k = k_ref[...]
    w_two = w2_ref[...]
    rates = lr_ref[0, block : block + 1, :] * step_scale
    rates = jnp.broadcast_to(rates, (HD, rates.shape[1])).T[:, :1]
    out_grad = (-rates * v_ref[...].astype(F32)).astype(BF)
    gate = mm(k, w1_ref[...])
    up = mm(k, w3_ref[...])
    hidden_grad = mm_nt(out_grad, w_two)
    sig = sigmoid(gate)
    gate_sig = gate * sig
    hidden = (gate_sig * up).astype(BF)
    up_grad = (hidden_grad * gate_sig).astype(BF)
    gate_grad = (hidden_grad * up * sig * (1.0 + gate - gate_sig)).astype(BF)
    parts = (mm_tn(k, gate_grad), mm_tn(k, up_grad), mm_tn(hidden, out_grad))

    @pl.when(step == 0)
    def _():
        for i, part in enumerate(parts):
            acc[i] = part

    @pl.when(step > 0)
    def _():
        for i, part in enumerate(parts):
            acc[i] = acc[i] + part

    @pl.when(step == pl.num_programs(0) - 1)
    def _():
        half = keep_ref.shape[1]
        own = pl.multiple_of(sc[0] * half, half)
        other = pl.multiple_of((1 - sc[0]) * half, half)
        keep_ref[...] = acc[:, pl.ds(own, half), :]
        send_ref[...] = acc[:, pl.ds(other, half), :].astype(BF)


def block_grads(block, scalars, projected, learn_rates, weights, step_scale, weight_specs, earlier=()):
    _, _, rows, feats = projected.shape
    half = feats // 2
    shape = jax.ShapeDtypeStruct((3, half, feats), BF)
    tile = min(TILE, rows)
    return call(
        functools.partial(grads_kernel, block, step_scale),
        f"grads_{block}",
        scalars,
        (projected, projected, learn_rates, *weights),
        [
            pl.BlockSpec((None, None, tile, feats), lambda i, s: (1, block, i, 0)),
            pl.BlockSpec((None, None, tile, feats), lambda i, s: (2, block, i, 0)),
            pl.BlockSpec((1, learn_rates.shape[1], tile), lambda i, s: (0, 0, i)),
            *weight_specs,
        ],
        [jax.ShapeDtypeStruct(shape.shape, F32), shape],
        scratch=[pltpu.VMEM((3, feats, feats), F32)],
        grid=(rows // tile,),
        earlier=earlier,
    )


def attend_rows(q, keys, values, usable):
    rows = q.shape[0]
    row_ids = lax.broadcasted_iota(jnp.int32, (rows, rows), 0)
    col_ids = lax.broadcasted_iota(jnp.int32, (rows, rows), 1)
    scale = math.log2(math.e) / math.sqrt(HD)
    scores = []
    last = len(keys) - 1
    for i, (key, before) in enumerate(keys):
        s = mm_nt(q, key)
        if before:
            s = s + usable
        if i == 0:
            s = jnp.where(col_ids > row_ids, s, MASKED)
        if i == last:
            s = jnp.where(col_ids <= row_ids, s, MASKED)
        scores.append(s)
    top = functools.reduce(jnp.maximum, scores)
    peak = jnp.max(top, axis=-1, keepdims=True) * scale
    total = None
    result = None
    for s, value in zip(scores, values):
        lifted = jnp.exp2(s * scale - peak)
        total = lifted if total is None else total + lifted
        part = mm(lifted.astype(BF), value)
        result = part if result is None else result + part
    return (result / jnp.sum(total, axis=-1, keepdims=True)).astype(BF)


def attend(q_ref, k_ref, v_ref, halo_ref, usable, store):
    rows, feats = q_ref.shape
    tile = min(TILE, rows)
    for start in range(0, rows, tile):
        for head in range(feats // HD):
            cols = slice(head * HD, (head + 1) * HD)
            keys, values = [], []
            for at in range(start - WIN, start + tile, tile):
                before = at < 0
                where = slice(at + WIN, at + WIN + tile) if before else slice(at, at + tile)
                keys.append(((halo_ref[0, where, cols] if before else k_ref[where, cols]), before))
                values.append(halo_ref[1, where, cols] if before else v_ref[where, cols])
            store(slice(start, start + tile), cols, attend_rows(q_ref[start : start + tile, cols], keys, values, usable))


def fast_rows(q, w_one, w_three, w_two):
    gate = mm(q, w_one)
    up = mm(q, w_three)
    hidden = (gate * sigmoid(gate) * up).astype(BF)
    result = mm(hidden, w_two)
    return result * lax.rsqrt(jnp.mean(result * result, axis=-1, keepdims=True) + 1e-05)


def usable_bias(block, sc):
    return jnp.where((sc[1] > 0) | (block > 0), 0.0, MASKED).astype(F32)


def mixed_kernel(block, sc, q_ref, k_ref, v_ref, halo_ref, w1_ref, w3_ref, w2_ref, out_ref, att):
    def store(rows, cols, value):
        att[rows, cols] = value

    attend(q_ref, k_ref, v_ref, halo_ref, usable_bias(block, sc), store)
    rows = q_ref.shape[0]
    tile = min(TILE, rows)
    for start in range(0, rows, tile):
        at = slice(start, start + tile)
        fast = fast_rows(q_ref[at, :], w1_ref[...], w3_ref[...], w2_ref[...])
        out_ref[at, :] = (att[at, :].astype(F32) + fast).astype(BF)


def attend_kernel(block, sc, q_ref, k_ref, v_ref, halo_ref, out_ref):
    def store(rows, cols, value):
        out_ref[rows, cols] = value

    attend(q_ref, k_ref, v_ref, halo_ref, usable_bias(block, sc), store)


def qkv_specs(block, projected):
    _, _, rows, feats = projected.shape
    return [
        pl.BlockSpec((None, None, rows, feats), functools.partial(lambda kind, i, s: (kind, block, 0, 0), kind))
        for kind in range(3)
    ]


def attention_only(block, scalars, projected, halo, earlier=(), passing=()):
    _, _, rows, feats = projected.shape
    return call(
        functools.partial(attend_kernel, block),
        f"attend_{block}",
        scalars,
        (projected, projected, projected, halo),
        [*qkv_specs(block, projected), whole(halo)],
        jax.ShapeDtypeStruct((rows, feats), BF),
        earlier=earlier,
        passing=passing,
    )


def mixed_first(block, scalars, projected, halo, weights, weight_specs, earlier=()):
    _, _, rows, feats = projected.shape
    return call(
        functools.partial(mixed_kernel, block),
        f"mixed_{block}",
        scalars,
        (projected, projected, projected, halo, *weights),
        [*qkv_specs(block, projected), whole(halo), *weight_specs],
        jax.ShapeDtypeStruct((rows, feats), BF),
        scratch=[pltpu.VMEM((rows, feats), BF)],
        earlier=earlier,
    )


def halves(parity, mine, theirs):
    half = mine.shape[0]
    own = pl.multiple_of(parity * half, half)
    other = pl.multiple_of((1 - parity) * half, half)
    return ((pl.ds(own, half), mine), (pl.ds(other, half), theirs))


def renorm_one(old, mine, theirs, parity, put, known=None):
    before = jnp.zeros((), F32) if known is None else known
    after = jnp.zeros((), F32)
    moved = []
    for rows, part in halves(parity, mine, theirs):
        w = old(rows).astype(F32)
        new = w - part.astype(F32)
        moved.append((rows, new))
        if known is None:
            before += jnp.sum(w * w)
        after += jnp.sum(new * new)
    ratio = jnp.sqrt(before) / jnp.sqrt(after + 1e-06)
    for rows, new in moved:
        put(rows, new * ratio)


def old_of(refs, i, rows):
    if len(refs) == 1:
        return refs[0][i, rows, :]
    return refs[0][i, 0, rows, :] if i < 2 else refs[1][0, rows, :]


def update_kernel(states, pieces, sc, mine_ref, theirs_ref, *refs):
    old, (q_ref, att_ref, mix_ref, new_bf_ref), piece_refs = refs[:states], refs[states : states + 4], refs[states + 4 :]
    for i in range(3):

        def put(rows, value, i=i):
            new_bf_ref[i, rows, :] = value.astype(BF)

        renorm_one(lambda rows, i=i: old_of(old, i, rows), mine_ref[i], theirs_ref[i], sc[0], put)
    rows = q_ref.shape[0]
    tile = min(TILE, rows)
    for start in range(0, rows, tile):
        at = slice(start, start + tile)
        fast = fast_rows(q_ref[at, :], new_bf_ref[0], new_bf_ref[1], new_bf_ref[2])
        mix_ref[at, :] = (att_ref[at, :].astype(F32) + fast).astype(BF)
    for i, piece_ref in enumerate(piece_refs):
        size = piece_ref.shape[0]
        piece_ref[...] = mix_ref[i * size : (i + 1) * size, :]


def update_and_mix(block, scalars, mine, theirs, state, projected, attended, parts, earlier=()):
    _, _, rows, feats = projected.shape
    pieces = parts if parts > 1 else 0
    got = call(
        functools.partial(update_kernel, len(state), pieces),
        f"update_{block}",
        scalars,
        (mine, theirs, *state, projected, attended),
        [
            whole(mine),
            whole(theirs),
            *[whole(a) for a in state],
            pl.BlockSpec((None, None, rows, feats), lambda i, s: (0, block, 0, 0)),
            whole(attended),
        ],
        [
            jax.ShapeDtypeStruct((rows, feats), BF),
            jax.ShapeDtypeStruct((3, feats, feats), BF),
            *[jax.ShapeDtypeStruct((rows // parts, feats), BF) for _ in range(pieces)],
        ],
        earlier=earlier,
    )
    return got[0], got[1], got[2:] or [got[0]]


def state_kernel(states, sc, mine_ref, theirs_ref, *refs):
    old, (new_ref, norm_ref) = refs[:states], refs[states:]
    for i in range(3):

        def put(rows, value, i=i):
            new_ref[i, rows, :] = value

        renorm_one(lambda rows, i=i: old_of(old, i, rows), mine_ref[i], theirs_ref[i], sc[0], put)
        norm_ref[i] = jnp.full(norm_ref.shape[1:], jnp.sum(new_ref[i] * new_ref[i]), F32)


def float_state(block, scalars, mine, theirs, state, earlier=()):
    feats = mine.shape[2]
    return call(
        functools.partial(state_kernel, len(state)),
        f"state_{block}",
        scalars,
        (mine, theirs, *state),
        [whole(mine), whole(theirs), *[whole(a) for a in state]],
        [jax.ShapeDtypeStruct((3, feats, feats), F32), jax.ShapeDtypeStruct((3, 8, HD), F32)],
        earlier=earlier,
    )


def final_kernel(sc, mine_ref, theirs_ref, old_ref, norm_ref, up_out, down_out, token):
    token[...] = jnp.zeros_like(token)
    step = pl.program_id(0)

    def run(out):
        def put(rows, value):
            out[rows, :] = value

        renorm_one(lambda rows: old_ref[rows, :], mine_ref[...], theirs_ref[...], sc[0], put, norm_ref[0:1, 0:1])

    pl.when(step < 2)(lambda: run(up_out))
    pl.when(step == 2)(lambda: run(down_out))


def final_update(scalars, mine, theirs, state, norms, earlier=()):
    _, half, feats = mine.shape
    return call(
        final_kernel,
        "final_update",
        scalars,
        (mine, theirs, state, norms),
        [
            pl.BlockSpec((None, half, feats), lambda i, s: (i, 0, 0)),
            pl.BlockSpec((None, half, feats), lambda i, s: (i, 0, 0)),
            pl.BlockSpec((None, feats, feats), lambda i, s: (i, 0, 0)),
            pl.BlockSpec((None, 8, HD), lambda i, s: (i, 0, 0)),
        ],
        [
            jax.ShapeDtypeStruct((2, 1, feats, feats), F32),
            jax.ShapeDtypeStruct((1, feats, feats), F32),
            jax.ShapeDtypeStruct((8, HD), F32),
        ],
        out_specs=[
            pl.BlockSpec((None, None, feats, feats), lambda i, s: (jnp.minimum(i, 1), 0, 0, 0)),
            pl.BlockSpec((None, feats, feats), lambda i, s: (0, 0, 0)),
            pl.BlockSpec((8, HD), lambda i, s: (0, 0)),
        ],
        grid=(3,),
        earlier=earlier,
    )


def pick_kernel(sc, w_ref, out_ref):
    half = out_ref.shape[1]
    feats = 2 * half
    for i in range(3):
        start = (sc[2] ^ (i + 1)) * feats + sc[0] * half
        out_ref[i] = w_ref[pl.ds(pl.multiple_of(start, half), half), :]


def pick_parts(scalars, w_out, earlier=()):
    feats = w_out.shape[1]
    return call(
        pick_kernel,
        "pick_parts",
        scalars,
        (w_out,),
        [whole(w_out)],
        jax.ShapeDtypeStruct((3, feats // 2, feats), BF),
        earlier=earlier,
    )


def gate_kernel(sc, x_ref, x_out_ref):
    pass


def gate(scalars, x, earlier):
    return call(
        gate_kernel,
        "gate",
        scalars,
        (x,),
        [pl.BlockSpec(memory_space=pl.ANY)],
        like(x),
        out_specs=[pl.BlockSpec(memory_space=pl.ANY)],
        aliases={0: 0},
        earlier=earlier,
    )


def split_kernel(sc, x_ref, *piece_refs):
    size = piece_refs[0].shape[0]
    for i, piece_ref in enumerate(piece_refs):
        piece_ref[...] = x_ref[i * size : (i + 1) * size, :]


def split(scalars, x, parts, earlier):
    rows, feats = x.shape
    piece = jax.ShapeDtypeStruct((rows // parts, feats), BF)
    return call(split_kernel, "split", scalars, (x,), [whole(x)], [piece] * parts, earlier=earlier)


def add_kernel(sc, a_ref, b_ref, out_ref):
    out_ref[...] = (a_ref[...].astype(F32) + b_ref[...].astype(F32)).astype(BF)


def add(scalars, a, b, earlier=(), passing=()):
    return call(add_kernel, "add", scalars, (a, b), [whole(a), whole(b)], like(a, BF), earlier=earlier, passing=passing)


def pack_kernel(sc, k_ref, v_ref, out_ref):
    out_ref[0] = k_ref[...]
    out_ref[1] = v_ref[...]


def pack_halo(block, scalars, projected, last, earlier=()):
    _, _, rows, feats = projected.shape

    def which(s):
        return block if block == 0 else jnp.where(s[1] == last, block - 1, block)

    return call(
        pack_kernel,
        f"pack_{block}",
        scalars,
        (projected, projected),
        [
            pl.BlockSpec((None, None, WIN, feats), lambda i, s: (1, which(s), rows // WIN - 1, 0)),
            pl.BlockSpec((None, None, WIN, feats), lambda i, s: (2, which(s), rows // WIN - 1, 0)),
        ],
        jax.ShapeDtypeStruct((2, WIN, feats), BF),
        earlier=earlier,
    )


def edge_kernel(sc, m_ref, ya_ref, yb_ref, mine_ref, theirs_ref, out_ref):
    half = mine_ref.shape[1]
    total = None
    for part, parity in ((mine_ref, sc[0]), (theirs_ref, 1 - sc[0])):
        cols = pl.ds(pl.multiple_of(parity * half, half), half)
        for i, ref in enumerate((m_ref, ya_ref, yb_ref)):
            term = mm(ref[:, cols], part[i])
            total = term if total is None else total + term
    out_ref[...] = total.astype(BF)


def part_spec(rows, feats, part):
    return pl.BlockSpec((rows, feats), lambda i, s: (part, 0))


def edge_part(name, scalars, part, m, ya, yb, v_mine, v_other, earlier=(), passing=()):
    rows, feats = yb.shape
    return call(
        edge_kernel,
        f"edge_{name}",
        scalars,
        (m, ya, yb, v_mine, v_other),
        [part_spec(rows, feats, part), part_spec(rows, feats, part), whole(yb), whole(v_mine), whole(v_other)],
        jax.ShapeDtypeStruct((rows, feats), BF),
        earlier=earlier,
        passing=passing,
    )


def own_rows(sc, m, x, ya, yb, w_ref, hid, put, get):
    feats = w_ref.shape[1]
    head = sc[2]

    def weight(which):
        return w_ref[pl.ds(pl.multiple_of(which * feats, feats), feats), :]

    put(hid.astype(F32) + mm(m, weight(head)))

    @pl.when(sc[3] == 1)
    def _():
        put(get() + mm(x[...], weight(head ^ 1)) + mm(ya[...], weight(head ^ 3)) + mm(yb[...], weight(head ^ 2)))


def own_kernel(sc, m_ref, x_ref, ya_ref, yb_ref, w_ref, hid_ref, c_ref, *refs):
    out_ref, token, acc = refs[-3:]
    token[...] = jnp.zeros_like(token)

    def put(value):
        acc[...] = value

    own_rows(sc, m_ref[...], x_ref, ya_ref, yb_ref, w_ref, hid_ref[...], put, lambda: acc[...])
    out_ref[...] = (acc[...] + c_ref[...].astype(F32)).astype(BF)


def own_part(block, scalars, m, x, ya, yb, w_out, hidden_in, c, so_far, earlier=()):
    rows, feats = m.shape
    return call(
        own_kernel,
        f"own_{block}",
        scalars,
        (m, x, ya, yb, w_out, hidden_in, c, *so_far),
        [
            *[whole(a) for a in (m, x, ya, yb, w_out)],
            pl.BlockSpec((None, rows, feats), lambda i, s: (block, 0, 0)),
            whole(c),
            *[pl.BlockSpec(memory_space=pl.ANY) for _ in so_far],
        ],
        [like(hidden_in), jax.ShapeDtypeStruct((8, HD), F32)],
        out_specs=[pl.BlockSpec((None, rows, feats), lambda i, s: (block, 0, 0)), whole_out((8, HD))],
        aliases={7: 0} if so_far else None,
        scratch=[pltpu.VMEM((rows, feats), F32)],
        earlier=earlier,
    )


def last_kernel(parts, sc, *refs):
    m_ref, ya_ref = refs[:2]
    xs, ybs = refs[2 : 2 + parts], refs[2 + parts : 2 + 2 * parts]
    w_ref, hid_ref, out_ref = refs[2 + 2 * parts :]
    rows = m_ref.shape[0] // parts
    for i in range(parts):
        at = pl.ds(i * rows, rows)

        def put(value, at=at):
            out_ref[at, :] = value

        own_rows(
            sc, m_ref[at, :], xs[i], ya_ref.at[at, :], ybs[i], w_ref, hid_ref[at, :], put, lambda at=at: out_ref[at, :]
        )


def own_last(block, scalars, m, xs, ya, ybs, w_out, hidden_in, earlier=()):
    rows, feats = m.shape
    return call(
        functools.partial(last_kernel, len(xs)),
        f"own_{block}",
        scalars,
        (m, ya, *xs, *ybs, w_out, hidden_in),
        [
            *[whole(a) for a in (m, ya, *xs, *ybs, w_out)],
            pl.BlockSpec((None, rows, feats), lambda i, s: (block, 0, 0)),
        ],
        jax.ShapeDtypeStruct((rows, feats), F32),
        earlier=earlier,
    )


def finish_kernel(parts, sc, acc_ref, *refs):
    out_ref = refs[-1]
    rows = acc_ref.shape[0] // parts
    for i in range(parts):
        at = pl.ds(i * rows, rows)
        out_ref[at, :] = (acc_ref[at, :] + refs[i][...].astype(F32)).astype(BF)


def finish(block, scalars, acc, cs, so_far, earlier=()):
    rows, feats = acc.shape
    return call(
        functools.partial(finish_kernel, len(cs)),
        "finish",
        scalars,
        (acc, *cs, *so_far),
        [whole(acc), *[whole(c) for c in cs], *[pl.BlockSpec(memory_space=pl.ANY) for _ in so_far]],
        like(so_far[0]) if so_far else None,
        out_specs=[pl.BlockSpec((None, rows, feats), lambda i, s: (block, 0, 0))],
        aliases={1 + len(cs): 0},
        earlier=earlier,
    )


def move(x, axis, pairs):
    return lax.ppermute(x, axis, pairs)


def flip(x, bit):
    count = lax.axis_size("ctx")
    return move(x, "ctx", [(i, i ^ (1 << bit)) for i in range(count)])


def partners(count, step):
    bits = list(range(1, count.bit_length() - 1))
    return [(i, i ^ (1 << (bits if i % 2 == 0 else bits[::-1])[step])) for i in range(count)]


def body(hidden_in, projected, w_out, fast_up, fast_down, learn_rates):
    blocks, rows, feats = hidden_in.shape
    ctx = lax.axis_index("ctx")
    head = lax.axis_index("head")
    ctx_count = lax.axis_size("ctx")
    steps = ctx_count.bit_length() - 2
    parity = ctx % 2
    inner = ((head == 1) | (head == 2)).astype(jnp.int32)
    scalars = jnp.stack([parity, ctx, head, inner]).astype(jnp.int32)
    step_scale = 1.0 / math.sqrt(rows * ctx_count)
    forward = [(i, i + 1) for i in range(ctx_count - 1)]
    around = forward + [(ctx_count - 1, 0)]
    edge_in = [(0, 1), (3, 2)]
    middle = [(1, 2), (2, 1)]
    up_spec = [
        pl.BlockSpec((None, None, feats, feats), lambda *_: (0, 0, 0, 0)),
        pl.BlockSpec((None, None, feats, feats), lambda *_: (1, 0, 0, 0)),
        pl.BlockSpec((None, feats, feats), lambda *_: (0, 0, 0)),
    ]
    bf_spec = [
        pl.BlockSpec((None, feats, feats), functools.partial(lambda k, *_: (k, 0, 0), k)) for k in range(3)
    ]

    weights, specs = (fast_up, fast_up, fast_down), up_spec
    state = (fast_up, fast_down)
    edge_out = [(1, 0), (2, 3)]

    kv_now = pack_halo(0, scalars, projected, ctx_count - 1)
    halo = move(kv_now, "ctx", forward)
    keep, send = block_grads(0, scalars, projected, learn_rates, weights, step_scale, specs, earlier=(kv_now,))
    keep = gate(scalars, keep, earlier=(send,))
    total = add(scalars, keep, flip(send, 0))
    received = move(total, "ctx", partners(ctx_count, 0))
    kv_now = pack_halo(1, scalars, projected, ctx_count - 1, earlier=(total,))
    halo_next = move(kv_now, "ctx", around)
    mixed = mixed_first(0, scalars, projected, halo, weights, specs, earlier=(kv_now,))
    x = move(mixed, "head", edge_in)
    ya = move(mixed, "head", middle)
    v_send = last = pick_parts(scalars, w_out, earlier=(mixed,))
    v_mine = move(v_send, "head", edge_in)
    so_far = ()
    for block in range(1, blocks):
        for step in range(steps):
            total = last = add(scalars, total, received, earlier=(last,))
            if step + 1 < steps:
                received = move(total, "ctx", partners(ctx_count, step + 1))
            if step == 0:
                attended = last = attention_only(block, scalars, projected, halo_next, earlier=(last,))
                x = last = gate(scalars, x, earlier=(last,))
                yb = move(x, "head", middle)
        theirs = flip(total, 0)
        ya = last = gate(scalars, ya, earlier=(total,))
        mixed_next, new_bf = update_and_mix(
            block, scalars, total, theirs, state, projected, attended, 1, earlier=(last,)
        )[:2]
        x_next = move(mixed_next, "head", edge_in)
        ya_next = move(mixed_next, "head", middle)
        weights, specs = (new_bf, new_bf, new_bf), bf_spec
        keep, send = block_grads(
            block, scalars, projected, learn_rates, weights, step_scale, specs, earlier=(mixed_next,)
        )
        if block == 1:
            v_mine = last = gate(scalars, v_mine, earlier=(send,))
            v_other = flip(v_mine, 0)
        else:
            keep = last = gate(scalars, keep, earlier=(send,))
        summed = add(scalars, keep, flip(send, 0), earlier=(last,))
        received = move(summed, "ctx", partners(ctx_count, 0))
        c = last = edge_part(block - 1, scalars, 0, mixed, ya, yb, v_mine, v_other, earlier=(summed,))
        c_there = move(c, "head", edge_out)
        if block < blocks - 1:
            now, norms = float_state(block, scalars, total, theirs, state, earlier=(last,))
            kv_now = last = pack_halo(block + 1, scalars, projected, ctx_count - 1, earlier=(norms,))
            halo_next = move(kv_now, "ctx", around)
            out, last = own_part(
                block - 1, scalars, mixed, x, ya, yb, w_out, hidden_in, c_there, so_far, earlier=(last,)
            )
            so_far = (out,)
            state, total = (now,), summed
            mixed, x, ya = mixed_next, x_next, ya_next
    xs = split(scalars, x_next, PARTS, (last,))
    ybs = [move(piece, "head", middle) for piece in xs]
    now, norms = float_state(blocks - 1, scalars, total, theirs, state, earlier=(xs[0],))
    total, last = summed, norms
    for step in range(steps):
        total = last = add(scalars, total, received, earlier=(last,))
        if step + 1 < steps:
            received = move(total, "ctx", partners(ctx_count, step + 1))
        if step == 0:
            c_last = []
            for i in range(PARTS):
                c = last = edge_part(
                    f"{blocks - 1}_{i}", scalars, i, mixed_next, ya_next, ybs[i], v_mine, v_other, earlier=(last,)
                )
                c_last.append(move(c, "head", edge_out))
                if i == 0:
                    out, last = own_part(
                        blocks - 2, scalars, mixed, x, ya, yb, w_out, hidden_in, c_there, so_far, earlier=(last,)
                    )
            acc = last = own_last(
                blocks - 1, scalars, mixed_next, xs, ya_next, ybs, w_out, hidden_in, earlier=(last,)
            )
    theirs = flip(total, 0)
    acc = gate(scalars, acc, earlier=(total,))
    up_final, down_final, token = final_update(scalars, total, theirs, now, norms, earlier=(acc,))
    out = finish(blocks - 1, scalars, acc, c_last, (out,), earlier=(token,))
    return out, up_final, down_final


def solution(mesh):
    in_specs = (
        P(None, "ctx", "head"),
        P(None, None, "ctx", "head"),
        P(None, "head"),
        P(None, "head", None, None),
        P("head", None, None),
        P("head", None, "ctx"),
    )
    out_specs = (P(None, "ctx", "head"), P(None, "head", None, None), P("head", None, None))
    return jax.shard_map(body, mesh=mesh, in_specs=in_specs, out_specs=out_specs, check_vma=False)
```

```python
import functools
import math

import jax
import jax.numpy as jnp
from jax import lax
from jax.experimental import pallas as pl
from jax.experimental.pallas import tpu as pltpu
from jax.sharding import PartitionSpec as P

HD = 128
WIN = 512
TILE = 256
MASKED = -1e30
BF = jnp.bfloat16
F32 = jnp.float32
PARTS = 2
AHEAD = 1
FAST_TILE = 256
EDGES = [(0, 1), (1, 0), (2, 3), (3, 2)]
LIMIT = 36 * 1024 * 1024


def mm(a, b):
    return jnp.dot(a, b, preferred_element_type=F32)


def mm_nt(a, b):
    return lax.dot_general(a, b, (((1,), (1,)), ((), ())), preferred_element_type=F32)


def mm_tn(a, b):
    return lax.dot_general(a, b, (((0,), (0,)), ((), ())), preferred_element_type=F32)


def sigmoid(x):
    return 0.5 + 0.5 * jnp.tanh(0.5 * x)


def whole(array):
    return pl.BlockSpec(memory_space=pltpu.VMEM)


def whole_out(shape):
    return pl.BlockSpec(memory_space=pltpu.VMEM)


def call(
    kernel, name, scalars, inputs, specs, outs, earlier=(), passing=(), scratch=(), grid=(1,), out_specs=None, aliases=None
):
    single = not isinstance(outs, (list, tuple)) and not passing
    outs_list = list(outs) if isinstance(outs, (list, tuple)) else [outs]
    any_spec = pl.BlockSpec(memory_space=pl.ANY)
    first = 1 + len(inputs)
    past = first + len(earlier) + len(passing)

    def ordered(*refs):
        kernel(*refs[:first], *refs[past : past + len(outs_list)], *refs[past + len(outs_list) + len(passing) :])

    pass_at = {first + len(earlier) + i: len(outs_list) + i for i in range(len(passing))}
    got = pl.pallas_call(
        ordered,
        out_shape=[*outs_list, *[like(x) for x in passing]],
        grid_spec=pltpu.PrefetchScalarGridSpec(
            num_scalar_prefetch=1,
            grid=grid,
            in_specs=[*specs, *[any_spec for _ in (*earlier, *passing)]],
            out_specs=[*(out_specs or [whole_out(o.shape) for o in outs_list]), *[any_spec for _ in passing]],
            scratch_shapes=list(scratch),
        ),
        input_output_aliases={**{k + 1: v for k, v in (aliases or {}).items()}, **pass_at},
        compiler_params=pltpu.CompilerParams(vmem_limit_bytes=LIMIT),
        cost_estimate=pl.CostEstimate(flops=20 * 10**9, bytes_accessed=1, transcendentals=0),
        name=name,
    )(scalars, *inputs, *earlier, *passing)
    return got[0] if single else got


def like(array, dtype=None):
    return jax.ShapeDtypeStruct(array.shape, dtype or array.dtype)


def grads_kernel(block, step_scale, sc, k_ref, v_ref, lr_ref, w1_ref, w3_ref, w2_ref, keep_ref, send_ref, acc):
    step = pl.program_id(0)
    k = k_ref[...]
    w_two = w2_ref[...]
    rates = lr_ref[0, block : block + 1, :] * step_scale
    rates = jnp.broadcast_to(rates, (HD, rates.shape[1])).T[:, :1]
    out_grad = (-rates * v_ref[...].astype(F32)).astype(BF)
    gate = mm(k, w1_ref[...])
    up = mm(k, w3_ref[...])
    hidden_grad = mm_nt(out_grad, w_two)
    sig = sigmoid(gate)
    gate_sig = gate * sig
    hidden = (gate_sig * up).astype(BF)
    up_grad = (hidden_grad * gate_sig).astype(BF)
    gate_grad = (hidden_grad * up * sig * (1.0 + gate - gate_sig)).astype(BF)
    parts = (mm_tn(k, gate_grad), mm_tn(k, up_grad), mm_tn(hidden, out_grad))

    @pl.when(step == 0)
    def _():
        for i, part in enumerate(parts):
            acc[i] = part

    @pl.when(step > 0)
    def _():
        for i, part in enumerate(parts):
            acc[i] = acc[i] + part

    @pl.when(step == pl.num_programs(0) - 1)
    def _():
        half = keep_ref.shape[1]
        own = pl.multiple_of(sc[0] * half, half)
        other = pl.multiple_of((1 - sc[0]) * half, half)
        keep_ref[...] = acc[:, pl.ds(own, half), :]
        send_ref[...] = acc[:, pl.ds(other, half), :].astype(BF)


def block_grads(block, scalars, projected, learn_rates, weights, step_scale, weight_specs, earlier=()):
    _, _, rows, feats = projected.shape
    half = feats // 2
    shape = jax.ShapeDtypeStruct((3, half, feats), BF)
    tile = rows
    return call(
        functools.partial(grads_kernel, block, step_scale),
        f"grads_{block}",
        scalars,
        (projected, projected, learn_rates, *weights),
        [
            pl.BlockSpec((None, None, tile, feats), lambda i, s: (1, block, i, 0)),
            pl.BlockSpec((None, None, tile, feats), lambda i, s: (2, block, i, 0)),
            pl.BlockSpec((1, learn_rates.shape[1], tile), lambda i, s: (0, 0, i)),
            *weight_specs,
        ],
        [jax.ShapeDtypeStruct(shape.shape, F32), shape],
        scratch=[pltpu.VMEM((3, feats, feats), F32)],
        grid=(rows // tile,),
        earlier=earlier,
    )


def window_scores(q, keys, usable):
    rows = q.shape[0]
    row_ids = lax.broadcasted_iota(jnp.int32, (rows, rows), 0)
    col_ids = lax.broadcasted_iota(jnp.int32, (rows, rows), 1)
    scores = []
    last = len(keys) - 1
    for i, (key, before) in enumerate(keys):
        s = mm_nt(q, key)
        if before and usable is not None:
            s = s + usable
        if i == 0:
            s = jnp.where(col_ids > row_ids, s, MASKED)
        if i == last:
            s = jnp.where(col_ids <= row_ids, s, MASKED)
        scores.append(s)
    return scores


def weigh(scores, values):
    scale = math.log2(math.e) / math.sqrt(HD)
    peak = jnp.max(functools.reduce(jnp.maximum, scores), axis=-1, keepdims=True) * scale
    result = None
    for s, value in zip(scores, values):
        lifted = jnp.exp2(s * scale - peak).astype(BF)
        part = mm(lifted, jnp.concatenate([value, jnp.ones_like(value)], axis=1))
        result = part if result is None else result + part
    return (result[:, :HD] / result[:, HD:]).astype(BF)


def attend(q_ref, k_ref, v_ref, halo_ref, usable, store):
    rows, feats = q_ref.shape
    tile = min(TILE, rows)

    def pieces(start, cols, which, own_ref):
        for at in range(start - WIN, start + tile, tile):
            before = at < 0
            where = slice(at + WIN, at + WIN + tile) if before else slice(at, at + tile)
            yield (halo_ref[which, where, cols] if before else own_ref[where, cols]), before

    work = [
        (start, slice(head * HD, (head + 1) * HD)) for start in range(0, rows, tile) for head in range(feats // HD)
    ]
    scored = []
    for start, cols in work:
        scored.append(window_scores(q_ref[start : start + tile, cols], list(pieces(start, cols, 0, k_ref)), usable))
        if len(scored) > AHEAD:
            at, there = work[len(scored) - 1 - AHEAD]
            values = [value for value, _ in pieces(at, there, 1, v_ref)]
            store(slice(at, at + tile), there, weigh(scored[len(scored) - 1 - AHEAD], values))
    for (at, there), scores in zip(work[len(work) - AHEAD :], scored[len(work) - AHEAD :]):
        values = [value for value, _ in pieces(at, there, 1, v_ref)]
        store(slice(at, at + tile), there, weigh(scores, values))


def fast_rows(q, w_one, w_three, w_two):
    gate = mm(q, w_one)
    up = mm(q, w_three)
    hidden = (gate * sigmoid(gate) * up).astype(BF)
    result = mm(hidden, w_two)
    return result * lax.rsqrt(jnp.mean(result * result, axis=-1, keepdims=True) + 1e-05)


def usable_bias(block, sc):
    if block > 0:
        return None
    return jnp.where(sc[1] > 0, 0.0, MASKED).astype(F32)


def mixed_kernel(block, sc, q_ref, k_ref, v_ref, halo_ref, w1_ref, w3_ref, w2_ref, out_ref, att):
    def store(rows, cols, value):
        att[rows, cols] = value

    attend(q_ref, k_ref, v_ref, halo_ref, usable_bias(block, sc), store)
    rows = q_ref.shape[0]
    tile = min(TILE, rows)
    for start in range(0, rows, tile):
        at = slice(start, start + tile)
        fast = fast_rows(q_ref[at, :], w1_ref[...], w3_ref[...], w2_ref[...])
        out_ref[at, :] = (att[at, :].astype(F32) + fast).astype(BF)


def attend_kernel(block, sc, q_ref, k_ref, v_ref, halo_ref, out_ref):
    def store(rows, cols, value):
        out_ref[rows, cols] = value

    attend(q_ref, k_ref, v_ref, halo_ref, usable_bias(block, sc), store)


def qkv_specs(block, projected):
    _, _, rows, feats = projected.shape
    return [
        pl.BlockSpec((None, None, rows, feats), functools.partial(lambda kind, i, s: (kind, block, 0, 0), kind))
        for kind in range(3)
    ]


def attention_only(block, scalars, projected, halo, earlier=(), passing=()):
    _, _, rows, feats = projected.shape
    return call(
        functools.partial(attend_kernel, block),
        f"attend_{block}",
        scalars,
        (projected, projected, projected, halo),
        [*qkv_specs(block, projected), whole(halo)],
        jax.ShapeDtypeStruct((rows, feats), BF),
        earlier=earlier,
        passing=passing,
    )


def mixed_first(block, scalars, projected, halo, weights, weight_specs, earlier=()):
    _, _, rows, feats = projected.shape
    return call(
        functools.partial(mixed_kernel, block),
        f"mixed_{block}",
        scalars,
        (projected, projected, projected, halo, *weights),
        [*qkv_specs(block, projected), whole(halo), *weight_specs],
        jax.ShapeDtypeStruct((rows, feats), BF),
        scratch=[pltpu.VMEM((rows, feats), BF)],
        earlier=earlier,
    )


def halves(parity, mine, theirs):
    half = mine.shape[0]
    own = pl.multiple_of(parity * half, half)
    other = pl.multiple_of((1 - parity) * half, half)
    return ((pl.ds(own, half), mine), (pl.ds(other, half), theirs))


def renorm_all(old, mine, theirs, parity, moved, put, known=None):
    ratios = []
    for i in range(3):
        before = None if known is None else known[i, 0:1, 0:1]
        after = None
        for rows, part in halves(parity, mine[i], theirs[i]):
            w = old(i, rows).astype(F32)
            new = w - part.astype(F32)
            moved[i, rows, :] = new
            squares = jnp.sum(new * new, axis=0, keepdims=True)
            after = squares if after is None else after + squares
            if known is None:
                squares = jnp.sum(w * w, axis=0, keepdims=True)
                before = squares if before is None else before + squares
        after = jnp.sum(after, axis=1, keepdims=True)
        if known is None:
            before = jnp.sum(before, axis=1, keepdims=True)
        ratios.append(jnp.sqrt(before) / jnp.sqrt(after + 1e-06))
    for i in range(3):
        half = mine.shape[1]
        for start in (0, half):
            rows = slice(start, start + half)
            put(i, rows, moved[i, rows, :] * ratios[i])


def old_of(refs, i, rows):
    if len(refs) == 1:
        return refs[0][i, rows, :]
    return refs[0][i, 0, rows, :] if i < 2 else refs[1][0, rows, :]


def update_kernel(states, pieces, sc, mine_ref, theirs_ref, *refs):
    *refs, moved = refs
    old, (q_ref, att_ref, mix_ref, new_bf_ref), piece_refs = refs[:states], refs[states : states + 4], refs[states + 4 :]

    def put(i, rows, value):
        new_bf_ref[i, rows, :] = value.astype(BF)

    renorm_all(functools.partial(old_of, old), mine_ref, theirs_ref, sc[0], moved, put)
    rows = q_ref.shape[0]
    tile = min(FAST_TILE, rows)
    for start in range(0, rows, tile):
        at = slice(start, start + tile)
        fast = fast_rows(q_ref[at, :], new_bf_ref[0], new_bf_ref[1], new_bf_ref[2])
        mix_ref[at, :] = (att_ref[at, :].astype(F32) + fast).astype(BF)
    for i, piece_ref in enumerate(piece_refs):
        size = piece_ref.shape[0]
        piece_ref[...] = mix_ref[i * size : (i + 1) * size, :]


def update_and_mix(block, scalars, mine, theirs, state, projected, attended, parts, earlier=()):
    _, _, rows, feats = projected.shape
    pieces = parts if parts > 1 else 0
    got = call(
        functools.partial(update_kernel, len(state), pieces),
        f"update_{block}",
        scalars,
        (mine, theirs, *state, projected, attended),
        [
            whole(mine),
            whole(theirs),
            *[whole(a) for a in state],
            pl.BlockSpec((None, None, rows, feats), lambda i, s: (0, block, 0, 0)),
            whole(attended),
        ],
        [
            jax.ShapeDtypeStruct((rows, feats), BF),
            jax.ShapeDtypeStruct((3, feats, feats), BF),
            *[jax.ShapeDtypeStruct((rows // parts, feats), BF) for _ in range(pieces)],
        ],
        scratch=[pltpu.VMEM((3, *mine.shape[2:] * 2), F32)],
        earlier=earlier,
    )
    return got[0], got[1], got[2:] or [got[0]]


def state_kernel(states, sc, mine_ref, theirs_ref, *refs):
    old, (new_ref, norm_ref, moved) = refs[:states], refs[states:]

    def put(i, rows, value):
        new_ref[i, rows, :] = value

    renorm_all(functools.partial(old_of, old), mine_ref, theirs_ref, sc[0], moved, put)
    for i in range(3):
        norm_ref[i] = jnp.full(norm_ref.shape[1:], jnp.sum(new_ref[i] * new_ref[i]), F32)


def float_state(block, scalars, mine, theirs, state, earlier=()):
    feats = mine.shape[2]
    return call(
        functools.partial(state_kernel, len(state)),
        f"state_{block}",
        scalars,
        (mine, theirs, *state),
        [whole(mine), whole(theirs), *[whole(a) for a in state]],
        [jax.ShapeDtypeStruct((3, feats, feats), F32), jax.ShapeDtypeStruct((3, 8, HD), F32)],
        scratch=[pltpu.VMEM((3, feats, feats), F32)],
        earlier=earlier,
    )


def final_kernel(sc, mine_ref, theirs_ref, old_ref, norm_ref, up_out, down_out, token, moved, done, sems):
    token[...] = jnp.zeros_like(token)
    half = mine_ref.shape[1]
    outs = (up_out.at[0, 0], up_out.at[1, 0], down_out.at[0])
    copies = []

    def put(i, rows, value):
        done[i, rows, :] = value
        part = rows.start // half
        copy = pltpu.make_async_copy(done.at[i, rows, :], outs[i].at[rows, :], sems.at[i, part])
        copy.start()
        copies.append(copy)

    renorm_all(lambda i, rows: old_ref[i, rows, :], mine_ref, theirs_ref, sc[0], moved, put, norm_ref)
    for copy in copies:
        copy.wait()


def final_update(scalars, mine, theirs, state, norms, earlier=()):
    _, half, feats = mine.shape
    any_spec = pl.BlockSpec(memory_space=pl.ANY)
    return call(
        final_kernel,
        "final_update",
        scalars,
        (mine, theirs, state, norms),
        [whole(mine), whole(theirs), whole(state), whole(norms)],
        [
            jax.ShapeDtypeStruct((2, 1, feats, feats), F32),
            jax.ShapeDtypeStruct((1, feats, feats), F32),
            jax.ShapeDtypeStruct((8, HD), F32),
        ],
        out_specs=[any_spec, any_spec, whole_out((8, HD))],
        scratch=[
            pltpu.VMEM((3, feats, feats), F32),
            pltpu.VMEM((3, feats, feats), F32),
            pltpu.SemaphoreType.DMA((3, 2)),
        ],
        earlier=earlier,
    )


def pick_kernel(sc, w_ref, out_ref):
    half = out_ref.shape[1]
    feats = 2 * half
    for i in range(3):
        start = (sc[2] ^ (i + 1)) * feats + sc[0] * half
        out_ref[i] = w_ref[pl.ds(pl.multiple_of(start, half), half), :]


def pick_parts(scalars, w_out, earlier=()):
    feats = w_out.shape[1]
    return call(
        pick_kernel,
        "pick_parts",
        scalars,
        (w_out,),
        [whole(w_out)],
        jax.ShapeDtypeStruct((3, feats // 2, feats), BF),
        earlier=earlier,
    )


def gate_kernel(sc, x_ref, x_out_ref):
    pass


def gate(scalars, x, earlier):
    return call(
        gate_kernel,
        "gate",
        scalars,
        (x,),
        [pl.BlockSpec(memory_space=pl.ANY)],
        like(x),
        out_specs=[pl.BlockSpec(memory_space=pl.ANY)],
        aliases={0: 0},
        earlier=earlier,
    )


def split_kernel(sc, x_ref, *piece_refs):
    size = piece_refs[0].shape[0]
    for i, piece_ref in enumerate(piece_refs):
        piece_ref[...] = x_ref[i * size : (i + 1) * size, :]


def split(scalars, x, parts, earlier):
    rows, feats = x.shape
    piece = jax.ShapeDtypeStruct((rows // parts, feats), BF)
    return call(split_kernel, "split", scalars, (x,), [whole(x)], [piece] * parts, earlier=earlier)


def add_kernel(sc, a_ref, b_ref, out_ref):
    out_ref[...] = (a_ref[...].astype(F32) + b_ref[...].astype(F32)).astype(BF)


def add(scalars, a, b, earlier=(), passing=()):
    return call(add_kernel, "add", scalars, (a, b), [whole(a), whole(b)], like(a, BF), earlier=earlier, passing=passing)


def pack_kernel(sc, k_ref, v_ref, out_ref):
    out_ref[0] = k_ref[...]
    out_ref[1] = v_ref[...]


def pack_halo(block, scalars, projected, last, earlier=()):
    _, _, rows, feats = projected.shape

    def which(s):
        return block if block == 0 else jnp.where(s[1] == last, block - 1, block)

    return call(
        pack_kernel,
        f"pack_{block}",
        scalars,
        (projected, projected),
        [
            pl.BlockSpec((None, None, WIN, feats), lambda i, s: (1, which(s), rows // WIN - 1, 0)),
            pl.BlockSpec((None, None, WIN, feats), lambda i, s: (2, which(s), rows // WIN - 1, 0)),
        ],
        jax.ShapeDtypeStruct((2, WIN, feats), BF),
        earlier=earlier,
    )


def edge_kernel(sc, m_ref, ya_ref, yb_ref, mine_ref, theirs_ref, out_ref):
    half = mine_ref.shape[1]
    total = None
    for part, parity in ((mine_ref, sc[0]), (theirs_ref, 1 - sc[0])):
        cols = pl.ds(pl.multiple_of(parity * half, half), half)
        for i, ref in enumerate((m_ref, ya_ref, yb_ref)):
            term = mm(ref[:, cols], part[i])
            total = term if total is None else total + term
    out_ref[...] = total.astype(BF)


def part_spec(rows, feats, part):
    return pl.BlockSpec((rows, feats), lambda i, s: (part, 0))


def edge_part(name, scalars, part, m, ya, yb, v_mine, v_other, earlier=(), passing=()):
    rows, feats = yb.shape
    return call(
        edge_kernel,
        f"edge_{name}",
        scalars,
        (m, ya, yb, v_mine, v_other),
        [part_spec(rows, feats, part), part_spec(rows, feats, part), whole(yb), whole(v_mine), whole(v_other)],
        jax.ShapeDtypeStruct((rows, feats), BF),
        earlier=earlier,
        passing=passing,
    )


def for_edge(sc, c):
    return jnp.where(sc[3] == 0, c.astype(F32), 0.0)


def own_rows(sc, m, x, ya, yb, w_ref, hid, put, get):
    feats = w_ref.shape[1]
    head = sc[2]

    def weight(which):
        return w_ref[pl.ds(pl.multiple_of(which * feats, feats), feats), :]

    put(hid.astype(F32) + mm(m, weight(head)))

    @pl.when(sc[3] == 1)
    def _():
        put(get() + mm(x[...], weight(head ^ 1)) + mm(ya[...], weight(head ^ 3)) + mm(yb[...], weight(head ^ 2)))


def own_kernel(sc, m_ref, x_ref, ya_ref, yb_ref, w_ref, hid_ref, c_ref, *refs):
    out_ref, token, acc = refs[-3:]
    token[...] = jnp.zeros_like(token)

    def put(value):
        acc[...] = value

    own_rows(sc, m_ref[...], x_ref, ya_ref, yb_ref, w_ref, hid_ref[...], put, lambda: acc[...])
    out_ref[...] = (acc[...] + for_edge(sc, c_ref[...])).astype(BF)


def own_part(block, scalars, m, x, ya, yb, w_out, hidden_in, c, so_far, earlier=()):
    rows, feats = m.shape
    return call(
        own_kernel,
        f"own_{block}",
        scalars,
        (m, x, ya, yb, w_out, hidden_in, c, *so_far),
        [
            *[whole(a) for a in (m, x, ya, yb, w_out)],
            pl.BlockSpec((None, rows, feats), lambda i, s: (block, 0, 0)),
            whole(c),
            *[pl.BlockSpec(memory_space=pl.ANY) for _ in so_far],
        ],
        [like(hidden_in), jax.ShapeDtypeStruct((8, HD), F32)],
        out_specs=[pl.BlockSpec((None, rows, feats), lambda i, s: (block, 0, 0)), whole_out((8, HD))],
        aliases={7: 0} if so_far else None,
        scratch=[pltpu.VMEM((rows, feats), F32)],
        earlier=earlier,
    )


def last_kernel(parts, sc, *refs):
    m_ref, ya_ref = refs[:2]
    xs, ybs = refs[2 : 2 + parts], refs[2 + parts : 2 + 2 * parts]
    w_ref, hid_ref, out_ref = refs[2 + 2 * parts :]
    rows = m_ref.shape[0] // parts
    for i in range(parts):
        at = pl.ds(i * rows, rows)

        def put(value, at=at):
            out_ref[at, :] = value

        own_rows(
            sc, m_ref[at, :], xs[i], ya_ref.at[at, :], ybs[i], w_ref, hid_ref[at, :], put, lambda at=at: out_ref[at, :]
        )


def own_last(block, scalars, m, xs, ya, ybs, w_out, hidden_in, earlier=()):
    rows, feats = m.shape
    return call(
        functools.partial(last_kernel, len(xs)),
        f"own_{block}",
        scalars,
        (m, ya, *xs, *ybs, w_out, hidden_in),
        [
            *[whole(a) for a in (m, ya, *xs, *ybs, w_out)],
            pl.BlockSpec((None, rows, feats), lambda i, s: (block, 0, 0)),
        ],
        jax.ShapeDtypeStruct((rows, feats), F32),
        earlier=earlier,
    )


def finish_kernel(block, parts, sc, acc_ref, *refs):
    out_ref, done, sems = refs[-3:]
    rows = acc_ref.shape[0] // parts
    copies = []
    for i in range(parts):
        at = slice(i * rows, (i + 1) * rows)
        done[at, :] = (acc_ref[at, :] + for_edge(sc, refs[i][...])).astype(BF)
        copies.append(pltpu.make_async_copy(done.at[at, :], out_ref.at[block, at, :], sems.at[i]))
        copies[-1].start()
    for copy in copies:
        copy.wait()


def finish(block, scalars, acc, cs, so_far, earlier=()):
    any_spec = pl.BlockSpec(memory_space=pl.ANY)
    return call(
        functools.partial(finish_kernel, block, len(cs)),
        "finish",
        scalars,
        (acc, *cs, so_far),
        [whole(acc), *[whole(c) for c in cs], any_spec],
        like(so_far),
        out_specs=[any_spec],
        aliases={1 + len(cs): 0},
        scratch=[pltpu.VMEM(acc.shape, BF), pltpu.SemaphoreType.DMA((len(cs),))],
        earlier=earlier,
    )


def move(x, axis, pairs):
    return lax.ppermute(x, axis, pairs)


def between_inner(x):
    count = lax.axis_size("ctx")
    planes = lax.axis_size("head")
    pairs = []
    for i in range(count):
        pairs += [(i * planes + 1, i * planes + 2), (i * planes + 2, i * planes + 1)]
        pairs += [(i * planes + j, (i ^ 1) * planes + j) for j in (0, 3)]
    return move(x, ("ctx", "head"), pairs)


def flip(x, bit):
    count = lax.axis_size("ctx")
    return move(x, "ctx", [(i, i ^ (1 << bit)) for i in range(count)])


def partners(count, step):
    bits = list(range(1, count.bit_length() - 1))
    return [(i, i ^ (1 << (bits if i % 2 == 0 else bits[::-1])[step])) for i in range(count)]


def body(hidden_in, projected, w_out, fast_up, fast_down, learn_rates):
    blocks, rows, feats = hidden_in.shape
    ctx = lax.axis_index("ctx")
    head = lax.axis_index("head")
    ctx_count = lax.axis_size("ctx")
    steps = ctx_count.bit_length() - 2
    parity = ctx % 2
    inner = ((head == 1) | (head == 2)).astype(jnp.int32)
    scalars = jnp.stack([parity, ctx, head, inner]).astype(jnp.int32)
    step_scale = 1.0 / math.sqrt(rows * ctx_count)
    around = [(i, (i + 1) % ctx_count) for i in range(ctx_count)]

    up_spec = [
        pl.BlockSpec((None, None, feats, feats), lambda *_: (0, 0, 0, 0)),
        pl.BlockSpec((None, None, feats, feats), lambda *_: (1, 0, 0, 0)),
        pl.BlockSpec((None, feats, feats), lambda *_: (0, 0, 0)),
    ]
    bf_spec = [
        pl.BlockSpec((None, feats, feats), functools.partial(lambda k, *_: (k, 0, 0), k)) for k in range(3)
    ]

    weights, specs = (fast_up, fast_up, fast_down), up_spec
    state = (fast_up, fast_down)

    kv_now = pack_halo(0, scalars, projected, ctx_count - 1)
    halo = move(kv_now, "ctx", around)
    keep, send = block_grads(0, scalars, projected, learn_rates, weights, step_scale, specs, earlier=(kv_now,))
    keep = gate(scalars, keep, earlier=(send,))
    total = add(scalars, keep, flip(send, 0))
    received = move(total, "ctx", partners(ctx_count, 0))
    kv_now = pack_halo(1, scalars, projected, ctx_count - 1, earlier=(total,))
    halo_next = move(kv_now, "ctx", around)
    mixed = mixed_first(0, scalars, projected, halo, weights, specs, earlier=(kv_now,))
    x = move(mixed, "head", EDGES)
    ya = between_inner(mixed)
    v_send = last = pick_parts(scalars, w_out, earlier=(mixed,))
    v_mine = move(v_send, "head", EDGES)
    so_far = ()
    for block in range(1, blocks):
        for step in range(steps):
            total = last = add(scalars, total, received, earlier=(last,))
            if step + 1 < steps:
                received = move(total, "ctx", partners(ctx_count, step + 1))
            if step == 0:
                attended = last = attention_only(block, scalars, projected, halo_next, earlier=(last,))
                x = last = gate(scalars, x, earlier=(last,))
                yb = between_inner(x)
        theirs = flip(total, 0)
        ya = last = gate(scalars, ya, earlier=(total,))
        mixed_next, new_bf = update_and_mix(
            block, scalars, total, theirs, state, projected, attended, 1, earlier=(last,)
        )[:2]
        x_next = move(mixed_next, "head", EDGES)
        ya_next = between_inner(mixed_next)
        weights, specs = (new_bf, new_bf, new_bf), bf_spec
        keep, send = block_grads(
            block, scalars, projected, learn_rates, weights, step_scale, specs, earlier=(mixed_next,)
        )
        if block == 1:
            v_mine = last = gate(scalars, v_mine, earlier=(send,))
            v_other = flip(v_mine, 0)
        else:
            keep = last = gate(scalars, keep, earlier=(send,))
        summed = add(scalars, keep, flip(send, 0), earlier=(last,))
        received = move(summed, "ctx", partners(ctx_count, 0))
        c = last = edge_part(block - 1, scalars, 0, mixed, ya, yb, v_mine, v_other, earlier=(summed,))
        c_there = move(c, "head", EDGES)
        if block < blocks - 1:
            now, norms = float_state(block, scalars, total, theirs, state, earlier=(last,))
            kv_now = last = pack_halo(block + 1, scalars, projected, ctx_count - 1, earlier=(norms,))
            halo_next = move(kv_now, "ctx", around)
            out, last = own_part(
                block - 1, scalars, mixed, x, ya, yb, w_out, hidden_in, c_there, so_far, earlier=(last,)
            )
            so_far = (out,)
            state, total = (now,), summed
            mixed, x, ya = mixed_next, x_next, ya_next
    now, norms = float_state(blocks - 1, scalars, total, theirs, state, earlier=(last,))
    xs = split(scalars, x_next, PARTS, (norms,))
    ybs = [between_inner(piece) for piece in xs]
    total, last = summed, xs[0]
    for step in range(steps):
        total = last = add(scalars, total, received, earlier=(last,))
        if step + 1 < steps:
            received = move(total, "ctx", partners(ctx_count, step + 1))
        if step == 0:
            c_last = []
            for i in range(PARTS):
                c = last = edge_part(
                    f"{blocks - 1}_{i}", scalars, i, mixed_next, ya_next, ybs[i], v_mine, v_other, earlier=(last,)
                )
                c_last.append(move(c, "head", EDGES))
            out, last = own_part(
                blocks - 2, scalars, mixed, x, ya, yb, w_out, hidden_in, c_there, so_far, earlier=(last,)
            )
    theirs = flip(total, 0)
    acc = own_last(blocks - 1, scalars, mixed_next, xs, ya_next, ybs, w_out, hidden_in, earlier=(total,))
    up_final, down_final, token = final_update(scalars, total, theirs, now, norms, earlier=(acc,))
    out = finish(blocks - 1, scalars, acc, c_last, out, earlier=(token,))
    return out, up_final, down_final


def solution(mesh):
    in_specs = (
        P(None, "ctx", "head"),
        P(None, None, "ctx", "head"),
        P(None, "head"),
        P(None, "head", None, None),
        P("head", None, None),
        P("head", None, "ctx"),
    )
    out_specs = (P(None, "ctx", "head"), P(None, "head", None, None), P("head", None, None))
    return jax.shard_map(body, mesh=mesh, in_specs=in_specs, out_specs=out_specs, check_vma=False)
```

```python
import functools
import math

import jax
import jax.numpy as jnp
from jax import lax
from jax.experimental import pallas as pl
from jax.experimental.pallas import tpu as pltpu
from jax.sharding import PartitionSpec as P

HD = 128
WIN = 512
TILE = 256
MASKED = -1e30
BF = jnp.bfloat16
F32 = jnp.float32
PARTS = 2
AHEAD = 1
FAST_TILE = 256
EDGES = [(0, 1), (1, 0), (2, 3), (3, 2)]
LIMIT = 36 * 1024 * 1024


def mm(a, b):
    return jnp.dot(a, b, preferred_element_type=F32)


def mm_nt(a, b):
    return lax.dot_general(a, b, (((1,), (1,)), ((), ())), preferred_element_type=F32)


def mm_tn(a, b):
    return lax.dot_general(a, b, (((0,), (0,)), ((), ())), preferred_element_type=F32)


def sigmoid(x):
    return 0.5 + 0.5 * jnp.tanh(0.5 * x)


def whole(array):
    return pl.BlockSpec(memory_space=pltpu.VMEM)


def whole_out(shape):
    return pl.BlockSpec(memory_space=pltpu.VMEM)


def call(
    kernel, name, scalars, inputs, specs, outs, earlier=(), passing=(), scratch=(), grid=(1,), out_specs=None, aliases=None
):
    single = not isinstance(outs, (list, tuple)) and not passing
    outs_list = list(outs) if isinstance(outs, (list, tuple)) else [outs]
    any_spec = pl.BlockSpec(memory_space=pl.ANY)
    first = 1 + len(inputs)
    past = first + len(earlier) + len(passing)

    def ordered(*refs):
        kernel(*refs[:first], *refs[past : past + len(outs_list)], *refs[past + len(outs_list) + len(passing) :])

    pass_at = {first + len(earlier) + i: len(outs_list) + i for i in range(len(passing))}
    got = pl.pallas_call(
        ordered,
        out_shape=[*outs_list, *[like(x) for x in passing]],
        grid_spec=pltpu.PrefetchScalarGridSpec(
            num_scalar_prefetch=1,
            grid=grid,
            in_specs=[*specs, *[any_spec for _ in (*earlier, *passing)]],
            out_specs=[*(out_specs or [whole_out(o.shape) for o in outs_list]), *[any_spec for _ in passing]],
            scratch_shapes=list(scratch),
        ),
        input_output_aliases={**{k + 1: v for k, v in (aliases or {}).items()}, **pass_at},
        compiler_params=pltpu.CompilerParams(vmem_limit_bytes=LIMIT),
        cost_estimate=pl.CostEstimate(flops=20 * 10**9, bytes_accessed=1, transcendentals=0),
        name=name,
    )(scalars, *inputs, *earlier, *passing)
    return got[0] if single else got


def like(array, dtype=None):
    return jax.ShapeDtypeStruct(array.shape, dtype or array.dtype)


def grads_kernel(block, step_scale, sc, k_ref, v_ref, lr_ref, w1_ref, w3_ref, w2_ref, keep_ref, send_ref, acc):
    step = pl.program_id(0)
    k = k_ref[...]
    w_two = w2_ref[...]
    rates = lr_ref[0, block : block + 1, :] * step_scale
    rates = jnp.broadcast_to(rates, (HD, rates.shape[1])).T[:, :1]
    out_grad = (-rates * v_ref[...].astype(F32)).astype(BF)
    gate = mm(k, w1_ref[...])
    up = mm(k, w3_ref[...])
    hidden_grad = mm_nt(out_grad, w_two)
    sig = sigmoid(gate)
    gate_sig = gate * sig
    hidden = (gate_sig * up).astype(BF)
    up_grad = (hidden_grad * gate_sig).astype(BF)
    gate_grad = (hidden_grad * up * sig * (1.0 + gate - gate_sig)).astype(BF)
    parts = (mm_tn(k, gate_grad), mm_tn(k, up_grad), mm_tn(hidden, out_grad))

    @pl.when(step == 0)
    def _():
        for i, part in enumerate(parts):
            acc[i] = part

    @pl.when(step > 0)
    def _():
        for i, part in enumerate(parts):
            acc[i] = acc[i] + part

    @pl.when(step == pl.num_programs(0) - 1)
    def _():
        half = keep_ref.shape[1]
        own = pl.multiple_of(sc[0] * half, half)
        other = pl.multiple_of((1 - sc[0]) * half, half)
        keep_ref[...] = acc[:, pl.ds(own, half), :]
        send_ref[...] = acc[:, pl.ds(other, half), :].astype(BF)


def block_grads(block, scalars, projected, learn_rates, weights, step_scale, weight_specs, earlier=(), own=None):
    _, _, rows, feats = projected.shape
    half = feats // 2
    shape = jax.ShapeDtypeStruct((3, half, feats), BF)
    tile = rows
    return call(
        functools.partial(grads_kernel, block, step_scale),
        f"grads_{block}",
        scalars,
        (*(own or (projected, projected)), learn_rates, *weights),
        [
            *(
                [whole(x) for x in own]
                if own
                else [
                    pl.BlockSpec((None, None, tile, feats), lambda i, s: (1, block, i, 0)),
                    pl.BlockSpec((None, None, tile, feats), lambda i, s: (2, block, i, 0)),
                ]
            ),
            pl.BlockSpec((1, learn_rates.shape[1], tile), lambda i, s: (0, 0, i)),
            *weight_specs,
        ],
        [jax.ShapeDtypeStruct(shape.shape, F32), shape],
        scratch=[pltpu.VMEM((3, feats, feats), F32)],
        grid=(rows // tile,),
        earlier=earlier,
    )


def window_scores(q, keys, usable):
    rows = q.shape[0]
    row_ids = lax.broadcasted_iota(jnp.int32, (rows, rows), 0)
    col_ids = lax.broadcasted_iota(jnp.int32, (rows, rows), 1)
    scores = []
    last = len(keys) - 1
    for i, (key, before) in enumerate(keys):
        s = mm_nt(q, key)
        if before and usable is not None:
            s = s + usable
        if i == 0:
            s = jnp.where(col_ids > row_ids, s, MASKED)
        if i == last:
            s = jnp.where(col_ids <= row_ids, s, MASKED)
        scores.append(s)
    return scores


def weigh(scores, values):
    scale = math.log2(math.e) / math.sqrt(HD)
    peak = jnp.max(functools.reduce(jnp.maximum, scores), axis=-1, keepdims=True) * scale
    result = None
    for s, value in zip(scores, values):
        lifted = jnp.exp2(s * scale - peak).astype(BF)
        part = mm(lifted, jnp.concatenate([value, jnp.ones_like(value)], axis=1))
        result = part if result is None else result + part
    return (result[:, :HD] / result[:, HD:]).astype(BF)


def attend(q_ref, k_ref, v_ref, halo, usable, store):
    rows, feats = q_ref.shape
    tile = min(TILE, rows)

    def pieces(start, cols, which, own_ref):
        for at in range(start - WIN, start + tile, tile):
            before = at < 0
            where = slice(at + WIN, at + WIN + tile) if before else slice(at, at + tile)
            yield (halo[which][where, cols] if before else own_ref[where, cols]), before

    work = [
        (start, slice(head * HD, (head + 1) * HD)) for start in range(0, rows, tile) for head in range(feats // HD)
    ]
    scored = []
    for start, cols in work:
        scored.append(window_scores(q_ref[start : start + tile, cols], list(pieces(start, cols, 0, k_ref)), usable))
        if len(scored) > AHEAD:
            at, there = work[len(scored) - 1 - AHEAD]
            values = [value for value, _ in pieces(at, there, 1, v_ref)]
            store(slice(at, at + tile), there, weigh(scored[len(scored) - 1 - AHEAD], values))
    for (at, there), scores in zip(work[len(work) - AHEAD :], scored[len(work) - AHEAD :]):
        values = [value for value, _ in pieces(at, there, 1, v_ref)]
        store(slice(at, at + tile), there, weigh(scores, values))


def fast_rows(q, w_one, w_three, w_two):
    gate = mm(q, w_one)
    up = mm(q, w_three)
    hidden = (gate * sigmoid(gate) * up).astype(BF)
    result = mm(hidden, w_two)
    return result * lax.rsqrt(jnp.mean(result * result, axis=-1, keepdims=True) + 1e-05)


def usable_bias(block, sc):
    if block > 0:
        return None
    return jnp.where(sc[1] > 0, 0.0, MASKED).astype(F32)


def mixed_kernel(block, sc, q_ref, k_ref, v_ref, k_halo, v_halo, w1_ref, w3_ref, w2_ref, out_ref, att):
    def store(rows, cols, value):
        att[rows, cols] = value

    attend(q_ref, k_ref, v_ref, (k_halo, v_halo), usable_bias(block, sc), store)
    rows = q_ref.shape[0]
    tile = min(TILE, rows)
    for start in range(0, rows, tile):
        at = slice(start, start + tile)
        fast = fast_rows(q_ref[at, :], w1_ref[...], w3_ref[...], w2_ref[...])
        out_ref[at, :] = (att[at, :].astype(F32) + fast).astype(BF)


def attend_kernel(block, sc, q_ref, k_ref, v_ref, halo_ref, out_ref):
    def store(rows, cols, value):
        out_ref[rows, cols] = value

    attend(q_ref, k_ref, v_ref, (halo_ref.at[0], halo_ref.at[1]), usable_bias(block, sc), store)


def qkv_specs(block, projected):
    _, _, rows, feats = projected.shape
    return [
        pl.BlockSpec((None, None, rows, feats), functools.partial(lambda kind, i, s: (kind, block, 0, 0), kind))
        for kind in range(3)
    ]


def attention_only(block, scalars, projected, halo, earlier=(), passing=()):
    _, _, rows, feats = projected.shape
    return call(
        functools.partial(attend_kernel, block),
        f"attend_{block}",
        scalars,
        (projected, projected, projected, halo),
        [*qkv_specs(block, projected), whole(halo)],
        jax.ShapeDtypeStruct((rows, feats), BF),
        earlier=earlier,
        passing=passing,
    )


def mixed_first(block, scalars, projected, halo, weights, weight_specs, earlier=()):
    _, _, rows, feats = projected.shape
    return call(
        functools.partial(mixed_kernel, block),
        f"mixed_{block}",
        scalars,
        (projected, projected, projected, *halo, *weights),
        [*qkv_specs(block, projected), *[whole(x) for x in halo], *weight_specs],
        jax.ShapeDtypeStruct((rows, feats), BF),
        scratch=[pltpu.VMEM((rows, feats), BF)],
        earlier=earlier,
    )


def halves(parity, mine, theirs):
    half = mine.shape[0]
    own = pl.multiple_of(parity * half, half)
    other = pl.multiple_of((1 - parity) * half, half)
    return ((pl.ds(own, half), mine), (pl.ds(other, half), theirs))


def renorm_all(old, mine, theirs, parity, moved, put, known=None):
    ratios = []
    for i in range(3):
        before = None if known is None else known[i, 0:1, 0:1]
        after = None
        for rows, part in halves(parity, mine[i], theirs[i]):
            w = old(i, rows).astype(F32)
            new = w - part.astype(F32)
            moved[i, rows, :] = new
            squares = jnp.sum(new * new, axis=0, keepdims=True)
            after = squares if after is None else after + squares
            if known is None:
                squares = jnp.sum(w * w, axis=0, keepdims=True)
                before = squares if before is None else before + squares
        after = jnp.sum(after, axis=1, keepdims=True)
        if known is None:
            before = jnp.sum(before, axis=1, keepdims=True)
        ratios.append(jnp.sqrt(before) / jnp.sqrt(after + 1e-06))
    for i in range(3):
        half = mine.shape[1]
        for start in (0, half):
            rows = slice(start, start + half)
            put(i, rows, moved[i, rows, :] * ratios[i])


def old_of(refs, i, rows):
    if len(refs) == 1:
        return refs[0][i, rows, :]
    return refs[0][i, 0, rows, :] if i < 2 else refs[1][0, rows, :]


def update_kernel(states, pieces, sc, mine_ref, theirs_ref, *refs):
    *refs, moved = refs
    old, (q_ref, att_ref, mix_ref, new_bf_ref), piece_refs = refs[:states], refs[states : states + 4], refs[states + 4 :]

    def put(i, rows, value):
        new_bf_ref[i, rows, :] = value.astype(BF)

    renorm_all(functools.partial(old_of, old), mine_ref, theirs_ref, sc[0], moved, put)
    rows = q_ref.shape[0]
    tile = min(FAST_TILE, rows)
    for start in range(0, rows, tile):
        at = slice(start, start + tile)
        fast = fast_rows(q_ref[at, :], new_bf_ref[0], new_bf_ref[1], new_bf_ref[2])
        mix_ref[at, :] = (att_ref[at, :].astype(F32) + fast).astype(BF)
    for i, piece_ref in enumerate(piece_refs):
        size = piece_ref.shape[0]
        piece_ref[...] = mix_ref[i * size : (i + 1) * size, :]


def update_and_mix(block, scalars, mine, theirs, state, projected, attended, parts, earlier=()):
    _, _, rows, feats = projected.shape
    pieces = parts if parts > 1 else 0
    got = call(
        functools.partial(update_kernel, len(state), pieces),
        f"update_{block}",
        scalars,
        (mine, theirs, *state, projected, attended),
        [
            whole(mine),
            whole(theirs),
            *[whole(a) for a in state],
            pl.BlockSpec((None, None, rows, feats), lambda i, s: (0, block, 0, 0)),
            whole(attended),
        ],
        [
            jax.ShapeDtypeStruct((rows, feats), BF),
            jax.ShapeDtypeStruct((3, feats, feats), BF),
            *[jax.ShapeDtypeStruct((rows // parts, feats), BF) for _ in range(pieces)],
        ],
        scratch=[pltpu.VMEM((3, *mine.shape[2:] * 2), F32)],
        earlier=earlier,
    )
    return got[0], got[1], got[2:] or [got[0]]


def state_kernel(states, sc, mine_ref, theirs_ref, *refs):
    old, (new_ref, norm_ref, moved) = refs[:states], refs[states:]

    def put(i, rows, value):
        new_ref[i, rows, :] = value

    renorm_all(functools.partial(old_of, old), mine_ref, theirs_ref, sc[0], moved, put)
    for i in range(3):
        norm_ref[i] = jnp.full(norm_ref.shape[1:], jnp.sum(new_ref[i] * new_ref[i]), F32)


def float_state(block, scalars, mine, theirs, state, earlier=()):
    feats = mine.shape[2]
    return call(
        functools.partial(state_kernel, len(state)),
        f"state_{block}",
        scalars,
        (mine, theirs, *state),
        [whole(mine), whole(theirs), *[whole(a) for a in state]],
        [jax.ShapeDtypeStruct((3, feats, feats), F32), jax.ShapeDtypeStruct((3, 8, HD), F32)],
        scratch=[pltpu.VMEM((3, feats, feats), F32)],
        earlier=earlier,
    )


def final_kernel(sc, mine_ref, theirs_ref, old_ref, norm_ref, up_out, down_out, token, moved, done, sems):
    token[...] = jnp.zeros_like(token)
    half = mine_ref.shape[1]
    outs = (up_out.at[0, 0], up_out.at[1, 0], down_out.at[0])
    copies = []

    def put(i, rows, value):
        done[i, rows, :] = value
        part = rows.start // half
        copy = pltpu.make_async_copy(done.at[i, rows, :], outs[i].at[rows, :], sems.at[i, part])
        copy.start()
        copies.append(copy)

    renorm_all(lambda i, rows: old_ref[i, rows, :], mine_ref, theirs_ref, sc[0], moved, put, norm_ref)
    for copy in copies:
        copy.wait()


def final_update(scalars, mine, theirs, state, norms, earlier=()):
    _, half, feats = mine.shape
    any_spec = pl.BlockSpec(memory_space=pl.ANY)
    return call(
        final_kernel,
        "final_update",
        scalars,
        (mine, theirs, state, norms),
        [whole(mine), whole(theirs), whole(state), whole(norms)],
        [
            jax.ShapeDtypeStruct((2, 1, feats, feats), F32),
            jax.ShapeDtypeStruct((1, feats, feats), F32),
            jax.ShapeDtypeStruct((8, HD), F32),
        ],
        out_specs=[any_spec, any_spec, whole_out((8, HD))],
        scratch=[
            pltpu.VMEM((3, feats, feats), F32),
            pltpu.VMEM((3, feats, feats), F32),
            pltpu.SemaphoreType.DMA((3, 2)),
        ],
        earlier=earlier,
    )


def pick_kernel(sc, w_ref, out_ref):
    half = out_ref.shape[1]
    feats = 2 * half
    for i in range(3):
        start = (sc[2] ^ (i + 1)) * feats + sc[0] * half
        out_ref[i] = w_ref[pl.ds(pl.multiple_of(start, half), half), :]


def pick_parts(scalars, w_out, earlier=()):
    feats = w_out.shape[1]
    return call(
        pick_kernel,
        "pick_parts",
        scalars,
        (w_out,),
        [whole(w_out)],
        jax.ShapeDtypeStruct((3, feats // 2, feats), BF),
        earlier=earlier,
    )


def gate_kernel(sc, x_ref, x_out_ref):
    pass


def gate(scalars, x, earlier):
    return call(
        gate_kernel,
        "gate",
        scalars,
        (x,),
        [pl.BlockSpec(memory_space=pl.ANY)],
        like(x),
        out_specs=[pl.BlockSpec(memory_space=pl.ANY)],
        aliases={0: 0},
        earlier=earlier,
    )


def split_kernel(sc, x_ref, *piece_refs):
    size = piece_refs[0].shape[0]
    for i, piece_ref in enumerate(piece_refs):
        piece_ref[...] = x_ref[i * size : (i + 1) * size, :]


def split(scalars, x, parts, earlier):
    rows, feats = x.shape
    piece = jax.ShapeDtypeStruct((rows // parts, feats), BF)
    return call(split_kernel, "split", scalars, (x,), [whole(x)], [piece] * parts, earlier=earlier)


def add_kernel(sc, a_ref, b_ref, out_ref):
    out_ref[...] = (a_ref[...].astype(F32) + b_ref[...].astype(F32)).astype(BF)


def add(scalars, a, b, earlier=(), passing=()):
    return call(add_kernel, "add", scalars, (a, b), [whole(a), whole(b)], like(a, BF), earlier=earlier, passing=passing)


def pack_kernel(sc, k_ref, v_ref, out_ref):
    out_ref[0] = k_ref[...]
    out_ref[1] = v_ref[...]


def first_rows(projected, kind):
    _, _, rows, feats = projected.shape
    return lax.slice(projected, (kind, 0, 0, 0), (kind + 1, 1, rows, feats)).reshape(rows, feats)


def pack_halo(block, scalars, projected, last, earlier=()):
    _, _, rows, feats = projected.shape

    def which(s):
        return block if block == 0 else jnp.where(s[1] == last, block - 1, block)

    return call(
        pack_kernel,
        f"pack_{block}",
        scalars,
        (projected, projected),
        [
            pl.BlockSpec((None, None, WIN, feats), lambda i, s: (1, which(s), rows // WIN - 1, 0)),
            pl.BlockSpec((None, None, WIN, feats), lambda i, s: (2, which(s), rows // WIN - 1, 0)),
        ],
        jax.ShapeDtypeStruct((2, WIN, feats), BF),
        earlier=earlier,
    )


def edge_kernel(sc, m_ref, ya_ref, yb_ref, mine_ref, theirs_ref, out_ref):
    half = mine_ref.shape[1]
    total = None
    for part, parity in ((mine_ref, sc[0]), (theirs_ref, 1 - sc[0])):
        cols = pl.ds(pl.multiple_of(parity * half, half), half)
        for i, ref in enumerate((m_ref, ya_ref, yb_ref)):
            term = mm(ref[:, cols], part[i])
            total = term if total is None else total + term
    out_ref[...] = total.astype(BF)


def part_spec(rows, feats, part):
    return pl.BlockSpec((rows, feats), lambda i, s: (part, 0))


def edge_part(name, scalars, part, m, ya, yb, v_mine, v_other, earlier=(), passing=()):
    rows, feats = yb.shape
    return call(
        edge_kernel,
        f"edge_{name}",
        scalars,
        (m, ya, yb, v_mine, v_other),
        [part_spec(rows, feats, part), part_spec(rows, feats, part), whole(yb), whole(v_mine), whole(v_other)],
        jax.ShapeDtypeStruct((rows, feats), BF),
        earlier=earlier,
        passing=passing,
    )


def for_edge(sc, c):
    return jnp.where(sc[3] == 0, c.astype(F32), 0.0)


def own_rows(sc, m, x, ya, yb, w_ref, hid, put, get):
    feats = w_ref.shape[1]
    head = sc[2]

    def weight(which):
        return w_ref[pl.ds(pl.multiple_of(which * feats, feats), feats), :]

    put(hid.astype(F32) + mm(m, weight(head)))

    @pl.when(sc[3] == 1)
    def _():
        put(get() + mm(x[...], weight(head ^ 1)) + mm(ya[...], weight(head ^ 3)) + mm(yb[...], weight(head ^ 2)))


def own_kernel(sc, m_ref, x_ref, ya_ref, yb_ref, w_ref, hid_ref, c_ref, *refs):
    out_ref, token, acc = refs[-3:]
    token[...] = jnp.zeros_like(token)

    def put(value):
        acc[...] = value

    own_rows(sc, m_ref[...], x_ref, ya_ref, yb_ref, w_ref, hid_ref[...], put, lambda: acc[...])
    out_ref[...] = (acc[...] + for_edge(sc, c_ref[...])).astype(BF)


def own_part(block, scalars, m, x, ya, yb, w_out, hidden_in, c, so_far, earlier=()):
    rows, feats = m.shape
    return call(
        own_kernel,
        f"own_{block}",
        scalars,
        (m, x, ya, yb, w_out, hidden_in, c, *so_far),
        [
            *[whole(a) for a in (m, x, ya, yb, w_out)],
            pl.BlockSpec((None, rows, feats), lambda i, s: (block, 0, 0)),
            whole(c),
            *[pl.BlockSpec(memory_space=pl.ANY) for _ in so_far],
        ],
        [like(hidden_in), jax.ShapeDtypeStruct((8, HD), F32)],
        out_specs=[pl.BlockSpec((None, rows, feats), lambda i, s: (block, 0, 0)), whole_out((8, HD))],
        aliases={7: 0} if so_far else None,
        scratch=[pltpu.VMEM((rows, feats), F32)],
        earlier=earlier,
    )


def last_kernel(parts, sc, *refs):
    m_ref, ya_ref = refs[:2]
    xs, ybs = refs[2 : 2 + parts], refs[2 + parts : 2 + 2 * parts]
    w_ref, hid_ref, out_ref = refs[2 + 2 * parts :]
    rows = m_ref.shape[0] // parts
    for i in range(parts):
        at = pl.ds(i * rows, rows)

        def put(value, at=at):
            out_ref[at, :] = value

        own_rows(
            sc, m_ref[at, :], xs[i], ya_ref.at[at, :], ybs[i], w_ref, hid_ref[at, :], put, lambda at=at: out_ref[at, :]
        )


def own_last(block, scalars, m, xs, ya, ybs, w_out, hidden_in, earlier=()):
    rows, feats = m.shape
    return call(
        functools.partial(last_kernel, len(xs)),
        f"own_{block}",
        scalars,
        (m, ya, *xs, *ybs, w_out, hidden_in),
        [
            *[whole(a) for a in (m, ya, *xs, *ybs, w_out)],
            pl.BlockSpec((None, rows, feats), lambda i, s: (block, 0, 0)),
        ],
        jax.ShapeDtypeStruct((rows, feats), F32),
        earlier=earlier,
    )


def finish_kernel(block, parts, sc, acc_ref, *refs):
    out_ref, done, sems = refs[-3:]
    rows = acc_ref.shape[0] // parts
    copies = []
    for i in range(parts):
        at = slice(i * rows, (i + 1) * rows)
        done[at, :] = (acc_ref[at, :] + for_edge(sc, refs[i][...])).astype(BF)
        copies.append(pltpu.make_async_copy(done.at[at, :], out_ref.at[block, at, :], sems.at[i]))
        copies[-1].start()
    for copy in copies:
        copy.wait()


def finish(block, scalars, acc, cs, so_far, earlier=()):
    any_spec = pl.BlockSpec(memory_space=pl.ANY)
    return call(
        functools.partial(finish_kernel, block, len(cs)),
        "finish",
        scalars,
        (acc, *cs, so_far),
        [whole(acc), *[whole(c) for c in cs], any_spec],
        like(so_far),
        out_specs=[any_spec],
        aliases={1 + len(cs): 0},
        scratch=[pltpu.VMEM(acc.shape, BF), pltpu.SemaphoreType.DMA((len(cs),))],
        earlier=earlier,
    )


def move(x, axis, pairs):
    return lax.ppermute(x, axis, pairs)


def between_inner(x):
    count = lax.axis_size("ctx")
    planes = lax.axis_size("head")
    pairs = []
    for i in range(count):
        pairs += [(i * planes + 1, i * planes + 2), (i * planes + 2, i * planes + 1)]
        pairs += [(i * planes + j, (i ^ 1) * planes + j) for j in (0, 3)]
    return move(x, ("ctx", "head"), pairs)


def flip(x, bit):
    count = lax.axis_size("ctx")
    return move(x, "ctx", [(i, i ^ (1 << bit)) for i in range(count)])


def partners(count, step):
    bits = list(range(1, count.bit_length() - 1))
    return [(i, i ^ (1 << (bits if i % 2 == 0 else bits[::-1])[step])) for i in range(count)]


def body(hidden_in, projected, w_out, fast_up, fast_down, learn_rates):
    blocks, rows, feats = hidden_in.shape
    ctx = lax.axis_index("ctx")
    head = lax.axis_index("head")
    ctx_count = lax.axis_size("ctx")
    steps = ctx_count.bit_length() - 2
    parity = ctx % 2
    inner = ((head == 1) | (head == 2)).astype(jnp.int32)
    scalars = jnp.stack([parity, ctx, head, inner]).astype(jnp.int32)
    step_scale = 1.0 / math.sqrt(rows * ctx_count)
    around = [(i, (i + 1) % ctx_count) for i in range(ctx_count)]

    up_spec = [
        pl.BlockSpec((None, None, feats, feats), lambda *_: (0, 0, 0, 0)),
        pl.BlockSpec((None, None, feats, feats), lambda *_: (1, 0, 0, 0)),
        pl.BlockSpec((None, feats, feats), lambda *_: (0, 0, 0)),
    ]
    bf_spec = [
        pl.BlockSpec((None, feats, feats), functools.partial(lambda k, *_: (k, 0, 0), k)) for k in range(3)
    ]

    weights, specs = (fast_up, fast_up, fast_down), up_spec
    state = (fast_up, fast_down)

    kv_now = [first_rows(projected, kind) for kind in (1, 2)]
    halo = [move(x[rows - WIN :], "ctx", around) for x in kv_now]
    keep, send = block_grads(0, scalars, projected, learn_rates, weights, step_scale, specs, own=kv_now)
    keep = gate(scalars, keep, earlier=(send,))
    total = add(scalars, keep, flip(send, 0))
    received = move(total, "ctx", partners(ctx_count, 0))
    kv_now = pack_halo(1, scalars, projected, ctx_count - 1, earlier=(total,))
    halo_next = move(kv_now, "ctx", around)
    mixed = mixed_first(0, scalars, projected, halo, weights, specs, earlier=(kv_now,))
    x = move(mixed, "head", EDGES)
    ya = between_inner(mixed)
    v_send = last = pick_parts(scalars, w_out, earlier=(mixed,))
    v_mine = move(v_send, "head", EDGES)
    so_far = ()
    for block in range(1, blocks):
        for step in range(steps):
            total = last = add(scalars, total, received, earlier=(last,))
            if step + 1 < steps:
                received = move(total, "ctx", partners(ctx_count, step + 1))
            if step == 0:
                attended = last = attention_only(block, scalars, projected, halo_next, earlier=(last,))
                x = last = gate(scalars, x, earlier=(last,))
                yb = between_inner(x)
        theirs = flip(total, 0)
        ya = last = gate(scalars, ya, earlier=(total,))
        mixed_next, new_bf = update_and_mix(
            block, scalars, total, theirs, state, projected, attended, 1, earlier=(last,)
        )[:2]
        x_next = move(mixed_next, "head", EDGES)
        ya_next = between_inner(mixed_next)
        weights, specs = (new_bf, new_bf, new_bf), bf_spec
        keep, send = block_grads(
            block, scalars, projected, learn_rates, weights, step_scale, specs, earlier=(mixed_next,)
        )
        if block == 1:
            v_mine = last = gate(scalars, v_mine, earlier=(send,))
            v_other = flip(v_mine, 0)
        else:
            keep = last = gate(scalars, keep, earlier=(send,))
        summed = add(scalars, keep, flip(send, 0), earlier=(last,))
        received = move(summed, "ctx", partners(ctx_count, 0))
        c = last = edge_part(block - 1, scalars, 0, mixed, ya, yb, v_mine, v_other, earlier=(summed,))
        c_there = move(c, "head", EDGES)
        if block < blocks - 1:
            now, norms = float_state(block, scalars, total, theirs, state, earlier=(last,))
            kv_now = last = pack_halo(block + 1, scalars, projected, ctx_count - 1, earlier=(norms,))
            halo_next = move(kv_now, "ctx", around)
            out, last = own_part(
                block - 1, scalars, mixed, x, ya, yb, w_out, hidden_in, c_there, so_far, earlier=(last,)
            )
            so_far = (out,)
            state, total = (now,), summed
            mixed, x, ya = mixed_next, x_next, ya_next
    now, norms = float_state(blocks - 1, scalars, total, theirs, state, earlier=(last,))
    xs = split(scalars, x_next, PARTS, (norms,))
    ybs = [between_inner(piece) for piece in xs]
    total, last = summed, xs[0]
    for step in range(steps):
        total = last = add(scalars, total, received, earlier=(last,))
        if step + 1 < steps:
            received = move(total, "ctx", partners(ctx_count, step + 1))
        if step == 0:
            c_last = []
            for i in range(PARTS):
                c = last = edge_part(
                    f"{blocks - 1}_{i}", scalars, i, mixed_next, ya_next, ybs[i], v_mine, v_other, earlier=(last,)
                )
                c_last.append(move(c, "head", EDGES))
            out, last = own_part(
                blocks - 2, scalars, mixed, x, ya, yb, w_out, hidden_in, c_there, so_far, earlier=(last,)
            )
    theirs = flip(total, 0)
    acc = own_last(blocks - 1, scalars, mixed_next, xs, ya_next, ybs, w_out, hidden_in, earlier=(total,))
    up_final, down_final, token = final_update(scalars, total, theirs, now, norms, earlier=(acc,))
    out = finish(blocks - 1, scalars, acc, c_last, out, earlier=(token,))
    return out, up_final, down_final


def solution(mesh):
    in_specs = (
        P(None, "ctx", "head"),
        P(None, None, "ctx", "head"),
        P(None, "head"),
        P(None, "head", None, None),
        P("head", None, None),
        P("head", None, "ctx"),
    )
    out_specs = (P(None, "ctx", "head"), P(None, "head", None, None), P("head", None, None))
    return jax.shard_map(body, mesh=mesh, in_specs=in_specs, out_specs=out_specs, check_vma=False)
```

```python
import functools
import math

import jax
import jax.numpy as jnp
from jax import lax
from jax.experimental import pallas as pl
from jax.experimental.pallas import tpu as pltpu
from jax.sharding import PartitionSpec as P

HD = 128
WIN = 512
TILE = 256
MASKED = -1e30
BF = jnp.bfloat16
F32 = jnp.float32
PARTS = 2
AHEAD = 1
FAST_TILE = 256
EDGES = [(0, 1), (1, 0), (2, 3), (3, 2)]
LIMIT = 36 * 1024 * 1024


def mm(a, b):
    return jnp.dot(a, b, preferred_element_type=F32)


def mm_nt(a, b):
    return lax.dot_general(a, b, (((1,), (1,)), ((), ())), preferred_element_type=F32)


def mm_tn(a, b):
    return lax.dot_general(a, b, (((0,), (0,)), ((), ())), preferred_element_type=F32)


def sigmoid(x):
    return 0.5 + 0.5 * jnp.tanh(0.5 * x)


def whole(array):
    return pl.BlockSpec(memory_space=pltpu.VMEM)


def whole_out(shape):
    return pl.BlockSpec(memory_space=pltpu.VMEM)


def call(
    kernel, name, scalars, inputs, specs, outs, earlier=(), passing=(), scratch=(), grid=(1,), out_specs=None, aliases=None
):
    single = not isinstance(outs, (list, tuple)) and not passing
    outs_list = list(outs) if isinstance(outs, (list, tuple)) else [outs]
    any_spec = pl.BlockSpec(memory_space=pl.ANY)
    first = 1 + len(inputs)
    past = first + len(earlier) + len(passing)

    def ordered(*refs):
        kernel(*refs[:first], *refs[past : past + len(outs_list)], *refs[past + len(outs_list) + len(passing) :])

    pass_at = {first + len(earlier) + i: len(outs_list) + i for i in range(len(passing))}
    got = pl.pallas_call(
        ordered,
        out_shape=[*outs_list, *[like(x) for x in passing]],
        grid_spec=pltpu.PrefetchScalarGridSpec(
            num_scalar_prefetch=1,
            grid=grid,
            in_specs=[*specs, *[any_spec for _ in (*earlier, *passing)]],
            out_specs=[*(out_specs or [whole_out(o.shape) for o in outs_list]), *[any_spec for _ in passing]],
            scratch_shapes=list(scratch),
        ),
        input_output_aliases={**{k + 1: v for k, v in (aliases or {}).items()}, **pass_at},
        compiler_params=pltpu.CompilerParams(vmem_limit_bytes=LIMIT),
        cost_estimate=pl.CostEstimate(flops=20 * 10**9, bytes_accessed=1, transcendentals=0),
        name=name,
    )(scalars, *inputs, *earlier, *passing)
    return got[0] if single else got


def like(array, dtype=None):
    return jax.ShapeDtypeStruct(array.shape, dtype or array.dtype)


def grads_kernel(block, step_scale, sc, k_ref, v_ref, lr_ref, w1_ref, w3_ref, w2_ref, keep_ref, send_ref, acc):
    step = pl.program_id(0)
    k = k_ref[...]
    w_two = w2_ref[...]
    rates = lr_ref[0, block : block + 1, :] * step_scale
    rates = jnp.broadcast_to(rates, (HD, rates.shape[1])).T[:, :1]
    out_grad = (-rates * v_ref[...].astype(F32)).astype(BF)
    gate = mm(k, w1_ref[...])
    up = mm(k, w3_ref[...])
    hidden_grad = mm_nt(out_grad, w_two)
    sig = sigmoid(gate)
    gate_sig = gate * sig
    hidden = (gate_sig * up).astype(BF)
    up_grad = (hidden_grad * gate_sig).astype(BF)
    gate_grad = (hidden_grad * up * sig * (1.0 + gate - gate_sig)).astype(BF)
    parts = (mm_tn(k, gate_grad), mm_tn(k, up_grad), mm_tn(hidden, out_grad))

    @pl.when(step == 0)
    def _():
        for i, part in enumerate(parts):
            acc[i] = part

    @pl.when(step > 0)
    def _():
        for i, part in enumerate(parts):
            acc[i] = acc[i] + part

    @pl.when(step == pl.num_programs(0) - 1)
    def _():
        half = keep_ref.shape[1]
        own = pl.multiple_of(sc[0] * half, half)
        other = pl.multiple_of((1 - sc[0]) * half, half)
        keep_ref[...] = acc[:, pl.ds(own, half), :]
        send_ref[...] = acc[:, pl.ds(other, half), :].astype(BF)


def block_grads(block, scalars, projected, learn_rates, weights, step_scale, weight_specs, earlier=(), own=None):
    _, _, rows, feats = projected.shape
    half = feats // 2
    shape = jax.ShapeDtypeStruct((3, half, feats), BF)
    tile = rows
    return call(
        functools.partial(grads_kernel, block, step_scale),
        f"grads_{block}",
        scalars,
        (*(own or (projected, projected)), learn_rates, *weights),
        [
            *(
                [whole(x) for x in own]
                if own
                else [
                    pl.BlockSpec((None, None, tile, feats), lambda i, s: (1, block, i, 0)),
                    pl.BlockSpec((None, None, tile, feats), lambda i, s: (2, block, i, 0)),
                ]
            ),
            pl.BlockSpec((1, learn_rates.shape[1], tile), lambda i, s: (0, 0, i)),
            *weight_specs,
        ],
        [jax.ShapeDtypeStruct(shape.shape, F32), shape],
        scratch=[pltpu.VMEM((3, feats, feats), F32)],
        grid=(rows // tile,),
        earlier=earlier,
    )


def window_scores(q, keys, usable):
    rows = q.shape[0]
    row_ids = lax.broadcasted_iota(jnp.int32, (rows, rows), 0)
    col_ids = lax.broadcasted_iota(jnp.int32, (rows, rows), 1)
    scores = []
    last = len(keys) - 1
    for i, (key, before) in enumerate(keys):
        s = mm_nt(q, key)
        if before and usable is not None:
            s = s + usable
        if i == 0:
            s = jnp.where(col_ids > row_ids, s, MASKED)
        if i == last:
            s = jnp.where(col_ids <= row_ids, s, MASKED)
        scores.append(s)
    return scores


def weigh(scores, values):
    scale = math.log2(math.e) / math.sqrt(HD)
    peak = jnp.max(functools.reduce(jnp.maximum, scores), axis=-1, keepdims=True) * scale
    result = None
    for s, value in zip(scores, values):
        lifted = jnp.exp2(s * scale - peak).astype(BF)
        part = mm(lifted, jnp.concatenate([value, jnp.ones_like(value)], axis=1))
        result = part if result is None else result + part
    return (result[:, :HD] / result[:, HD:]).astype(BF)


def attend(q_ref, k_ref, v_ref, halo, usable, store):
    rows, feats = q_ref.shape
    tile = min(TILE, rows)

    def pieces(start, cols, which, own_ref):
        for at in range(start - WIN, start + tile, tile):
            before = at < 0
            where = slice(at + WIN, at + WIN + tile) if before else slice(at, at + tile)
            yield (halo[which][where, cols] if before else own_ref[where, cols]), before

    work = [
        (start, slice(head * HD, (head + 1) * HD)) for start in range(0, rows, tile) for head in range(feats // HD)
    ]
    scored = []
    for start, cols in work:
        scored.append(window_scores(q_ref[start : start + tile, cols], list(pieces(start, cols, 0, k_ref)), usable))
        if len(scored) > AHEAD:
            at, there = work[len(scored) - 1 - AHEAD]
            values = [value for value, _ in pieces(at, there, 1, v_ref)]
            store(slice(at, at + tile), there, weigh(scored[len(scored) - 1 - AHEAD], values))
    for (at, there), scores in zip(work[len(work) - AHEAD :], scored[len(work) - AHEAD :]):
        values = [value for value, _ in pieces(at, there, 1, v_ref)]
        store(slice(at, at + tile), there, weigh(scores, values))


def fast_rows(q, w_one, w_three, w_two):
    gate = mm(q, w_one)
    up = mm(q, w_three)
    hidden = (gate * sigmoid(gate) * up).astype(BF)
    result = mm(hidden, w_two)
    return result * lax.rsqrt(jnp.mean(result * result, axis=-1, keepdims=True) + 1e-05)


def usable_bias(block, sc):
    if block > 0:
        return None
    return jnp.where(sc[1] > 0, 0.0, MASKED).astype(F32)


def mixed_kernel(block, sc, q_ref, k_ref, v_ref, k_halo, v_halo, w1_ref, w3_ref, w2_ref, out_ref, att):
    def store(rows, cols, value):
        att[rows, cols] = value

    attend(q_ref, k_ref, v_ref, (k_halo, v_halo), usable_bias(block, sc), store)
    rows = q_ref.shape[0]
    tile = min(TILE, rows)
    for start in range(0, rows, tile):
        at = slice(start, start + tile)
        fast = fast_rows(q_ref[at, :], w1_ref[...], w3_ref[...], w2_ref[...])
        out_ref[at, :] = (att[at, :].astype(F32) + fast).astype(BF)


def attend_kernel(block, sc, q_ref, k_ref, v_ref, halo_ref, out_ref):
    def store(rows, cols, value):
        out_ref[rows, cols] = value

    attend(q_ref, k_ref, v_ref, (halo_ref.at[0], halo_ref.at[1]), usable_bias(block, sc), store)


def qkv_specs(block, projected):
    _, _, rows, feats = projected.shape
    return [
        pl.BlockSpec((None, None, rows, feats), functools.partial(lambda kind, i, s: (kind, block, 0, 0), kind))
        for kind in range(3)
    ]


def attention_only(block, scalars, projected, halo, earlier=(), passing=()):
    _, _, rows, feats = projected.shape
    return call(
        functools.partial(attend_kernel, block),
        f"attend_{block}",
        scalars,
        (projected, projected, projected, halo),
        [*qkv_specs(block, projected), whole(halo)],
        jax.ShapeDtypeStruct((rows, feats), BF),
        earlier=earlier,
        passing=passing,
    )


def mixed_first(block, scalars, projected, halo, weights, weight_specs, earlier=()):
    _, _, rows, feats = projected.shape
    return call(
        functools.partial(mixed_kernel, block),
        f"mixed_{block}",
        scalars,
        (projected, projected, projected, *halo, *weights),
        [*qkv_specs(block, projected), *[whole(x) for x in halo], *weight_specs],
        jax.ShapeDtypeStruct((rows, feats), BF),
        scratch=[pltpu.VMEM((rows, feats), BF)],
        earlier=earlier,
    )


def halves(parity, mine, theirs):
    half = mine.shape[0]
    own = pl.multiple_of(parity * half, half)
    other = pl.multiple_of((1 - parity) * half, half)
    return ((pl.ds(own, half), mine), (pl.ds(other, half), theirs))


def renorm_all(old, mine, theirs, parity, moved, put, known=None):
    ratios = []
    for i in range(3):
        before = None if known is None else known[i, 0:1, 0:1]
        after = None
        for rows, part in halves(parity, mine[i], theirs[i]):
            w = old(i, rows).astype(F32)
            new = w - part.astype(F32)
            moved[i, rows, :] = new
            squares = jnp.sum(new * new, axis=0, keepdims=True)
            after = squares if after is None else after + squares
            if known is None:
                squares = jnp.sum(w * w, axis=0, keepdims=True)
                before = squares if before is None else before + squares
        after = jnp.sum(after, axis=1, keepdims=True)
        if known is None:
            before = jnp.sum(before, axis=1, keepdims=True)
        ratios.append(jnp.sqrt(before) / jnp.sqrt(after + 1e-06))
    for i in range(3):
        half = mine.shape[1]
        for start in (0, half):
            rows = slice(start, start + half)
            put(i, rows, moved[i, rows, :] * ratios[i])


def old_of(refs, i, rows):
    if len(refs) == 1:
        return refs[0][i, rows, :]
    return refs[0][i, 0, rows, :] if i < 2 else refs[1][0, rows, :]


def update_kernel(states, pieces, sc, mine_ref, theirs_ref, *refs):
    *refs, moved = refs
    old, (q_ref, att_ref, mix_ref, new_bf_ref), piece_refs = refs[:states], refs[states : states + 4], refs[states + 4 :]

    def put(i, rows, value):
        new_bf_ref[i, rows, :] = value.astype(BF)

    renorm_all(functools.partial(old_of, old), mine_ref, theirs_ref, sc[0], moved, put)
    rows = q_ref.shape[0]
    tile = min(FAST_TILE, rows)
    for start in range(0, rows, tile):
        at = slice(start, start + tile)
        fast = fast_rows(q_ref[at, :], new_bf_ref[0], new_bf_ref[1], new_bf_ref[2])
        mix_ref[at, :] = (att_ref[at, :].astype(F32) + fast).astype(BF)
    for i, piece_ref in enumerate(piece_refs):
        size = piece_ref.shape[0]
        piece_ref[...] = mix_ref[i * size : (i + 1) * size, :]


def update_and_mix(block, scalars, mine, theirs, state, projected, attended, parts, earlier=()):
    _, _, rows, feats = projected.shape
    pieces = parts if parts > 1 else 0
    got = call(
        functools.partial(update_kernel, len(state), pieces),
        f"update_{block}",
        scalars,
        (mine, theirs, *state, projected, attended),
        [
            whole(mine),
            whole(theirs),
            *[whole(a) for a in state],
            pl.BlockSpec((None, None, rows, feats), lambda i, s: (0, block, 0, 0)),
            whole(attended),
        ],
        [
            jax.ShapeDtypeStruct((rows, feats), BF),
            jax.ShapeDtypeStruct((3, feats, feats), BF),
            *[jax.ShapeDtypeStruct((rows // parts, feats), BF) for _ in range(pieces)],
        ],
        scratch=[pltpu.VMEM((3, *mine.shape[2:] * 2), F32)],
        earlier=earlier,
    )
    return got[0], got[1], got[2:] or [got[0]]


def state_kernel(states, sc, mine_ref, theirs_ref, *refs):
    old, (new_ref, norm_ref, moved) = refs[:states], refs[states:]

    def put(i, rows, value):
        new_ref[i, rows, :] = value

    renorm_all(functools.partial(old_of, old), mine_ref, theirs_ref, sc[0], moved, put)
    for i in range(3):
        norm_ref[i] = jnp.full(norm_ref.shape[1:], jnp.sum(new_ref[i] * new_ref[i]), F32)


def float_state(block, scalars, mine, theirs, state, earlier=()):
    feats = mine.shape[2]
    return call(
        functools.partial(state_kernel, len(state)),
        f"state_{block}",
        scalars,
        (mine, theirs, *state),
        [whole(mine), whole(theirs), *[whole(a) for a in state]],
        [jax.ShapeDtypeStruct((3, feats, feats), F32), jax.ShapeDtypeStruct((3, 8, HD), F32)],
        scratch=[pltpu.VMEM((3, feats, feats), F32)],
        earlier=earlier,
    )


def final_kernel(sc, mine_ref, theirs_ref, old_ref, norm_ref, up_out, down_out, token, moved, done, sems):
    token[...] = jnp.zeros_like(token)
    half = mine_ref.shape[1]
    outs = (up_out.at[0, 0], up_out.at[1, 0], down_out.at[0])
    copies = []

    def put(i, rows, value):
        done[i, rows, :] = value
        part = rows.start // half
        copy = pltpu.make_async_copy(done.at[i, rows, :], outs[i].at[rows, :], sems.at[i, part])
        copy.start()
        copies.append(copy)

    renorm_all(lambda i, rows: old_ref[i, rows, :], mine_ref, theirs_ref, sc[0], moved, put, norm_ref)
    for copy in copies:
        copy.wait()


def final_update(scalars, mine, theirs, state, norms, earlier=()):
    _, half, feats = mine.shape
    any_spec = pl.BlockSpec(memory_space=pl.ANY)
    return call(
        final_kernel,
        "final_update",
        scalars,
        (mine, theirs, state, norms),
        [whole(mine), whole(theirs), whole(state), whole(norms)],
        [
            jax.ShapeDtypeStruct((2, 1, feats, feats), F32),
            jax.ShapeDtypeStruct((1, feats, feats), F32),
            jax.ShapeDtypeStruct((8, HD), F32),
        ],
        out_specs=[any_spec, any_spec, whole_out((8, HD))],
        scratch=[
            pltpu.VMEM((3, feats, feats), F32),
            pltpu.VMEM((3, feats, feats), F32),
            pltpu.SemaphoreType.DMA((3, 2)),
        ],
        earlier=earlier,
    )


def pick_kernel(sc, w_ref, out_ref):
    half = out_ref.shape[1]
    feats = 2 * half
    for i in range(3):
        start = (sc[2] ^ (i + 1)) * feats + sc[0] * half
        out_ref[i] = w_ref[pl.ds(pl.multiple_of(start, half), half), :]


def pick_parts(scalars, w_out, earlier=()):
    feats = w_out.shape[1]
    return call(
        pick_kernel,
        "pick_parts",
        scalars,
        (w_out,),
        [whole(w_out)],
        jax.ShapeDtypeStruct((3, feats // 2, feats), BF),
        earlier=earlier,
    )


def gate_kernel(sc, x_ref, x_out_ref):
    pass


def gate(scalars, x, earlier):
    return call(
        gate_kernel,
        "gate",
        scalars,
        (x,),
        [pl.BlockSpec(memory_space=pl.ANY)],
        like(x),
        out_specs=[pl.BlockSpec(memory_space=pl.ANY)],
        aliases={0: 0},
        earlier=earlier,
    )


def split_kernel(sc, x_ref, *piece_refs):
    size = piece_refs[0].shape[0]
    for i, piece_ref in enumerate(piece_refs):
        piece_ref[...] = x_ref[i * size : (i + 1) * size, :]


def split(scalars, x, parts, earlier):
    rows, feats = x.shape
    piece = jax.ShapeDtypeStruct((rows // parts, feats), BF)
    return call(split_kernel, "split", scalars, (x,), [whole(x)], [piece] * parts, earlier=earlier)


def add_kernel(sc, a_ref, b_ref, out_ref):
    out_ref[...] = (a_ref[...].astype(F32) + b_ref[...].astype(F32)).astype(BF)


def add(scalars, a, b, earlier=(), passing=()):
    return call(add_kernel, "add", scalars, (a, b), [whole(a), whole(b)], like(a, BF), earlier=earlier, passing=passing)


def pack_kernel(sc, k_ref, v_ref, out_ref):
    out_ref[0] = k_ref[...]
    out_ref[1] = v_ref[...]


def first_rows(projected, kind):
    _, _, rows, feats = projected.shape
    return lax.slice(projected, (kind, 0, 0, 0), (kind + 1, 1, rows, feats)).reshape(rows, feats)


def pack_halo(block, scalars, projected, last, earlier=()):
    _, _, rows, feats = projected.shape

    def which(s):
        return block if block == 0 else jnp.where(s[1] == last, block - 1, block)

    return call(
        pack_kernel,
        f"pack_{block}",
        scalars,
        (projected, projected),
        [
            pl.BlockSpec((None, None, WIN, feats), lambda i, s: (1, which(s), rows // WIN - 1, 0)),
            pl.BlockSpec((None, None, WIN, feats), lambda i, s: (2, which(s), rows // WIN - 1, 0)),
        ],
        jax.ShapeDtypeStruct((2, WIN, feats), BF),
        earlier=earlier,
    )


def edge_kernel(sc, m_ref, ya_ref, yb_ref, mine_ref, theirs_ref, out_ref):
    half = mine_ref.shape[1]
    total = None
    for part, parity in ((mine_ref, sc[0]), (theirs_ref, 1 - sc[0])):
        cols = pl.ds(pl.multiple_of(parity * half, half), half)
        for i, ref in enumerate((m_ref, ya_ref, yb_ref)):
            term = mm(ref[:, cols], part[i])
            total = term if total is None else total + term
    out_ref[...] = total.astype(BF)


def part_spec(rows, feats, part):
    return pl.BlockSpec((rows, feats), lambda i, s: (part, 0))


def edge_part(name, scalars, part, m, ya, yb, v_mine, v_other, earlier=(), passing=()):
    rows, feats = yb.shape
    return call(
        edge_kernel,
        f"edge_{name}",
        scalars,
        (m, ya, yb, v_mine, v_other),
        [part_spec(rows, feats, part), part_spec(rows, feats, part), whole(yb), whole(v_mine), whole(v_other)],
        jax.ShapeDtypeStruct((rows, feats), BF),
        earlier=earlier,
        passing=passing,
    )


def for_edge(sc, c):
    return jnp.where(sc[3] == 0, c.astype(F32), 0.0)


def own_rows(sc, m, x, ya, yb, w_ref, hid, put, get):
    feats = w_ref.shape[1]
    head = sc[2]

    def weight(which):
        return w_ref[pl.ds(pl.multiple_of(which * feats, feats), feats), :]

    put(hid.astype(F32) + mm(m, weight(head)))

    @pl.when(sc[3] == 1)
    def _():
        put(get() + mm(x[...], weight(head ^ 1)) + mm(ya[...], weight(head ^ 3)) + mm(yb[...], weight(head ^ 2)))


def own_kernel(sc, m_ref, x_ref, ya_ref, yb_ref, w_ref, hid_ref, c_ref, *refs):
    out_ref, token, acc = refs[-3:]
    token[...] = jnp.zeros_like(token)

    def put(value):
        acc[...] = value

    own_rows(sc, m_ref[...], x_ref, ya_ref, yb_ref, w_ref, hid_ref[...], put, lambda: acc[...])
    out_ref[...] = (acc[...] + for_edge(sc, c_ref[...])).astype(BF)


def own_part(block, scalars, m, x, ya, yb, w_out, hidden_in, c, so_far, earlier=()):
    rows, feats = m.shape
    return call(
        own_kernel,
        f"own_{block}",
        scalars,
        (m, x, ya, yb, w_out, hidden_in, c, *so_far),
        [
            *[whole(a) for a in (m, x, ya, yb, w_out)],
            pl.BlockSpec((None, rows, feats), lambda i, s: (block, 0, 0)),
            whole(c),
            *[pl.BlockSpec(memory_space=pl.ANY) for _ in so_far],
        ],
        [like(hidden_in), jax.ShapeDtypeStruct((8, HD), F32)],
        out_specs=[pl.BlockSpec((None, rows, feats), lambda i, s: (block, 0, 0)), whole_out((8, HD))],
        aliases={7: 0} if so_far else None,
        scratch=[pltpu.VMEM((rows, feats), F32)],
        earlier=earlier,
    )


def last_kernel(parts, sc, *refs):
    m_ref, ya_ref = refs[:2]
    xs, ybs = refs[2 : 2 + parts], refs[2 + parts : 2 + 2 * parts]
    w_ref, hid_ref, out_ref = refs[2 + 2 * parts :]
    rows = m_ref.shape[0] // parts
    for i in range(parts):
        at = pl.ds(i * rows, rows)

        def put(value, at=at):
            out_ref[at, :] = value

        own_rows(
            sc, m_ref[at, :], xs[i], ya_ref.at[at, :], ybs[i], w_ref, hid_ref[at, :], put, lambda at=at: out_ref[at, :]
        )


def own_last(block, scalars, m, xs, ya, ybs, w_out, hidden_in, earlier=()):
    rows, feats = m.shape
    return call(
        functools.partial(last_kernel, len(xs)),
        f"own_{block}",
        scalars,
        (m, ya, *xs, *ybs, w_out, hidden_in),
        [
            *[whole(a) for a in (m, ya, *xs, *ybs, w_out)],
            pl.BlockSpec((None, rows, feats), lambda i, s: (block, 0, 0)),
        ],
        jax.ShapeDtypeStruct((rows, feats), F32),
        earlier=earlier,
    )


def finish_kernel(block, parts, sc, acc_ref, *refs):
    out_ref, done, sems = refs[-3:]
    rows = acc_ref.shape[0] // parts
    copies = []
    for i in range(parts):
        at = slice(i * rows, (i + 1) * rows)
        done[at, :] = (acc_ref[at, :] + for_edge(sc, refs[i][...])).astype(BF)
        copies.append(pltpu.make_async_copy(done.at[at, :], out_ref.at[block, at, :], sems.at[i]))
        copies[-1].start()
    for copy in copies:
        copy.wait()


def finish(block, scalars, acc, cs, so_far, earlier=()):
    any_spec = pl.BlockSpec(memory_space=pl.ANY)
    return call(
        functools.partial(finish_kernel, block, len(cs)),
        "finish",
        scalars,
        (acc, *cs, so_far),
        [whole(acc), *[whole(c) for c in cs], any_spec],
        like(so_far),
        out_specs=[any_spec],
        aliases={1 + len(cs): 0},
        scratch=[pltpu.VMEM(acc.shape, BF), pltpu.SemaphoreType.DMA((len(cs),))],
        earlier=earlier,
    )


def move(x, axis, pairs):
    return lax.ppermute(x, axis, pairs)


def between_inner(x):
    count = lax.axis_size("ctx")
    planes = lax.axis_size("head")
    pairs = []
    for i in range(count):
        pairs += [(i * planes + 1, i * planes + 2), (i * planes + 2, i * planes + 1)]
        pairs += [(i * planes + j, (i ^ 1) * planes + j) for j in (0, 3)]
    return move(x, ("ctx", "head"), pairs)


def flip(x, bit):
    count = lax.axis_size("ctx")
    return move(x, "ctx", [(i, i ^ (1 << bit)) for i in range(count)])


def partners(count, step):
    bits = list(range(1, count.bit_length() - 1))
    return [(i, i ^ (1 << (bits if i % 2 == 0 else bits[::-1])[step])) for i in range(count)]


def body(hidden_in, projected, w_out, fast_up, fast_down, learn_rates):
    blocks, rows, feats = hidden_in.shape
    ctx = lax.axis_index("ctx")
    head = lax.axis_index("head")
    ctx_count = lax.axis_size("ctx")
    steps = ctx_count.bit_length() - 2
    parity = ctx % 2
    inner = ((head == 1) | (head == 2)).astype(jnp.int32)
    scalars = jnp.stack([parity, ctx, head, inner]).astype(jnp.int32)
    step_scale = 1.0 / math.sqrt(rows * ctx_count)
    around = [(i, (i + 1) % ctx_count) for i in range(ctx_count)]

    up_spec = [
        pl.BlockSpec((None, None, feats, feats), lambda *_: (0, 0, 0, 0)),
        pl.BlockSpec((None, None, feats, feats), lambda *_: (1, 0, 0, 0)),
        pl.BlockSpec((None, feats, feats), lambda *_: (0, 0, 0)),
    ]
    bf_spec = [
        pl.BlockSpec((None, feats, feats), functools.partial(lambda k, *_: (k, 0, 0), k)) for k in range(3)
    ]

    weights, specs = (fast_up, fast_up, fast_down), up_spec
    state = (fast_up, fast_down)

    kv_now = [first_rows(projected, kind) for kind in (1, 2)]
    halo = [move(x[rows - WIN :], "ctx", around) for x in kv_now]
    keep, send = block_grads(0, scalars, projected, learn_rates, weights, step_scale, specs, own=kv_now)
    keep = gate(scalars, keep, earlier=(send,))
    total = add(scalars, keep, flip(send, 0))
    received = move(total, "ctx", partners(ctx_count, 0))
    kv_now = pack_halo(1, scalars, projected, ctx_count - 1, earlier=(total,))
    halo_next = move(kv_now, "ctx", around)
    mixed = mixed_first(0, scalars, projected, halo, weights, specs, earlier=(kv_now,))
    x = move(mixed, "head", EDGES)
    ya = between_inner(mixed)
    v_send = last = pick_parts(scalars, w_out, earlier=(mixed,))
    v_mine = move(v_send, "head", EDGES)
    so_far = ()
    for block in range(1, blocks):
        for step in range(steps):
            total = last = add(scalars, total, received, earlier=(last,))
            if step + 1 < steps:
                received = move(total, "ctx", partners(ctx_count, step + 1))
            if step == 0:
                attended = last = attention_only(block, scalars, projected, halo_next, earlier=(last,))
                x = last = gate(scalars, x, earlier=(last,))
                yb = between_inner(x)
        theirs = flip(total, 0)
        ya = last = gate(scalars, ya, earlier=(total,))
        mixed_next, new_bf = update_and_mix(
            block, scalars, total, theirs, state, projected, attended, 1, earlier=(last,)
        )[:2]
        x_next = move(mixed_next, "head", EDGES)
        ya_next = between_inner(mixed_next)
        weights, specs = (new_bf, new_bf, new_bf), bf_spec
        keep, send = block_grads(
            block, scalars, projected, learn_rates, weights, step_scale, specs, earlier=(mixed_next,)
        )
        if block == 1:
            v_mine = last = gate(scalars, v_mine, earlier=(send,))
            v_other = flip(v_mine, 0)
        else:
            keep = last = gate(scalars, keep, earlier=(send,))
        summed = add(scalars, keep, flip(send, 0), earlier=(last,))
        received = move(summed, "ctx", partners(ctx_count, 0))
        c = last = edge_part(block - 1, scalars, 0, mixed, ya, yb, v_mine, v_other, earlier=(summed,))
        c_there = move(c, "head", EDGES)
        if block < blocks - 1:
            now, norms = float_state(block, scalars, total, theirs, state, earlier=(last,))
            kv_now = last = pack_halo(block + 1, scalars, projected, ctx_count - 1, earlier=(norms,))
            halo_next = move(kv_now, "ctx", around)
            out, last = own_part(
                block - 1, scalars, mixed, x, ya, yb, w_out, hidden_in, c_there, so_far, earlier=(last,)
            )
            so_far = (out,)
            state, total = (now,), summed
            mixed, x, ya = mixed_next, x_next, ya_next
    now, norms = float_state(blocks - 1, scalars, total, theirs, state, earlier=(last,))
    xs = split(scalars, x_next, PARTS, (norms,))
    ybs = [between_inner(piece) for piece in xs]
    total, last = summed, xs[0]
    for step in range(steps):
        total = last = add(scalars, total, received, earlier=(last,))
        if step + 1 < steps:
            received = move(total, "ctx", partners(ctx_count, step + 1))
        if step == 0:
            c_last = []
            for i in range(PARTS):
                c = last = edge_part(
                    f"{blocks - 1}_{i}", scalars, i, mixed_next, ya_next, ybs[i], v_mine, v_other, earlier=(last,)
                )
                c_last.append(move(c, "head", EDGES))
                if i == 0:
                    out, last = own_part(
                        blocks - 2, scalars, mixed, x, ya, yb, w_out, hidden_in, c_there, so_far, earlier=(last,)
                    )
    theirs = flip(total, 0)
    acc = own_last(blocks - 1, scalars, mixed_next, xs, ya_next, ybs, w_out, hidden_in, earlier=(total,))
    up_final, down_final, token = final_update(scalars, total, theirs, now, norms, earlier=(acc,))
    out = finish(blocks - 1, scalars, acc, c_last, out, earlier=(token,))
    return out, up_final, down_final


def solution(mesh):
    in_specs = (
        P(None, "ctx", "head"),
        P(None, None, "ctx", "head"),
        P(None, "head"),
        P(None, "head", None, None),
        P("head", None, None),
        P("head", None, "ctx"),
    )
    out_specs = (P(None, "ctx", "head"), P(None, "head", None, None), P("head", None, None))
    return jax.shard_map(body, mesh=mesh, in_specs=in_specs, out_specs=out_specs, check_vma=False)
```

```python
import functools
import math

import jax
import jax.numpy as jnp
from jax import lax
from jax.experimental import pallas as pl
from jax.experimental.pallas import tpu as pltpu
from jax.sharding import PartitionSpec as P

HD = 128
WIN = 512
TILE = 256
MASKED = -1e30
BF = jnp.bfloat16
F32 = jnp.float32
PARTS = 2
AHEAD = 1
FAST_TILE = 256
EDGES = [(0, 1), (1, 0), (2, 3), (3, 2)]
LIMIT = 36 * 1024 * 1024


def mm(a, b):
    return jnp.dot(a, b, preferred_element_type=F32)


def mm_nt(a, b):
    return lax.dot_general(a, b, (((1,), (1,)), ((), ())), preferred_element_type=F32)


def mm_tn(a, b):
    return lax.dot_general(a, b, (((0,), (0,)), ((), ())), preferred_element_type=F32)


def sigmoid(x):
    return 0.5 + 0.5 * jnp.tanh(0.5 * x)


def whole(array):
    return pl.BlockSpec(memory_space=pltpu.VMEM)


def whole_out(shape):
    return pl.BlockSpec(memory_space=pltpu.VMEM)


def call(
    kernel, name, scalars, inputs, specs, outs, earlier=(), passing=(), scratch=(), grid=(1,), out_specs=None, aliases=None
):
    single = not isinstance(outs, (list, tuple)) and not passing
    outs_list = list(outs) if isinstance(outs, (list, tuple)) else [outs]
    any_spec = pl.BlockSpec(memory_space=pl.ANY)
    first = 1 + len(inputs)
    past = first + len(earlier) + len(passing)

    def ordered(*refs):
        kernel(*refs[:first], *refs[past : past + len(outs_list)], *refs[past + len(outs_list) + len(passing) :])

    pass_at = {first + len(earlier) + i: len(outs_list) + i for i in range(len(passing))}
    got = pl.pallas_call(
        ordered,
        out_shape=[*outs_list, *[like(x) for x in passing]],
        grid_spec=pltpu.PrefetchScalarGridSpec(
            num_scalar_prefetch=1,
            grid=grid,
            in_specs=[*specs, *[any_spec for _ in (*earlier, *passing)]],
            out_specs=[*(out_specs or [whole_out(o.shape) for o in outs_list]), *[any_spec for _ in passing]],
            scratch_shapes=list(scratch),
        ),
        input_output_aliases={**{k + 1: v for k, v in (aliases or {}).items()}, **pass_at},
        compiler_params=pltpu.CompilerParams(vmem_limit_bytes=LIMIT),
        cost_estimate=pl.CostEstimate(flops=20 * 10**9, bytes_accessed=1, transcendentals=0),
        name=name,
    )(scalars, *inputs, *earlier, *passing)
    return got[0] if single else got


def like(array, dtype=None):
    return jax.ShapeDtypeStruct(array.shape, dtype or array.dtype)


def grads_kernel(block, step_scale, sc, k_ref, v_ref, lr_ref, w1_ref, w3_ref, w2_ref, keep_ref, send_ref, acc):
    step = pl.program_id(0)
    k = k_ref[...]
    w_two = w2_ref[...]
    rates = lr_ref[0, block : block + 1, :] * step_scale
    rates = jnp.broadcast_to(rates, (HD, rates.shape[1])).T[:, :1]
    out_grad = (-rates * v_ref[...].astype(F32)).astype(BF)
    gate = mm(k, w1_ref[...])
    up = mm(k, w3_ref[...])
    hidden_grad = mm_nt(out_grad, w_two)
    sig = sigmoid(gate)
    gate_sig = gate * sig
    hidden = (gate_sig * up).astype(BF)
    up_grad = (hidden_grad * gate_sig).astype(BF)
    gate_grad = (hidden_grad * up * sig * (1.0 + gate - gate_sig)).astype(BF)
    parts = (mm_tn(k, gate_grad), mm_tn(k, up_grad), mm_tn(hidden, out_grad))

    @pl.when(step == 0)
    def _():
        for i, part in enumerate(parts):
            acc[i] = part

    @pl.when(step > 0)
    def _():
        for i, part in enumerate(parts):
            acc[i] = acc[i] + part

    @pl.when(step == pl.num_programs(0) - 1)
    def _():
        half = keep_ref.shape[1]
        own = pl.multiple_of(sc[0] * half, half)
        other = pl.multiple_of((1 - sc[0]) * half, half)
        keep_ref[...] = acc[:, pl.ds(own, half), :]
        send_ref[...] = acc[:, pl.ds(other, half), :].astype(BF)


def block_grads(block, scalars, projected, learn_rates, weights, step_scale, weight_specs, earlier=(), own=None):
    _, _, rows, feats = projected.shape
    half = feats // 2
    shape = jax.ShapeDtypeStruct((3, half, feats), BF)
    tile = rows
    return call(
        functools.partial(grads_kernel, block, step_scale),
        f"grads_{block}",
        scalars,
        (*(own or (projected, projected)), learn_rates, *weights),
        [
            *(
                [whole(x) for x in own]
                if own
                else [
                    pl.BlockSpec((None, None, tile, feats), lambda i, s: (1, block, i, 0)),
                    pl.BlockSpec((None, None, tile, feats), lambda i, s: (2, block, i, 0)),
                ]
            ),
            pl.BlockSpec((1, learn_rates.shape[1], tile), lambda i, s: (0, 0, i)),
            *weight_specs,
        ],
        [jax.ShapeDtypeStruct(shape.shape, F32), shape],
        scratch=[pltpu.VMEM((3, feats, feats), F32)],
        grid=(rows // tile,),
        earlier=earlier,
    )


def window_scores(q, keys, usable):
    rows = q.shape[0]
    row_ids = lax.broadcasted_iota(jnp.int32, (rows, rows), 0)
    col_ids = lax.broadcasted_iota(jnp.int32, (rows, rows), 1)
    scores = []
    last = len(keys) - 1
    for i, (key, before) in enumerate(keys):
        s = mm_nt(q, key)
        if before and usable is not None:
            s = s + usable
        if i == 0:
            s = jnp.where(col_ids > row_ids, s, MASKED)
        if i == last:
            s = jnp.where(col_ids <= row_ids, s, MASKED)
        scores.append(s)
    return scores


def weigh(scores, values):
    scale = math.log2(math.e) / math.sqrt(HD)
    peak = jnp.max(functools.reduce(jnp.maximum, scores), axis=-1, keepdims=True) * scale
    result = None
    for s, value in zip(scores, values):
        lifted = jnp.exp2(s * scale - peak).astype(BF)
        part = mm(lifted, jnp.concatenate([value, jnp.ones_like(value)], axis=1))
        result = part if result is None else result + part
    return (result[:, :HD] / result[:, HD:]).astype(BF)


def attend(q_ref, k_ref, v_ref, halo, usable, store):
    rows, feats = q_ref.shape
    tile = min(TILE, rows)

    def pieces(start, cols, which, own_ref):
        for at in range(start - WIN, start + tile, tile):
            before = at < 0
            where = slice(at + WIN, at + WIN + tile) if before else slice(at, at + tile)
            yield (halo[which][where, cols] if before else own_ref[where, cols]), before

    work = [
        (start, slice(head * HD, (head + 1) * HD)) for start in range(0, rows, tile) for head in range(feats // HD)
    ]
    scored = []
    for start, cols in work:
        scored.append(window_scores(q_ref[start : start + tile, cols], list(pieces(start, cols, 0, k_ref)), usable))
        if len(scored) > AHEAD:
            at, there = work[len(scored) - 1 - AHEAD]
            values = [value for value, _ in pieces(at, there, 1, v_ref)]
            store(slice(at, at + tile), there, weigh(scored[len(scored) - 1 - AHEAD], values))
    for (at, there), scores in zip(work[len(work) - AHEAD :], scored[len(work) - AHEAD :]):
        values = [value for value, _ in pieces(at, there, 1, v_ref)]
        store(slice(at, at + tile), there, weigh(scores, values))


def fast_rows(q, w_one, w_three, w_two):
    gate = mm(q, w_one)
    up = mm(q, w_three)
    hidden = (gate * sigmoid(gate) * up).astype(BF)
    result = mm(hidden, w_two)
    return result * lax.rsqrt(jnp.mean(result * result, axis=-1, keepdims=True) + 1e-05)


def usable_bias(block, sc):
    if block > 0:
        return None
    return jnp.where(sc[1] > 0, 0.0, MASKED).astype(F32)


def fast_kernel(sc, q_ref, w1_ref, w3_ref, w2_ref, out_ref):
    rows = q_ref.shape[0]
    tile = min(TILE, rows)
    for start in range(0, rows, tile):
        at = slice(start, start + tile)
        out_ref[at, :] = fast_rows(q_ref[at, :], w1_ref[...], w3_ref[...], w2_ref[...])


def fast_first(scalars, projected, weights, weight_specs, earlier=()):
    _, _, rows, feats = projected.shape
    return call(
        fast_kernel,
        "fast_0",
        scalars,
        (projected, *weights),
        [qkv_specs(0, projected)[0], *weight_specs],
        jax.ShapeDtypeStruct((rows, feats), F32),
        earlier=earlier,
    )


def mixed_kernel(block, sc, q_ref, k_ref, v_ref, k_halo, v_halo, fast_ref, out_ref):
    def store(rows, cols, value):
        out_ref[rows, cols] = (value.astype(F32) + fast_ref[rows, cols]).astype(BF)

    attend(q_ref, k_ref, v_ref, (k_halo, v_halo), usable_bias(block, sc), store)


def attend_kernel(block, sc, q_ref, k_ref, v_ref, halo_ref, out_ref):
    def store(rows, cols, value):
        out_ref[rows, cols] = value

    attend(q_ref, k_ref, v_ref, (halo_ref.at[0], halo_ref.at[1]), usable_bias(block, sc), store)


def qkv_specs(block, projected):
    _, _, rows, feats = projected.shape
    return [
        pl.BlockSpec((None, None, rows, feats), functools.partial(lambda kind, i, s: (kind, block, 0, 0), kind))
        for kind in range(3)
    ]


def attention_only(block, scalars, projected, halo, earlier=(), passing=()):
    _, _, rows, feats = projected.shape
    return call(
        functools.partial(attend_kernel, block),
        f"attend_{block}",
        scalars,
        (projected, projected, projected, halo),
        [*qkv_specs(block, projected), whole(halo)],
        jax.ShapeDtypeStruct((rows, feats), BF),
        earlier=earlier,
        passing=passing,
    )


def mixed_first(block, scalars, projected, halo, fast, earlier=()):
    _, _, rows, feats = projected.shape
    return call(
        functools.partial(mixed_kernel, block),
        f"mixed_{block}",
        scalars,
        (projected, projected, projected, *halo, fast),
        [*qkv_specs(block, projected), *[whole(x) for x in halo], whole(fast)],
        jax.ShapeDtypeStruct((rows, feats), BF),
        earlier=earlier,
    )


def halves(parity, mine, theirs):
    half = mine.shape[0]
    own = pl.multiple_of(parity * half, half)
    other = pl.multiple_of((1 - parity) * half, half)
    return ((pl.ds(own, half), mine), (pl.ds(other, half), theirs))


def renorm_all(old, mine, theirs, parity, moved, put, known=None):
    ratios = []
    for i in range(3):
        before = None if known is None else known[i, 0:1, 0:1]
        after = None
        for rows, part in halves(parity, mine[i], theirs[i]):
            w = old(i, rows).astype(F32)
            new = w - part.astype(F32)
            moved[i, rows, :] = new
            squares = jnp.sum(new * new, axis=0, keepdims=True)
            after = squares if after is None else after + squares
            if known is None:
                squares = jnp.sum(w * w, axis=0, keepdims=True)
                before = squares if before is None else before + squares
        after = jnp.sum(after, axis=1, keepdims=True)
        if known is None:
            before = jnp.sum(before, axis=1, keepdims=True)
        ratios.append(jnp.sqrt(before) / jnp.sqrt(after + 1e-06))
    for i in range(3):
        half = mine.shape[1]
        for start in (0, half):
            rows = slice(start, start + half)
            put(i, rows, moved[i, rows, :] * ratios[i])


def old_of(refs, i, rows):
    if len(refs) == 1:
        return refs[0][i, rows, :]
    return refs[0][i, 0, rows, :] if i < 2 else refs[1][0, rows, :]


def update_kernel(states, pieces, sc, mine_ref, theirs_ref, *refs):
    *refs, moved = refs
    old, (q_ref, att_ref, mix_ref, new_bf_ref), piece_refs = refs[:states], refs[states : states + 4], refs[states + 4 :]

    def put(i, rows, value):
        new_bf_ref[i, rows, :] = value.astype(BF)

    renorm_all(functools.partial(old_of, old), mine_ref, theirs_ref, sc[0], moved, put)
    rows = q_ref.shape[0]
    tile = min(FAST_TILE, rows)
    for start in range(0, rows, tile):
        at = slice(start, start + tile)
        fast = fast_rows(q_ref[at, :], new_bf_ref[0], new_bf_ref[1], new_bf_ref[2])
        mix_ref[at, :] = (att_ref[at, :].astype(F32) + fast).astype(BF)
    for i, piece_ref in enumerate(piece_refs):
        size = piece_ref.shape[0]
        piece_ref[...] = mix_ref[i * size : (i + 1) * size, :]


def update_and_mix(block, scalars, mine, theirs, state, projected, attended, parts, earlier=()):
    _, _, rows, feats = projected.shape
    pieces = parts if parts > 1 else 0
    got = call(
        functools.partial(update_kernel, len(state), pieces),
        f"update_{block}",
        scalars,
        (mine, theirs, *state, projected, attended),
        [
            whole(mine),
            whole(theirs),
            *[whole(a) for a in state],
            pl.BlockSpec((None, None, rows, feats), lambda i, s: (0, block, 0, 0)),
            whole(attended),
        ],
        [
            jax.ShapeDtypeStruct((rows, feats), BF),
            jax.ShapeDtypeStruct((3, feats, feats), BF),
            *[jax.ShapeDtypeStruct((rows // parts, feats), BF) for _ in range(pieces)],
        ],
        scratch=[pltpu.VMEM((3, *mine.shape[2:] * 2), F32)],
        earlier=earlier,
    )
    return got[0], got[1], got[2:] or [got[0]]


def state_kernel(states, sc, mine_ref, theirs_ref, *refs):
    old, (new_ref, norm_ref, moved) = refs[:states], refs[states:]

    def put(i, rows, value):
        new_ref[i, rows, :] = value

    renorm_all(functools.partial(old_of, old), mine_ref, theirs_ref, sc[0], moved, put)
    for i in range(3):
        norm_ref[i] = jnp.full(norm_ref.shape[1:], jnp.sum(new_ref[i] * new_ref[i]), F32)


def float_state(block, scalars, mine, theirs, state, earlier=()):
    feats = mine.shape[2]
    return call(
        functools.partial(state_kernel, len(state)),
        f"state_{block}",
        scalars,
        (mine, theirs, *state),
        [whole(mine), whole(theirs), *[whole(a) for a in state]],
        [jax.ShapeDtypeStruct((3, feats, feats), F32), jax.ShapeDtypeStruct((3, 8, HD), F32)],
        scratch=[pltpu.VMEM((3, feats, feats), F32)],
        earlier=earlier,
    )


def final_kernel(sc, mine_ref, theirs_ref, old_ref, norm_ref, up_out, down_out, token, moved, done, sems):
    token[...] = jnp.zeros_like(token)
    half = mine_ref.shape[1]
    outs = (up_out.at[0, 0], up_out.at[1, 0], down_out.at[0])
    copies = []

    def put(i, rows, value):
        done[i, rows, :] = value
        part = rows.start // half
        copy = pltpu.make_async_copy(done.at[i, rows, :], outs[i].at[rows, :], sems.at[i, part])
        copy.start()
        copies.append(copy)

    renorm_all(lambda i, rows: old_ref[i, rows, :], mine_ref, theirs_ref, sc[0], moved, put, norm_ref)
    for copy in copies:
        copy.wait()


def final_update(scalars, mine, theirs, state, norms, earlier=()):
    _, half, feats = mine.shape
    any_spec = pl.BlockSpec(memory_space=pl.ANY)
    return call(
        final_kernel,
        "final_update",
        scalars,
        (mine, theirs, state, norms),
        [whole(mine), whole(theirs), whole(state), whole(norms)],
        [
            jax.ShapeDtypeStruct((2, 1, feats, feats), F32),
            jax.ShapeDtypeStruct((1, feats, feats), F32),
            jax.ShapeDtypeStruct((8, HD), F32),
        ],
        out_specs=[any_spec, any_spec, whole_out((8, HD))],
        scratch=[
            pltpu.VMEM((3, feats, feats), F32),
            pltpu.VMEM((3, feats, feats), F32),
            pltpu.SemaphoreType.DMA((3, 2)),
        ],
        earlier=earlier,
    )


def pick_kernel(sc, w_ref, out_ref):
    half = out_ref.shape[1]
    feats = 2 * half
    for i in range(3):
        start = (sc[2] ^ (i + 1)) * feats + sc[0] * half
        out_ref[i] = w_ref[pl.ds(pl.multiple_of(start, half), half), :]


def pick_parts(scalars, w_out, earlier=()):
    feats = w_out.shape[1]
    return call(
        pick_kernel,
        "pick_parts",
        scalars,
        (w_out,),
        [whole(w_out)],
        jax.ShapeDtypeStruct((3, feats // 2, feats), BF),
        earlier=earlier,
    )


def gate_kernel(sc, x_ref, x_out_ref):
    pass


def gate(scalars, x, earlier):
    return call(
        gate_kernel,
        "gate",
        scalars,
        (x,),
        [pl.BlockSpec(memory_space=pl.ANY)],
        like(x),
        out_specs=[pl.BlockSpec(memory_space=pl.ANY)],
        aliases={0: 0},
        earlier=earlier,
    )


def split_kernel(sc, x_ref, *piece_refs):
    size = piece_refs[0].shape[0]
    for i, piece_ref in enumerate(piece_refs):
        piece_ref[...] = x_ref[i * size : (i + 1) * size, :]


def split(scalars, x, parts, earlier):
    rows, feats = x.shape
    piece = jax.ShapeDtypeStruct((rows // parts, feats), BF)
    return call(split_kernel, "split", scalars, (x,), [whole(x)], [piece] * parts, earlier=earlier)


def add_kernel(sc, a_ref, b_ref, out_ref):
    out_ref[...] = (a_ref[...].astype(F32) + b_ref[...].astype(F32)).astype(BF)


def add(scalars, a, b, earlier=(), passing=()):
    return call(add_kernel, "add", scalars, (a, b), [whole(a), whole(b)], like(a, BF), earlier=earlier, passing=passing)


def pack_kernel(sc, k_ref, v_ref, out_ref):
    out_ref[0] = k_ref[...]
    out_ref[1] = v_ref[...]


def first_rows(projected, kind):
    _, _, rows, feats = projected.shape
    return lax.slice(projected, (kind, 0, 0, 0), (kind + 1, 1, rows, feats)).reshape(rows, feats)


def pack_halo(block, scalars, projected, last, earlier=()):
    _, _, rows, feats = projected.shape

    def which(s):
        return block if block == 0 else jnp.where(s[1] == last, block - 1, block)

    return call(
        pack_kernel,
        f"pack_{block}",
        scalars,
        (projected, projected),
        [
            pl.BlockSpec((None, None, WIN, feats), lambda i, s: (1, which(s), rows // WIN - 1, 0)),
            pl.BlockSpec((None, None, WIN, feats), lambda i, s: (2, which(s), rows // WIN - 1, 0)),
        ],
        jax.ShapeDtypeStruct((2, WIN, feats), BF),
        earlier=earlier,
    )


def edge_kernel(sc, m_ref, ya_ref, yb_ref, mine_ref, theirs_ref, out_ref):
    half = mine_ref.shape[1]
    total = None
    for part, parity in ((mine_ref, sc[0]), (theirs_ref, 1 - sc[0])):
        cols = pl.ds(pl.multiple_of(parity * half, half), half)
        for i, ref in enumerate((m_ref, ya_ref, yb_ref)):
            term = mm(ref[:, cols], part[i])
            total = term if total is None else total + term
    out_ref[...] = total.astype(BF)


def part_spec(rows, feats, part):
    return pl.BlockSpec((rows, feats), lambda i, s: (part, 0))


def edge_part(name, scalars, part, m, ya, yb, v_mine, v_other, earlier=(), passing=()):
    rows, feats = yb.shape
    return call(
        edge_kernel,
        f"edge_{name}",
        scalars,
        (m, ya, yb, v_mine, v_other),
        [part_spec(rows, feats, part), part_spec(rows, feats, part), whole(yb), whole(v_mine), whole(v_other)],
        jax.ShapeDtypeStruct((rows, feats), BF),
        earlier=earlier,
        passing=passing,
    )


def for_edge(sc, c):
    return jnp.where(sc[3] == 0, c.astype(F32), 0.0)


def own_rows(sc, m, x, ya, yb, w_ref, hid, put, get):
    feats = w_ref.shape[1]
    head = sc[2]

    def weight(which):
        return w_ref[pl.ds(pl.multiple_of(which * feats, feats), feats), :]

    put(hid.astype(F32) + mm(m, weight(head)))

    @pl.when(sc[3] == 1)
    def _():
        put(get() + mm(x[...], weight(head ^ 1)) + mm(ya[...], weight(head ^ 3)) + mm(yb[...], weight(head ^ 2)))


def own_kernel(sc, m_ref, x_ref, ya_ref, yb_ref, w_ref, hid_ref, c_ref, *refs):
    out_ref, token, acc = refs[-3:]
    token[...] = jnp.zeros_like(token)

    def put(value):
        acc[...] = value

    own_rows(sc, m_ref[...], x_ref, ya_ref, yb_ref, w_ref, hid_ref[...], put, lambda: acc[...])
    out_ref[...] = (acc[...] + for_edge(sc, c_ref[...])).astype(BF)


def own_part(block, scalars, m, x, ya, yb, w_out, hidden_in, c, so_far, earlier=()):
    rows, feats = m.shape
    return call(
        own_kernel,
        f"own_{block}",
        scalars,
        (m, x, ya, yb, w_out, hidden_in, c, *so_far),
        [
            *[whole(a) for a in (m, x, ya, yb, w_out)],
            pl.BlockSpec((None, rows, feats), lambda i, s: (block, 0, 0)),
            whole(c),
            *[pl.BlockSpec(memory_space=pl.ANY) for _ in so_far],
        ],
        [like(hidden_in), jax.ShapeDtypeStruct((8, HD), F32)],
        out_specs=[pl.BlockSpec((None, rows, feats), lambda i, s: (block, 0, 0)), whole_out((8, HD))],
        aliases={7: 0} if so_far else None,
        scratch=[pltpu.VMEM((rows, feats), F32)],
        earlier=earlier,
    )


def last_kernel(parts, sc, *refs):
    m_ref, ya_ref = refs[:2]
    xs, ybs = refs[2 : 2 + parts], refs[2 + parts : 2 + 2 * parts]
    w_ref, hid_ref, out_ref = refs[2 + 2 * parts :]
    rows = m_ref.shape[0] // parts
    for i in range(parts):
        at = pl.ds(i * rows, rows)

        def put(value, at=at):
            out_ref[at, :] = value

        own_rows(
            sc, m_ref[at, :], xs[i], ya_ref.at[at, :], ybs[i], w_ref, hid_ref[at, :], put, lambda at=at: out_ref[at, :]
        )


def own_last(block, scalars, m, xs, ya, ybs, w_out, hidden_in, earlier=()):
    rows, feats = m.shape
    return call(
        functools.partial(last_kernel, len(xs)),
        f"own_{block}",
        scalars,
        (m, ya, *xs, *ybs, w_out, hidden_in),
        [
            *[whole(a) for a in (m, ya, *xs, *ybs, w_out)],
            pl.BlockSpec((None, rows, feats), lambda i, s: (block, 0, 0)),
        ],
        jax.ShapeDtypeStruct((rows, feats), F32),
        earlier=earlier,
    )


def finish_kernel(block, parts, sc, acc_ref, *refs):
    out_ref, done, sems = refs[-3:]
    rows = acc_ref.shape[0] // parts
    copies = []
    for i in range(parts):
        at = slice(i * rows, (i + 1) * rows)
        done[at, :] = (acc_ref[at, :] + for_edge(sc, refs[i][...])).astype(BF)
        copies.append(pltpu.make_async_copy(done.at[at, :], out_ref.at[block, at, :], sems.at[i]))
        copies[-1].start()
    for copy in copies:
        copy.wait()


def finish(block, scalars, acc, cs, so_far, earlier=()):
    any_spec = pl.BlockSpec(memory_space=pl.ANY)
    return call(
        functools.partial(finish_kernel, block, len(cs)),
        "finish",
        scalars,
        (acc, *cs, so_far),
        [whole(acc), *[whole(c) for c in cs], any_spec],
        like(so_far),
        out_specs=[any_spec],
        aliases={1 + len(cs): 0},
        scratch=[pltpu.VMEM(acc.shape, BF), pltpu.SemaphoreType.DMA((len(cs),))],
        earlier=earlier,
    )


def move(x, axis, pairs):
    return lax.ppermute(x, axis, pairs)


def between_inner(x):
    count = lax.axis_size("ctx")
    planes = lax.axis_size("head")
    pairs = []
    for i in range(count):
        pairs += [(i * planes + 1, i * planes + 2), (i * planes + 2, i * planes + 1)]
        pairs += [(i * planes + j, (i ^ 1) * planes + j) for j in (0, 3)]
    return move(x, ("ctx", "head"), pairs)


def flip(x, bit):
    count = lax.axis_size("ctx")
    return move(x, "ctx", [(i, i ^ (1 << bit)) for i in range(count)])


def partners(count, step):
    bits = list(range(1, count.bit_length() - 1))
    return [(i, i ^ (1 << (bits if i % 2 == 0 else bits[::-1])[step])) for i in range(count)]


def body(hidden_in, projected, w_out, fast_up, fast_down, learn_rates):
    blocks, rows, feats = hidden_in.shape
    ctx = lax.axis_index("ctx")
    head = lax.axis_index("head")
    ctx_count = lax.axis_size("ctx")
    steps = ctx_count.bit_length() - 2
    parity = ctx % 2
    inner = ((head == 1) | (head == 2)).astype(jnp.int32)
    scalars = jnp.stack([parity, ctx, head, inner]).astype(jnp.int32)
    step_scale = 1.0 / math.sqrt(rows * ctx_count)
    around = [(i, (i + 1) % ctx_count) for i in range(ctx_count)]

    up_spec = [
        pl.BlockSpec((None, None, feats, feats), lambda *_: (0, 0, 0, 0)),
        pl.BlockSpec((None, None, feats, feats), lambda *_: (1, 0, 0, 0)),
        pl.BlockSpec((None, feats, feats), lambda *_: (0, 0, 0)),
    ]
    bf_spec = [
        pl.BlockSpec((None, feats, feats), functools.partial(lambda k, *_: (k, 0, 0), k)) for k in range(3)
    ]

    weights, specs = (fast_up, fast_up, fast_down), up_spec
    state = (fast_up, fast_down)

    kv_now = [first_rows(projected, kind) for kind in (1, 2)]
    halo = [move(x[rows - WIN :], "ctx", around) for x in kv_now]
    keep, send = block_grads(0, scalars, projected, learn_rates, weights, step_scale, specs, own=kv_now)
    keep = gate(scalars, keep, earlier=(send,))
    total = add(scalars, keep, flip(send, 0))
    received = move(total, "ctx", partners(ctx_count, 0))
    kv_now = pack_halo(1, scalars, projected, ctx_count - 1, earlier=(total,))
    halo_next = move(kv_now, "ctx", around)
    fast = fast_first(scalars, projected, weights, specs, earlier=(kv_now,))
    mixed = mixed_first(0, scalars, projected, halo, fast)
    x = move(mixed, "head", EDGES)
    ya = between_inner(mixed)
    v_send = last = pick_parts(scalars, w_out, earlier=(mixed,))
    v_mine = move(v_send, "head", EDGES)
    so_far = ()
    for block in range(1, blocks):
        for step in range(steps):
            total = last = add(scalars, total, received, earlier=(last,))
            if step + 1 < steps:
                received = move(total, "ctx", partners(ctx_count, step + 1))
            if step == 0:
                attended = last = attention_only(block, scalars, projected, halo_next, earlier=(last,))
                x = last = gate(scalars, x, earlier=(last,))
                yb = between_inner(x)
        theirs = flip(total, 0)
        ya = last = gate(scalars, ya, earlier=(total,))
        mixed_next, new_bf = update_and_mix(
            block, scalars, total, theirs, state, projected, attended, 1, earlier=(last,)
        )[:2]
        x_next = move(mixed_next, "head", EDGES)
        ya_next = between_inner(mixed_next)
        weights, specs = (new_bf, new_bf, new_bf), bf_spec
        keep, send = block_grads(
            block, scalars, projected, learn_rates, weights, step_scale, specs, earlier=(mixed_next,)
        )
        if block == 1:
            v_mine = last = gate(scalars, v_mine, earlier=(send,))
            v_other = flip(v_mine, 0)
        else:
            keep = last = gate(scalars, keep, earlier=(send,))
        summed = add(scalars, keep, flip(send, 0), earlier=(last,))
        received = move(summed, "ctx", partners(ctx_count, 0))
        c = last = edge_part(block - 1, scalars, 0, mixed, ya, yb, v_mine, v_other, earlier=(summed,))
        c_there = move(c, "head", EDGES)
        if block < blocks - 1:
            now, norms = float_state(block, scalars, total, theirs, state, earlier=(last,))
            kv_now = last = pack_halo(block + 1, scalars, projected, ctx_count - 1, earlier=(norms,))
            halo_next = move(kv_now, "ctx", around)
            out, last = own_part(
                block - 1, scalars, mixed, x, ya, yb, w_out, hidden_in, c_there, so_far, earlier=(last,)
            )
            so_far = (out,)
            state, total = (now,), summed
            mixed, x, ya = mixed_next, x_next, ya_next
    now, norms = float_state(blocks - 1, scalars, total, theirs, state, earlier=(last,))
    xs = split(scalars, x_next, PARTS, (norms,))
    ybs = [between_inner(piece) for piece in xs]
    total, last = summed, xs[0]
    for step in range(steps):
        total = last = add(scalars, total, received, earlier=(last,))
        if step + 1 < steps:
            received = move(total, "ctx", partners(ctx_count, step + 1))
        if step == 0:
            c_last = []
            for i in range(PARTS):
                c = last = edge_part(
                    f"{blocks - 1}_{i}", scalars, i, mixed_next, ya_next, ybs[i], v_mine, v_other, earlier=(last,)
                )
                c_last.append(move(c, "head", EDGES))
                if i == 0:
                    out, last = own_part(
                        blocks - 2, scalars, mixed, x, ya, yb, w_out, hidden_in, c_there, so_far, earlier=(last,)
                    )
    theirs = flip(total, 0)
    acc = own_last(blocks - 1, scalars, mixed_next, xs, ya_next, ybs, w_out, hidden_in, earlier=(total,))
    up_final, down_final, token = final_update(scalars, total, theirs, now, norms, earlier=(acc,))
    out = finish(blocks - 1, scalars, acc, c_last, out, earlier=(token,))
    return out, up_final, down_final


def solution(mesh):
    in_specs = (
        P(None, "ctx", "head"),
        P(None, None, "ctx", "head"),
        P(None, "head"),
        P(None, "head", None, None),
        P("head", None, None),
        P("head", None, "ctx"),
    )
    out_specs = (P(None, "ctx", "head"), P(None, "head", None, None), P("head", None, None))
    return jax.shard_map(body, mesh=mesh, in_specs=in_specs, out_specs=out_specs, check_vma=False)
```
